32 devices in a mesh: dp: 4 (over y, x), ctx: 8 (over z, core).
Axes of the slice: x: 2, y: 2, z: 4, core: 2. Of those that a mesh axis runs over, the one named last changes fastest.
Arguments:
- tokens: bfloat16 [2, 4, 1024, 1024], P(None, 'dp', 'ctx'), may hold values from -6 to 6
- segments: int32 [2, 4, 1024], P(None, 'dp', 'ctx'), may hold values from 0 to 1023, as said below
- cotangent: bfloat16 [2, 4, 1024, 1024], P(None, 'dp', 'ctx'), may hold values from -6 to 6
- first_norm: bfloat16 [1024], P(('dp', 'ctx')), may hold values from 0.25 to 1.75
- first_input: bfloat16 [1024, 4384], P(('dp', 'ctx')), may hold values from -0.1875 to 0.1875
- first_kernel: bfloat16 [4, 2304], P(None, ('dp', 'ctx')), may hold values from -3 to 3
- first_offset: bfloat16 [2304], P(('dp', 'ctx')), may hold values from -3 to 3
- first_timestep: float32 [32], replicated, may hold values from -6 to -2
- first_decay: float32 [32], replicated, may hold values from -3 to 0.5
- first_skip: float32 [32], replicated, may hold values from 0.5 to 2.5
- first_gate: bfloat16 [2048], P(('dp', 'ctx')), may hold values from 0.25 to 1.75
- first_output: bfloat16 [2048, 1024], P(('dp', 'ctx')), may hold values from -0.125 to 0.125
- second_norm: bfloat16 [1024], P(('dp', 'ctx')), may hold values from 0.25 to 1.75
- second_input: bfloat16 [1024, 4384], P(('dp', 'ctx')), may hold values from -0.1875 to 0.1875
- second_kernel: bfloat16 [4, 2304], P(None, ('dp', 'ctx')), may hold values from -3 to 3
- second_offset: bfloat16 [2304], P(('dp', 'ctx')), may hold values from -3 to 3
- second_timestep: float32 [32], replicated, may hold values from -6 to -2
- second_decay: float32 [32], replicated, may hold values from -3 to 0.5
- second_skip: float32 [32], replicated, may hold values from 0.5 to 2.5
- second_gate: bfloat16 [2048], P(('dp', 'ctx')), may hold values from 0.25 to 1.75
- second_output: bfloat16 [2048, 1024], P(('dp', 'ctx')), may hold values from -0.125 to 0.125
Outputs:
- block_output: float32 [2, 4, 1024, 1024], P(None, 'dp', 'ctx')
- token_grad: float32 [2, 4, 1024, 1024], P(None, 'dp', 'ctx')
- first_norm_grad: float32 [1024], P(('dp', 'ctx'))
- first_input_grad: float32 [1024, 4384], P(('dp', 'ctx'))
- first_kernel_grad: float32 [4, 2304], P(None, ('dp', 'ctx'))
- first_offset_grad: float32 [2304], P(('dp', 'ctx'))
- first_timestep_grad: float32 [32], replicated
- first_decay_grad: float32 [32], replicated
- first_skip_grad: float32 [32], replicated
- first_gate_grad: float32 [2048], P(('dp', 'ctx'))
- first_output_grad: float32 [2048, 1024], P(('dp', 'ctx'))
- second_norm_grad: float32 [1024], P(('dp', 'ctx'))
- second_input_grad: float32 [1024, 4384], P(('dp', 'ctx'))
- second_kernel_grad: float32 [4, 2304], P(None, ('dp', 'ctx'))
- second_offset_grad: float32 [2304], P(('dp', 'ctx'))
- second_timestep_grad: float32 [32], replicated
- second_decay_grad: float32 [32], replicated
- second_skip_grad: float32 [32], replicated
- second_gate_grad: float32 [2048], P(('dp', 'ctx'))
- second_output_grad: float32 [2048, 1024], P(('dp', 'ctx'))
The draws below stay inside these ranges and needn't reach their ends.
Inputs may be any that keep to these rules, and one draw needn't show every extreme that they name: `segments`: along each sequence the ids never fall and rise by 0 or 1 from one token to the next, and the last token of every sequence has id 1024 - 1. Of the 2 sequences on each index of dp, one has all its document starts within its first and its last 64 tokens.
All inputs are finite; a program needn't handle non-finite values.
Results may differ from the reference program's by a relative error of at most 0.011.
Values may be sent and summed in bfloat16 or wider, within the bound.
No kernel may reach another device: no remote copies, remote signals or barrier semaphores. Data moves between devices by JAX's collectives and lax.ppermute only.
A program may use at most 192 MiB of HBM per device.

```python
import math
import jax
import jax.numpy as jnp
from jax import lax

D = 1024
HEADS = 32
HEAD_DIM = 64
NSTATE = 128
KERNEL = 4
PIECE = 128
SEQS = 1
MB = 2
INNER = 2048
CONV = 2304
PROJ = 4384
NSEQ = 4
SEQ_LEN = 1024


def draw_segments(key, part):
    key = jax.random.fold_in(key, 17)
    rate_key, cut_key, pick_key = jax.random.split(key, 3)
    exponent = jax.random.randint(rate_key, (MB, NSEQ, 1), 4, 12)
    limit = jnp.right_shift(jnp.full((MB, NSEQ, 1), 1 << 20, jnp.int32), exponent)
    drawn = jax.random.randint(cut_key, (MB, NSEQ, SEQ_LEN), 0, 1 << 20)
    position = lax.broadcasted_iota(jnp.int32, (MB, NSEQ, SEQ_LEN), 2)
    chosen = jax.random.randint(pick_key, (1, NSEQ // SEQS, 1), 0, MB * SEQS)
    chosen = jnp.repeat(chosen, SEQS, axis=1)
    member = lax.broadcasted_iota(jnp.int32, (MB, NSEQ, 1), 0) * SEQS + lax.broadcasted_iota(jnp.int32, (MB, NSEQ, 1), 1) % SEQS
    edges = (position < PIECE // 2) | (position >= SEQ_LEN - PIECE // 2)
    boundary = ((drawn < limit) & (position > 0) & ((member != chosen) | edges)).astype(jnp.int32)
    counted = jnp.cumsum(boundary, axis=2)
    starts = jnp.sum(boundary, axis=2, keepdims=True)
    return counted + (SEQ_LEN - 1) - starts


def shard_levels(stream_key, shape, cuts, least, high):
    level, own = 1.0, jax.random.fold_in(stream_key, 6)
    for dim, shards_of in cuts:
        draws = jnp.exp(jax.random.uniform(jax.random.fold_in(own, dim), (shards_of,), jnp.float32, least / len(cuts), high / len(cuts)))
        level = level * jnp.repeat(draws, shape[dim] // shards_of).reshape([-1 if axis == dim else 1 for axis in range(len(shape))])
    return level


def normal_values(own_key, extent, spread, most, cuts=(), dtype=jnp.bfloat16):
    entries = spread * jax.random.normal(own_key, extent, jnp.float32)
    if cuts:
        entries = entries * shard_levels(own_key, extent, cuts, -0.22, 0.18)
    return jnp.clip(entries, -most, most).astype(dtype)


def setup_inputs(seed: int = 0) -> dict:
    key_of = jax.random.split(jax.random.key(seed), 22)
    return {
        "tokens": normal_values(key_of[0], (MB, NSEQ, SEQ_LEN, D), 1.0, 6.0, ((1, 4), (2, 8))),
        "segments": draw_segments(jax.random.fold_in(key_of[21], 71), 0),
        "cotangent": normal_values(key_of[2], (MB, NSEQ, SEQ_LEN, D), 1.0, 6.0, ((1, 4), (2, 8))),
        "first_norm": jnp.clip(1.0 + 0.15 * jax.random.normal(key_of[3], (D,), jnp.float32), 0.25, 1.75).astype(jnp.bfloat16),
        "first_input": normal_values(key_of[4], (D, PROJ), D ** -0.5, 0.1875, ((0, 32),)),
        "first_kernel": normal_values(key_of[5], (KERNEL, CONV), KERNEL ** -0.5, 3.0, ((1, 32),)),
        "first_offset": normal_values(key_of[6], (CONV,), 0.5, 3.0, ((0, 32),)),
        "first_timestep": jnp.clip(jax.random.uniform(key_of[7], (HEADS,), jnp.float32, -6.0, -2.0), -6.0, -2.0),
        "first_decay": jnp.clip(jax.random.uniform(key_of[8], (HEADS,), jnp.float32, -3.0, 0.5), -3.0, 0.5),
        "first_skip": jnp.clip(jax.random.uniform(key_of[9], (HEADS,), jnp.float32, 0.5, 2.5), 0.5, 2.5),
        "first_gate": jnp.clip(1.0 + 0.15 * jax.random.normal(key_of[10], (INNER,), jnp.float32), 0.25, 1.75).astype(jnp.bfloat16),
        "first_output": normal_values(key_of[11], (INNER, D), INNER ** -0.5, 0.125, ((0, 32),)),
        "second_norm": jnp.clip(1.0 + 0.15 * jax.random.normal(key_of[12], (D,), jnp.float32), 0.25, 1.75).astype(jnp.bfloat16),
        "second_input": normal_values(key_of[13], (D, PROJ), D ** -0.5, 0.1875, ((0, 32),)),
        "second_kernel": normal_values(key_of[14], (KERNEL, CONV), KERNEL ** -0.5, 3.0, ((1, 32),)),
        "second_offset": normal_values(key_of[15], (CONV,), 0.5, 3.0, ((0, 32),)),
        "second_timestep": jnp.clip(jax.random.uniform(key_of[16], (HEADS,), jnp.float32, -6.0, -2.0), -6.0, -2.0),
        "second_decay": jnp.clip(jax.random.uniform(key_of[17], (HEADS,), jnp.float32, -3.0, 0.5), -3.0, 0.5),
        "second_skip": jnp.clip(jax.random.uniform(key_of[18], (HEADS,), jnp.float32, 0.5, 2.5), 0.5, 2.5),
        "second_gate": jnp.clip(1.0 + 0.15 * jax.random.normal(key_of[19], (INNER,), jnp.float32), 0.25, 1.75).astype(jnp.bfloat16),
        "second_output": normal_values(key_of[20], (INNER, D), INNER ** -0.5, 0.125, ((0, 32),)),
    }


EPSILON = 1e-05
PRECISE = lax.Precision.HIGHEST

@jax.custom_vjp
def low(v):
    return lax.optimization_barrier(v.astype(jnp.bfloat16)).astype(jnp.float32)

@jax.custom_vjp
def low_back(v):
    return v

def low_keep(v):
    return (low(v), None)

def low_pass(kept, grad):
    return (grad,)

def back_keep(v):
    return (v, None)

def back_low(kept, grad):
    return (low(grad),)
low.defvjp(low_keep, low_pass)
low_back.defvjp(back_keep, back_low)

def rms_scale(values, gain_vector):
    return values * lax.rsqrt(lax.optimization_barrier(jnp.mean(values * values, axis=-1, keepdims=True)) + EPSILON) * gain_vector

def piece_terms(values, written, readout, step_size, cumulative, seg_block, before, incoming):
    length = seg_block.shape[1]
    last = cumulative[:, -1, :]
    same_last = (seg_block == seg_block[:, -1:]).astype(jnp.float32)
    weight_end = jnp.exp(last[:, None, :] - cumulative) * same_last[..., None] * step_size
    state_end = jnp.einsum('sjhp,sjn->shpn', values * weight_end[..., None], written, precision=PRECISE)
    through = jnp.exp(last) * (seg_block[:, -1] == before).astype(jnp.float32)[:, None]
    causal = jnp.tril(jnp.ones((length, length), jnp.bool_))
    allowed = causal[None] & (seg_block[:, :, None] == seg_block[:, None, :])
    scores = jnp.einsum('sin,sjn->sij', readout, written, precision=PRECISE)
    by_head = jnp.moveaxis(cumulative, 2, 1)
    log_gap = by_head[:, :, :, None] - by_head[:, :, None, :]
    allowed_heads = allowed[:, None]
    decay_matrix = jnp.where(allowed_heads, jnp.exp(jnp.where(allowed_heads, log_gap, 0.0)), 0.0)
    mixing = decay_matrix * scores[:, None] * jnp.moveaxis(step_size, 2, 1)[:, :, None, :]
    result = jnp.einsum('shij,sjhp->sihp', mixing, values, precision=PRECISE)
    entry_decay = jnp.exp(cumulative) * (seg_block == before[:, None]).astype(jnp.float32)[..., None]
    result = result + entry_decay[..., None] * jnp.einsum('shpn,sin->sihp', incoming, readout, precision=PRECISE)
    return (result, state_end, through)

def state_space(values, written, readout, step_size, cumulative, seg_f):
    sequences, length = seg_f.shape
    count = length // PIECE

    def blocks(array):
        return jnp.moveaxis(array.reshape((sequences, count, PIECE) + array.shape[2:]), 1, 0)

    def advance(carry, block):
        incoming, before = carry
        vals, wri, rea, stp, cum, seg_block = block
        result, state_end, through = piece_terms(vals, wri, rea, stp, cum, seg_block, before, incoming)
        return ((incoming * through[:, :, None, None] + state_end, seg_block[:, -1]), result)
    start = (jnp.zeros((sequences, HEADS, HEAD_DIM, NSTATE), jnp.float32), jnp.full((sequences,), -1.0, jnp.float32))
    inputs = (blocks(values), blocks(written), blocks(readout), blocks(step_size), blocks(cumulative), blocks(seg_f))
    _, outputs = lax.scan(jax.checkpoint(advance), start, inputs)
    return jnp.moveaxis(outputs, 0, 1).reshape(sequences, length, HEADS, HEAD_DIM)

def layer(hidden, seg_f, weights):
    norm_gain, in_weight, kernel, offset, timestep, decay_log, skip_gain, gate_gain, out_weight = weights
    sequences, length, _ = hidden.shape
    normed = low(rms_scale(hidden, norm_gain))
    projected = low_back(jnp.dot(normed, in_weight, precision=PRECISE))
    gate_input = projected[..., :INNER]
    kernel_input = projected[..., INNER:INNER + CONV]
    raw_step = projected[..., INNER + CONV:]
    padded = jnp.pad(kernel_input, ((0, 0), (KERNEL - 1, 0), (0, 0)))
    padded_ids = jnp.concatenate([jnp.full((sequences, KERNEL - 1), -1.0, jnp.float32), seg_f], axis=1)
    convolved = offset + jnp.zeros_like(kernel_input)
    for tap in range(KERNEL):
        matches = (padded_ids[:, tap:tap + length] == seg_f).astype(jnp.float32)
        convolved = convolved + kernel[tap] * padded[:, tap:tap + length] * matches[..., None]
    active = jax.nn.silu(convolved)
    values = active[..., :INNER].reshape(sequences, length, HEADS, HEAD_DIM)
    written = active[..., INNER:INNER + NSTATE]
    readout = active[..., INNER + NSTATE:]
    step_size = jax.nn.softplus(raw_step + timestep)
    rate = -step_size * jnp.exp(decay_log)
    cumulative = jnp.cumsum(rate.reshape(sequences, length // PIECE, PIECE, HEADS), axis=2).reshape(sequences, length, HEADS)
    heads_out = state_space(values, written, readout, step_size, cumulative, seg_f)
    heads_out = heads_out + skip_gain[:, None] * values
    gated = heads_out.reshape(sequences, length, INNER) * jax.nn.silu(gate_input)
    mixed = low(rms_scale(gated, gate_gain))
    update = low_back(jnp.dot(mixed, out_weight, precision=PRECISE))
    return hidden + update

def reference(tokens, segments, cotangent, first_norm, first_input, first_kernel, first_offset, first_timestep, first_decay, first_skip, first_gate, first_output, second_norm, second_input, second_kernel, second_offset, second_timestep, second_decay, second_skip, second_gate, second_output):
    layout = tokens.shape
    total = MB * NSEQ
    hidden = tokens.astype(jnp.float32).reshape(total, SEQ_LEN, D)
    seg_f = segments.reshape(total, SEQ_LEN).astype(jnp.float32)
    first = tuple((weight.astype(jnp.float32) for weight in (first_norm, first_input, first_kernel, first_offset, first_timestep, first_decay, first_skip, first_gate, first_output)))
    second = tuple((weight.astype(jnp.float32) for weight in (second_norm, second_input, second_kernel, second_offset, second_timestep, second_decay, second_skip, second_gate, second_output)))
    group = math.gcd(total, max(1, 4096 // SEQ_LEN))

    def two_layers(block_hidden, block_seg, first_weights, second_weights):
        return layer(layer(block_hidden, block_seg, first_weights), block_seg, second_weights)
    checked = jax.checkpoint(two_layers)

    def forward(hidden, first_weights, second_weights):
        grouped = hidden.reshape(total // group, group, SEQ_LEN, D)
        grouped_seg = seg_f.reshape(total // group, group, SEQ_LEN)

        def apply_group(pair):
            return checked(pair[0], pair[1], first_weights, second_weights)
        return lax.map(apply_group, (grouped, grouped_seg)).reshape(total, SEQ_LEN, D)
    result, pullback = jax.vjp(forward, hidden, first, second)
    back_hidden, back_first, back_second = pullback(cotangent.astype(jnp.float32).reshape(total, SEQ_LEN, D))
    return (result.reshape(layout), back_hidden.reshape(layout), back_first[0], back_first[1], back_first[2], back_first[3], back_first[4], back_first[5], back_first[6], back_first[7], back_first[8], back_second[0], back_second[1], back_second[2], back_second[3], back_second[4], back_second[5], back_second[6], back_second[7], back_second[8])
```

```python
import jax
import jax.numpy as jnp
from jax import lax
from jax.sharding import PartitionSpec as P

EPSILON = 1e-05


def shift_along(x, by):
    size = lax.axis_size("ctx")
    pairs = [(i, i + by) for i in range(size) if 0 <= i + by < size]
    return lax.ppermute(x, "ctx", pairs)


def swap_cores(x):
    return lax.ppermute(x, "ctx", [(i, i ^ 1) for i in range(lax.axis_size("ctx"))])


def rms_scale(values, gain_vector):
    return (
        values
        * lax.rsqrt(jnp.mean(values * values, axis=-1, keepdims=True) + EPSILON)
        * gain_vector
    )


def half_of(x, which):
    heads = x.shape[1] // 2
    return lax.dynamic_slice_in_dim(x, which * heads, heads, axis=1)


def join_halves(mine, other, core):
    first = jnp.where(core == 0, mine, other)
    second = jnp.where(core == 0, other, mine)
    return jnp.concatenate([first, second], axis=1)


def scaled(state, through):
    return state * through[:, :, None, None]


def chain(through, state, forward):
    count = lax.axis_size("ctx")
    position = lax.axis_index("ctx")
    core = position % 2
    chip = position // 2
    chips = count // 2
    low = state.astype(jnp.bfloat16)
    other_through = swap_cores(through)
    sent = swap_cores(half_of(low, 1 - core)).astype(jnp.float32)
    mine = half_of(state, core)
    leading = core == (0 if forward else 1)
    own_t, other_t = half_of(through, core), half_of(other_through, core)
    first_state = jnp.where(leading, mine, sent)
    second_state = jnp.where(leading, sent, mine)
    first_t = jnp.where(leading, own_t, other_t)
    second_t = jnp.where(leading, other_t, own_t)
    pair_t = first_t * second_t
    pair_state = scaled(first_state, second_t) + second_state
    incoming = jnp.zeros_like(pair_state)
    outgoing = pair_state
    for step in range(chips - 1):
        source, target = (step, step + 1) if forward else (chips - 1 - step, chips - 2 - step)
        pairs = [(2 * source + c, 2 * target + c) for c in range(2)]
        arrived = lax.ppermute(outgoing.astype(jnp.bfloat16), "ctx", pairs).astype(jnp.float32)
        incoming = incoming + arrived
        if step < chips - 2:
            outgoing = scaled(incoming, pair_t) + pair_state
    first_in = incoming
    second_in = scaled(incoming, first_t) + first_state
    keep = jnp.where(leading, first_in, second_in)
    give = jnp.where(leading, second_in, first_in)
    back = swap_cores(give.astype(jnp.bfloat16)).astype(jnp.float32)
    return join_halves(keep, back, core)


def layer_forward(hidden, seg_f, gathered, head_params):
    norm_gain, in_weight, kernel, offset, gate_gain, out_weight = gathered
    timestep, decay_log, skip_gain = head_params
    sequences, piece_size, _ = hidden.shape
    inner_width = gate_gain.shape[0]
    channel_width = offset.shape[0]
    kernel_taps = kernel.shape[0]
    head_count = timestep.shape[0]
    head_size = inner_width // head_count
    state_size = (channel_width - inner_width) // 2
    normed, norm_pull = jax.vjp(rms_scale, hidden, norm_gain.astype(jnp.float32))
    normed_low = normed.astype(jnp.bfloat16)
    projected = jnp.dot(normed_low, in_weight, preferred_element_type=jnp.float32)
    edge_rows = projected[
        :, piece_size - kernel_taps + 1 :, inner_width : inner_width + channel_width
    ]
    edge_ids = seg_f[:, piece_size - kernel_taps + 1 :]
    prev_rows, prev_ids = shift_along((edge_rows, edge_ids), 1)
    prev_last = prev_ids[:, -1]
    joined_ids = jnp.concatenate([prev_ids, seg_f], axis=1)
    causal = jnp.tril(jnp.ones((piece_size, piece_size), jnp.bool_))
    allowed = causal[None] & (seg_f[:, :, None] == seg_f[:, None, :])
    same_last = (seg_f == seg_f[:, -1:]).astype(jnp.float32)
    entry_mask = (seg_f == prev_last[:, None]).astype(jnp.float32)
    carry_mask = (seg_f[:, -1] == prev_last).astype(jnp.float32)

    def prepare(projected, prev_rows, kernel_taps_f, offset_f, timestep, decay_log):
        gate_input = projected[..., :inner_width]
        joined = jnp.concatenate(
            [prev_rows, projected[..., inner_width : inner_width + channel_width]], axis=1
        )
        convolved = offset_f + jnp.zeros_like(
            projected[..., inner_width : inner_width + channel_width]
        )
        for tap in range(kernel_taps):
            matches = (joined_ids[:, tap : tap + piece_size] == seg_f).astype(jnp.float32)
            convolved = (
                convolved
                + kernel_taps_f[tap] * joined[:, tap : tap + piece_size] * matches[..., None]
            )
        active = jax.nn.silu(convolved)
        values = active[..., :inner_width].reshape(sequences, piece_size, head_count, head_size)
        written = active[..., inner_width : inner_width + state_size]
        readout = active[..., inner_width + state_size :]
        step_size = jax.nn.softplus(projected[..., inner_width + channel_width :] + timestep)
        cumulative = jnp.cumsum(-step_size * jnp.exp(decay_log), axis=1)
        return (values, written, readout, step_size, cumulative, gate_input)

    def ending(values, written, step_size, cumulative):
        last = cumulative[:, -1, :]
        weight_end = jnp.exp(last[:, None, :] - cumulative) * same_last[..., None] * step_size
        state_end = jnp.einsum(
            "sjhp,sjn->shpn", values * weight_end[..., None], written
        )
        through = jnp.exp(last) * carry_mask[:, None]
        return (state_end, through)

    def outputs(
        values,
        written,
        readout,
        step_size,
        cumulative,
        gate_input,
        incoming,
        skip_gain,
        gate_gain_f,
    ):
        scores = jnp.einsum("sin,sjn->sij", readout, written)
        by_head = jnp.moveaxis(cumulative, 2, 1)
        log_gap = by_head[:, :, :, None] - by_head[:, :, None, :]
        allowed_heads = allowed[:, None]
        decay_matrix = jnp.where(
            allowed_heads, jnp.exp(jnp.where(allowed_heads, log_gap, 0.0)), 0.0
        )
        mixing = decay_matrix * scores[:, None] * jnp.moveaxis(step_size, 2, 1)[:, :, None, :]
        result = jnp.einsum("shij,sjhp->sihp", mixing, values)
        entry_decay = jnp.exp(cumulative) * entry_mask[..., None]
        result = result + entry_decay[..., None] * jnp.einsum(
            "shpn,sin->sihp", incoming, readout
        )
        result = result + skip_gain[:, None] * values
        gated = result.reshape(sequences, piece_size, inner_width) * jax.nn.silu(gate_input)
        return rms_scale(gated, gate_gain_f)

    prepared, prepare_pull = jax.vjp(
        prepare,
        projected,
        prev_rows,
        kernel.astype(jnp.float32),
        offset.astype(jnp.float32),
        timestep,
        decay_log,
    )
    values, written, readout, step_size, cumulative, gate_input = prepared
    ends, ending_pull = jax.vjp(ending, values, written, step_size, cumulative)
    state_end, through = ends
    incoming = chain(through, state_end, True)
    mixed, output_pull = jax.vjp(
        outputs,
        values,
        written,
        readout,
        step_size,
        cumulative,
        gate_input,
        incoming,
        skip_gain,
        gate_gain.astype(jnp.float32),
    )
    mixed_low = mixed.astype(jnp.bfloat16)
    update = jnp.dot(mixed_low, out_weight, preferred_element_type=jnp.float32)
    saved = (
        norm_pull,
        normed_low,
        prepare_pull,
        ending_pull,
        output_pull,
        mixed_low,
        through,
        incoming,
        kernel_taps,
        inner_width,
        channel_width,
    )
    return (hidden + update, saved)


def layer_backward(gradient, saved, gathered):
    (
        norm_pull,
        normed_low,
        prepare_pull,
        ending_pull,
        output_pull,
        mixed_low,
        through,
        incoming,
        kernel_taps,
        inner_width,
        channel_width,
    ) = saved
    in_weight = gathered[1]
    out_weight = gathered[5]
    update_low = gradient.astype(jnp.bfloat16)
    output_weight_grad = jnp.einsum(
        "spi,spd->id", mixed_low, update_low, preferred_element_type=jnp.float32
    )
    mixed_grad = jnp.einsum(
        "spd,id->spi", update_low, out_weight, preferred_element_type=jnp.float32
    )
    (
        back_values,
        back_written,
        back_readout,
        back_step,
        back_cumulative,
        back_gates,
        back_incoming,
        back_skip,
        back_gain,
    ) = output_pull(mixed_grad)
    state_back = chain(through, back_incoming, False)
    through_grad = jnp.sum(state_back * incoming, axis=(2, 3))
    extra_values, extra_written, extra_step, extra_cumulative = ending_pull(
        (state_back, through_grad)
    )
    projected_grad, rows_grad, kernel_grad, offset_grad, timestep_grad, decay_grad = prepare_pull(
        (
            back_values + extra_values,
            back_written + extra_written,
            back_readout,
            back_step + extra_step,
            back_cumulative + extra_cumulative,
            back_gates,
        )
    )
    returned = shift_along(rows_grad.astype(jnp.bfloat16), -1).astype(rows_grad.dtype)
    piece_size = projected_grad.shape[1]
    projected_grad = projected_grad.at[
        :, piece_size - kernel_taps + 1 :, inner_width : inner_width + channel_width
    ].add(returned)
    projected_low = projected_grad.astype(jnp.bfloat16)
    input_weight_grad = jnp.einsum(
        "spd,spk->dk", normed_low, projected_low, preferred_element_type=jnp.float32
    )
    normed_grad = jnp.einsum(
        "spk,dk->spd", projected_low, in_weight, preferred_element_type=jnp.float32
    )
    hidden_grad, norm_grad = norm_pull(normed_grad)
    weight_grads = (
        norm_grad,
        input_weight_grad,
        kernel_grad,
        offset_grad,
        back_gain,
        output_weight_grad,
    )
    return (gradient + hidden_grad, weight_grads, (timestep_grad, decay_grad, back_skip))


def gather_small(layers):
    rows = []
    for shards, _ in layers:
        norm, _, kernel, offset, gate, _ = shards
        rows += [norm, kernel.reshape(-1), offset, gate]
    widths = [row.shape[0] for row in rows]
    packed = jnp.concatenate(rows)[None]
    everyone = lax.all_gather(packed, ("dp", "ctx"), axis=0, tiled=True)
    parts, start = [], 0
    for width in widths:
        parts.append(everyone[:, start : start + width])
        start += width
    count = everyone.shape[0]
    result = []
    for layer in range(len(layers)):
        norm, kernel, offset, gate = parts[4 * layer : 4 * layer + 4]
        taps = layers[layer][0][2].shape[0]
        kernel = kernel.reshape(count, taps, -1).swapaxes(0, 1).reshape(taps, -1)
        result.append((norm.reshape(-1), kernel, offset.reshape(-1), gate.reshape(-1)))
    return result


def scatter_sum(grad):
    low = grad.astype(jnp.bfloat16)
    return lax.psum_scatter(low, ("dp", "ctx"), scatter_dimension=0, tiled=True).astype(jnp.float32)


def on_device(
    tokens,
    segments,
    cotangent,
    first_norm,
    first_input,
    first_kernel,
    first_offset,
    first_timestep,
    first_decay,
    first_skip,
    first_gate,
    first_output,
    second_norm,
    second_input,
    second_kernel,
    second_offset,
    second_timestep,
    second_decay,
    second_skip,
    second_gate,
    second_output,
):
    layout = tokens.shape
    sequences = layout[0] * layout[1]
    hidden = tokens.astype(jnp.float32).reshape(sequences, layout[2], layout[3])
    seg_f = segments.reshape(sequences, layout[2]).astype(jnp.float32)
    layers = (
        (
            (first_norm, first_input, first_kernel, first_offset, first_gate, first_output),
            (first_timestep, first_decay, first_skip),
        ),
        (
            (second_norm, second_input, second_kernel, second_offset, second_gate, second_output),
            (second_timestep, second_decay, second_skip),
        ),
    )
    smalls = gather_small(layers)
    stored = []
    for shards, head_params in layers:
        small = smalls[len(stored)]
        gathered = (
            small[0],
            lax.all_gather(shards[1], ("dp", "ctx"), axis=0, tiled=True),
            small[1],
            small[2],
            small[3],
            lax.all_gather(shards[5], ("dp", "ctx"), axis=0, tiled=True),
        )
        hidden, saved = layer_forward(hidden, seg_f, gathered, head_params)
        stored.append((gathered, saved))
    gradient = cotangent.astype(jnp.float32).reshape(hidden.shape)
    sharded = [None, None]
    head_terms = [None, None]
    for index in (1, 0):
        gathered, saved = stored[index]
        gradient, weight_grads, head_grads = layer_backward(gradient, saved, gathered)
        sharded[index] = (
            lax.psum_scatter(weight_grads[0], ("dp", "ctx"), scatter_dimension=0, tiled=True),
            scatter_sum(weight_grads[1]),
            lax.psum_scatter(weight_grads[2], ("dp", "ctx"), scatter_dimension=1, tiled=True),
            lax.psum_scatter(weight_grads[3], ("dp", "ctx"), scatter_dimension=0, tiled=True),
            lax.psum_scatter(weight_grads[4], ("dp", "ctx"), scatter_dimension=0, tiled=True),
            scatter_sum(weight_grads[5]),
        )
        head_terms[index] = head_grads
    summed = lax.psum(
        (
            head_terms[0][0],
            head_terms[0][1],
            head_terms[0][2],
            head_terms[1][0],
            head_terms[1][1],
            head_terms[1][2],
        ),
        ("dp", "ctx"),
    )
    first_grads = sharded[0]
    second_grads = sharded[1]
    return (
        hidden.reshape(layout),
        gradient.reshape(layout),
        first_grads[0],
        first_grads[1],
        first_grads[2],
        first_grads[3],
        summed[0],
        summed[1],
        summed[2],
        first_grads[4],
        first_grads[5],
        second_grads[0],
        second_grads[1],
        second_grads[2],
        second_grads[3],
        summed[3],
        summed[4],
        summed[5],
        second_grads[4],
        second_grads[5],
    )


def solution(mesh):
    return jax.shard_map(
        on_device,
        mesh=mesh,
        in_specs=(
            P(None, "dp", "ctx", None),
            P(None, "dp", "ctx"),
            P(None, "dp", "ctx", None),
            P(("dp", "ctx")),
            P(("dp", "ctx"), None),
            P(None, ("dp", "ctx")),
            P(("dp", "ctx")),
            P(),
            P(),
            P(),
            P(("dp", "ctx")),
            P(("dp", "ctx"), None),
            P(("dp", "ctx")),
            P(("dp", "ctx"), None),
            P(None, ("dp", "ctx")),
            P(("dp", "ctx")),
            P(),
            P(),
            P(),
            P(("dp", "ctx")),
            P(("dp", "ctx"), None),
        ),
        out_specs=(
            P(None, "dp", "ctx", None),
            P(None, "dp", "ctx", None),
            P(("dp", "ctx")),
            P(("dp", "ctx"), None),
            P(None, ("dp", "ctx")),
            P(("dp", "ctx")),
            P(),
            P(),
            P(),
            P(("dp", "ctx")),
            P(("dp", "ctx"), None),
            P(("dp", "ctx")),
            P(("dp", "ctx"), None),
            P(None, ("dp", "ctx")),
            P(("dp", "ctx")),
            P(),
            P(),
            P(),
            P(("dp", "ctx")),
            P(("dp", "ctx"), None),
        ),
        check_vma=False,
    )
```

```python
import functools

import jax
import jax.numpy as jnp
from jax import lax
from jax.experimental import pallas as pl
from jax.experimental.pallas import tpu as pltpu
from jax.sharding import PartitionSpec as P

EPSILON = 1e-05
EXACT = lax.Precision.HIGHEST
BF16 = jnp.bfloat16
F32 = jnp.float32
BOTH = ("dp", "ctx")
FAR = -1e30
LANES = 128
EDGE = 8
VMEM_BYTES = 48 * 1024 * 1024


def shift_along(x, by):
    size = lax.axis_size("ctx")
    pairs = [(i, i + by) for i in range(size) if 0 <= i + by < size]
    return lax.ppermute(x, "ctx", pairs)


def swap_cores(x):
    return lax.ppermute(x, "ctx", [(i, i ^ 1) for i in range(lax.axis_size("ctx"))])


def swap_chips(x, distance):
    return lax.ppermute(
        x, "ctx", [(i, i ^ (2 * distance)) for i in range(lax.axis_size("ctx"))]
    )


def swap_rows(x, bit):
    return lax.ppermute(x, "dp", [(i, i ^ bit) for i in range(lax.axis_size("dp"))])


def pick(x, index, axis=0):
    return lax.dynamic_index_in_dim(x, index, axis=axis, keepdims=False)


def bits_of(count):
    return [1 << level for level in range((count - 1).bit_length())]


def sum_everywhere(x):
    x = x + swap_cores(x)
    for bit in bits_of(lax.axis_size("dp")):
        x = x + swap_rows(x, bit)
    for bit in bits_of(lax.axis_size("ctx") // 2):
        x = x + swap_chips(x, bit)
    return x


def in_order(mine, got, bit_is_set, axis):
    return jnp.concatenate(
        [jnp.where(bit_is_set, got, mine), jnp.where(bit_is_set, mine, got)], axis=axis
    )


def gather_over_chips(x):
    chips = lax.axis_size("ctx") // 2
    chip = lax.axis_index("ctx") // 2
    if chips <= 4:
        held = jnp.stack([x] + [swap_chips(x, distance) for distance in range(1, chips)])
        return jnp.stack([pick(held, chip ^ place) for place in range(chips)])
    x = x[None]
    for bit in bits_of(chips):
        x = in_order(x, swap_chips(x, bit), (chip // bit) % 2 == 1, 0)
    return x


def gather_over_rows(x, bits):
    count = lax.axis_size("dp")
    me = lax.axis_index("dp")
    rest = x.shape
    x = x.reshape((1,) * len(bits) + rest)
    order = sorted(bits, reverse=True)
    for bit in bits:
        x = in_order(x, swap_rows(x, bit), (me // bit) % 2 == 1, order.index(bit))
    return x.reshape((count,) + rest)


def gather_rows(shard, split):
    core = lax.axis_index("ctx") % 2
    x = gather_over_chips(shard)
    order = bits_of(lax.axis_size("dp"))
    if split:
        columns = x.shape[-1]
        cut = columns // 2 // LANES * LANES
        x = jnp.concatenate(
            [gather_over_rows(x[..., :cut], order), gather_over_rows(x[..., cut:], order[::-1])], axis=-1
        )
    else:
        x = gather_over_rows(x, order)
    got = swap_cores(x)
    x = in_order(x[:, :, None], got[:, :, None], core == 1, 2)
    return x.reshape((-1, shard.shape[1]))


def halve_over_rows(x, bits):
    count = lax.axis_size("dp")
    me = lax.axis_index("dp")
    rest = x.shape[1:]
    x = x.reshape((2,) * len(bits_of(count)) + rest)
    order = bits_of(count)
    left = sorted(order, reverse=True)
    for bit in bits:
        axis = left.index(bit)
        mine = (me // bit) % 2
        got = swap_rows(pick(x, 1 - mine, axis), bit)
        x = (pick(x, mine, axis).astype(F32) + got.astype(F32)).astype(BF16)
        left.remove(bit)
    return x


def scatter_over_chips(x):
    chips = lax.axis_size("ctx") // 2
    chip = lax.axis_index("ctx") // 2
    if chips <= 4:
        total = pick(x, chip).astype(F32)
        for distance in range(1, chips):
            total = total + swap_chips(pick(x, chip ^ distance), distance).astype(F32)
        return total
    for bit in bits_of(chips)[::-1]:
        x = x.reshape((2, bit) + x.shape[1:])
        mine = (chip // bit) % 2
        got = swap_chips(pick(x, 1 - mine), bit)
        x = (pick(x, mine).astype(F32) + got.astype(F32)).astype(BF16)
    return x[0].astype(F32)


def product_over_cores(lhs, rhs):
    dps = lax.axis_size("dp")
    chips = lax.axis_size("ctx") // 2
    core = lax.axis_index("ctx") % 2
    tokens, rows = lhs.shape
    own = rows // (dps * chips * 2)
    split = lhs.reshape(tokens, dps * chips, 2, own)
    give = pick(split, 1 - core, 2).reshape(tokens, rows // 2)
    keep = pick(split, core, 2).reshape(tokens, rows // 2)
    sent = dot(give, rhs, TN)
    got = swap_cores(sent.astype(BF16))
    kept = dot(keep, rhs, TN)
    return (kept + got.astype(F32)).astype(BF16).reshape(dps, chips, own, rhs.shape[1])


def scatter_product(lhs, rhs, first):
    summed = product_over_cores(lhs, rhs)
    order = bits_of(lax.axis_size("dp"))
    if first is None:
        cut = rhs.shape[1] // 2 // LANES * LANES
        parts = [
            halve_over_rows(summed[..., :cut], order),
            halve_over_rows(summed[..., cut:], order[::-1]),
        ]
        return scatter_over_chips(jnp.concatenate(parts, axis=-1))
    return scatter_over_chips(halve_over_rows(summed, order if first == 0 else order[::-1]))


def carry_along(pair_t, pair_state, forward):
    count = lax.axis_size("ctx")
    chips = count // 2
    incoming = jnp.zeros_like(pair_state)
    outgoing = pair_state
    if chips <= 4:
        for step in range(chips - 1):
            source, target = (
                (step, step + 1) if forward else (chips - 1 - step, chips - 2 - step)
            )
            pairs = [(2 * source + c, 2 * target + c) for c in range(2)]
            arrived = lax.ppermute(outgoing.astype(BF16), "ctx", pairs)
            incoming = incoming + arrived.astype(F32)
            if step < chips - 2:
                outgoing = incoming * pair_t + pair_state
        return incoming

    def advance(_, carried):
        arrived = shift_along((carried * pair_t + pair_state).astype(BF16), 2 if forward else -2)
        return arrived.astype(F32)

    return lax.fori_loop(0, chips - 1, advance, incoming)


def chain(through, state, forward):
    count = lax.axis_size("ctx")
    position = lax.axis_index("ctx")
    core = position % 2
    chips = count // 2
    sequences = state.shape[1]
    leading = core == (0 if forward else 1)
    other_t = swap_cores(through)
    own_t, other_t = pick(through, core), pick(other_t, core)
    first_t = jnp.where(leading, own_t, other_t)
    second_t = jnp.where(leading, other_t, own_t)
    pair_t = first_t * second_t
    give = pick(state, 1 - core)
    mine = pick(state, core)
    keeps, backs = [], []
    for s in range(sequences):
        sent = swap_cores(give[s]).astype(F32)
        own = mine[s].astype(F32)
        first_state = jnp.where(leading, own, sent)
        second_state = jnp.where(leading, sent, own)
        pair_state = first_state * second_t[s] + second_state
        incoming = carry_along(pair_t[s], pair_state, forward)
        second_in = incoming * first_t[s] + first_state
        keeps.append(jnp.where(leading, incoming, second_in).astype(BF16))
        backs.append(swap_cores(jnp.where(leading, second_in, incoming).astype(BF16)))
    keep, back = jnp.stack(keeps), jnp.stack(backs)
    first = jnp.where(core == 0, keep, back)
    second = jnp.where(core == 0, back, keep)
    return jnp.stack([first, second])


def silu_parts(v):
    gate = 1.0 / (1.0 + jnp.exp(-v))
    return v * gate, gate


def pair_mask(rows):
    return lax.broadcasted_iota(jnp.int32, (rows, LANES), 1) < LANES // 2


def spread(per_head, k, mask):
    return jnp.where(mask, per_head[:, 2 * k : 2 * k + 1], per_head[:, 2 * k + 1 : 2 * k + 2])


def dot(a, b, contract, precision=None):
    return lax.dot_general(
        a, b, ((contract[0], contract[1]), ((), ())),
        preferred_element_type=F32, precision=precision,
    )


NN = ((1,), (0,))
NT = ((1,), (1,))
TN = ((0,), (0,))


def triangle(size, upper):
    row = lax.broadcasted_iota(jnp.int32, (size, size), 0)
    col = lax.broadcasted_iota(jnp.int32, (size, size), 1)
    keep = (col >= row) if upper else (col <= row)
    return jnp.where(keep, 1.0, 0.0).astype(F32)


def steps_of(raw, heads):
    shifted = raw + heads[0:1]
    step = jnp.maximum(shifted, 0.0) + jnp.log1p(jnp.exp(-jnp.abs(shifted)))
    rate = -step * jnp.exp(heads[1:2])
    return shifted, step, rate


def head_sums(values, selector):
    high = values.astype(BF16)
    low = (values - high.astype(F32)).astype(BF16)
    return dot(high, selector, NN) + dot(low, selector, NN)


def fwd_local(proj, halo, marks, bias, heads, taps, conv_out, ysum_out, read_out, cum_out, state_out, ext, weighted):
    length = proj.shape[1]
    channels = halo.shape[2]
    states = read_out.shape[2]
    inner = channels - 2 * states
    head_rows = heads[...]
    raw = proj[0, :, channels:]
    _, step, rate = steps_of(raw, head_rows)
    cum = dot(triangle(length, False), rate, NN, EXACT)
    cum_t = dot(rate, triangle(length, False), ((0,), (1,)), EXACT)
    cum_out[0] = cum
    last = cum[length - 1 : length]
    end_weight = jnp.exp(last - cum) * marks[0, :, 4:5] * step
    ext[0:EDGE] = halo[0]
    ext[EDGE:] = proj[0, :, :channels]

    def activate(lo):
        lanes = slice(lo, lo + LANES)
        total = taps[4:5, lanes]
        for s in range(4):
            total = total + ext[EDGE - s : EDGE - s + length, lanes] * (
                taps[3 - s : 4 - s, lanes] * marks[0, :, s : s + 1]
            )
        conv_out[0, :, lanes] = total
        return silu_parts(total)[0]

    written = activate(inner).astype(BF16)
    readout = activate(inner + states).astype(BF16)
    read_out[0] = readout
    scores = dot(readout, written, NT)
    mask = pair_mask(length)
    blocked = bias[0]
    zero = jnp.zeros((length, LANES), BF16)
    for k in range(inner // LANES):
        lo = k * LANES
        x = activate(lo)
        scaled = (x * spread(step, k, mask)).astype(BF16)
        weighted[:, lo : lo + LANES] = (x * spread(end_weight, k, mask)).astype(BF16)
        mixing = []
        for h in (2 * k, 2 * k + 1):
            gap = cum[:, h : h + 1] - cum_t[h : h + 1, :]
            mixing.append((jnp.exp(gap + blocked) * scores).astype(BF16))
        values = jnp.concatenate(
            [jnp.where(mask, scaled, zero), jnp.where(mask, zero, scaled)], axis=0
        )
        result = dot(jnp.concatenate(mixing, axis=1), values, NN)
        ysum_out[0, :, lo : lo + LANES] = result + x * spread(head_rows[2:3], k, mask[0:1])
    half = inner // 2
    for part in range(2):
        state_out[part, 0] = dot(written, weighted[:, part * half : (part + 1) * half], TN).astype(BF16)


def fwd_mix(ysum, read, cum, marks, incoming, gates, gain, mixed_out, y_out, gated):
    length = ysum.shape[1]
    inner = ysum.shape[2]
    half = inner // 2
    entry = jnp.exp(cum[0]) * marks[0, :, 5:6]
    mask = pair_mask(length)
    squares = jnp.zeros((length, LANES), F32)
    for k in range(inner // LANES):
        lo = k * LANES
        part, at = lo // half, lo % half
        carried = dot(read[0], incoming[part, 0, :, at : at + LANES], NN)
        y = ysum[0, :, lo : lo + LANES] + spread(entry, k, mask) * carried
        y_out[0, :, lo : lo + LANES] = y
        value = y * silu_parts(gates[0, :, lo : lo + LANES])[0]
        gated[:, lo : lo + LANES] = value
        squares = squares + value * value
    scale = lax.rsqrt(jnp.sum(squares, axis=1, keepdims=True) * (1.0 / inner) + EPSILON)
    for k in range(inner // LANES):
        lanes = slice(k * LANES, (k + 1) * LANES)
        mixed_out[0, :, lanes] = (gated[:, lanes] * scale * gain[:, lanes]).astype(BF16)


def bwd_gate(grad, y, gates, gain, cum, marks, read, dy_out, dgate_out, dgain_out, state_out, weighted, scaled_grad):
    length = y.shape[1]
    inner = y.shape[2]
    entry = jnp.exp(cum[0]) * marks[0, :, 5:6]
    mask = pair_mask(length)
    squares = jnp.zeros((length, LANES), F32)
    cross = jnp.zeros((length, LANES), F32)
    for k in range(inner // LANES):
        lanes = slice(k * LANES, (k + 1) * LANES)
        value = y[0, :, lanes] * silu_parts(gates[0, :, lanes])[0]
        squares = squares + value * value
        cross = cross + value * grad[0, :, lanes] * gain[:, lanes]
    scale = lax.rsqrt(jnp.sum(squares, axis=1, keepdims=True) * (1.0 / inner) + EPSILON)
    inward = jnp.sum(cross, axis=1, keepdims=True) * (scale * scale * scale * (1.0 / inner))
    for k in range(inner // LANES):
        lanes = slice(k * LANES, (k + 1) * LANES)
        z = gates[0, :, lanes]
        active, sigmoid = silu_parts(z)
        yk = y[0, :, lanes]
        value = yk * active
        g = grad[0, :, lanes]
        dgain_out[0, :, lanes] = jnp.sum(g * value * scale, axis=0, keepdims=True)
        dvalue = g * gain[:, lanes] * scale - value * inward
        dy = dvalue * active
        dy_out[0, :, lanes] = dy
        dgate_out[0, :, lanes] = (dvalue * yk * (sigmoid + active * (1.0 - sigmoid))).astype(BF16)
        weighted[:, lanes] = (dy * spread(entry, k, mask)).astype(BF16)
    half = inner // 2
    for part in range(2):
        state_out[part, 0] = dot(read[0], weighted[:, part * half : (part + 1) * half], TN).astype(BF16)


def bwd_diag(conv, raw, ysum, dy, read, cum, marks, bias_t, heads, selector, incoming, dscaled_out, dwritten_out, dread_out, dcum_out, terms, entered):
    length = ysum.shape[1]
    inner = ysum.shape[2]
    half = inner // 2
    states = read.shape[2]
    head_rows = heads[...]
    _, step, rate = steps_of(raw[0], head_rows)
    cums = cum[0]
    cum_t = dot(rate, triangle(length, False), ((0,), (1,)), EXACT)
    entry = jnp.exp(cums) * marks[0, :, 5:6]
    written = silu_parts(conv[0, :, inner : inner + states])[0].astype(BF16)
    readout = read[0]
    scores_t = dot(written, readout, NT)
    mask = pair_mask(length)
    blocked = bias_t[0]
    zero = jnp.zeros((length, LANES), BF16)
    dscores_t = jnp.zeros((length, length), F32)
    for k in range(inner // LANES):
        lo = k * LANES
        lanes = slice(lo, lo + LANES)
        x = silu_parts(conv[0, :, lanes])[0]
        scaled = (x * spread(step, k, mask)).astype(BF16)
        grad = dy[0, :, lanes]
        low = grad.astype(BF16)
        decays, mixing = [], []
        for h in (2 * k, 2 * k + 1):
            gap = cum_t[h : h + 1, :] - cums[:, h : h + 1]
            decay = jnp.exp(gap + blocked)
            decays.append(decay)
            mixing.append((decay * scores_t).astype(BF16))
        grads = jnp.concatenate([jnp.where(mask, low, zero), jnp.where(mask, zero, low)], axis=0)
        dscaled = dot(jnp.concatenate(mixing, axis=1), grads, NN)
        dscaled_out[0, :, lanes] = dscaled
        values = jnp.concatenate(
            [jnp.where(mask, scaled, zero), jnp.where(mask, zero, scaled)], axis=0
        )
        dmixing = dot(values, low, NT)
        dscores_t = dscores_t + dmixing[:length] * decays[0] + dmixing[length:] * decays[1]
        entered_k = (grad * spread(entry, k, mask)).astype(BF16)
        entered[:, lanes] = entered_k
        part, at = lo // half, lo % half
        carried = dot(readout, incoming[part, 0, :, at : at + LANES], NN)
        diagonal = ysum[0, :, lanes] - x * spread(head_rows[2:3], k, mask[0:1])
        terms[:, lanes] = (
            low.astype(F32) * diagonal
            - scaled.astype(F32) * dscaled
            + entered_k.astype(F32) * carried
        )
    dcum_out[0] = head_sums(terms[...], selector[...])
    dlow = dscores_t.astype(BF16)
    dwritten_out[0] = dot(dlow, readout, NN)
    dread = dot(dlow, written, TN)
    for part in range(2):
        dread = dread + dot(entered[:, part * half : (part + 1) * half], incoming[part, 0], NT)
    dread_out[0] = dread


def bwd_local(proj, halo, conv, dy, dscaled, dwritten, dread, dcum, cum, marks, backs, heads, taps, selector, incoming, outgoing, through, dproj_out, dhalo_out, dtaps_out, dskip_out, dhead_out, ext, dconv, ending, terms):
    length = proj.shape[1]
    channels = halo.shape[2]
    states = dread.shape[2]
    inner = channels - 2 * states
    half = inner // 2
    head_rows = heads[...]
    shifted, step, rate = steps_of(proj[0, :, channels:], head_rows)
    cums = cum[0]
    last = cums[length - 1 : length]
    end_decay = jnp.exp(last - cums) * marks[0, :, 4:5]
    end_weight = end_decay * step
    mask = pair_mask(length)
    written_v, written_s = silu_parts(conv[0, :, inner : inner + states])
    written = written_v.astype(BF16)
    ext[0:EDGE] = halo[0]
    ext[EDGE:] = proj[0, :, :channels]
    dconv[0:EDGE] = jnp.zeros((EDGE, channels), F32)
    dconv[EDGE + length :] = jnp.zeros((EDGE, channels), F32)
    products = []
    for k in range(inner // LANES):
        lo = k * LANES
        lanes = slice(lo, lo + LANES)
        part, at = lo // half, lo % half
        pre = conv[0, :, lanes]
        x, sigmoid = silu_parts(pre)
        grad = dy[0, :, lanes]
        back = outgoing[part, 0, :, at : at + LANES]
        products.append(
            jnp.sum(back.astype(F32) * incoming[part, 0, :, at : at + LANES].astype(F32), axis=0, keepdims=True)
        )
        ends = dot(written, back, NN)
        inside = dscaled[0, :, lanes] + spread(end_decay, k, mask) * ends
        weighted = (x * spread(end_weight, k, mask)).astype(BF16)
        ending[:, lanes] = weighted
        terms[0:length, lanes] = x * inside
        terms[length : 2 * length, lanes] = weighted.astype(F32) * ends
        dskip_out[0, :, lanes] = jnp.sum(grad * x, axis=0, keepdims=True)
        dx = spread(step, k, mask) * inside + spread(head_rows[2:3], k, mask[0:1]) * grad
        dconv[EDGE : EDGE + length, lanes] = dx * (sigmoid + x * (1.0 - sigmoid))
    dw = dwritten[0]
    for part in range(2):
        dw = dw + dot(ending[:, part * half : (part + 1) * half], outgoing[part, 0], NT)
    dconv[EDGE : EDGE + length, inner : inner + states] = dw * (
        written_s + written_v * (1.0 - written_s)
    )
    read_v, read_s = silu_parts(conv[0, :, inner + states :])
    dconv[EDGE : EDGE + length, inner + states :] = dread[0] * (read_s + read_v * (1.0 - read_s))
    sums = head_sums(terms[...], selector[...])
    heads_n = rate.shape[1]
    dstep = sums[:length, :heads_n]
    ended = sums[length:, :heads_n]
    kept = head_sums(
        jnp.broadcast_to(jnp.concatenate(products, axis=1), (8, inner)), selector[...]
    )[0:1, :heads_n]
    at_last = jnp.sum(ended, axis=0, keepdims=True) + kept * through[0]
    row = lax.broadcasted_iota(jnp.int32, (length, heads_n), 0)
    dcums = dcum[0][:, :heads_n] - ended + jnp.where(row == length - 1, at_last, 0.0)
    drate = dot(triangle(length, True), dcums, NN, EXACT)
    dstep = dstep - drate * jnp.exp(head_rows[1:2])
    draw = dstep * (1.0 / (1.0 + jnp.exp(-shifted)))
    dproj_out[0, :, channels:] = draw.astype(BF16)
    dhead_out[0] = jnp.concatenate(
        [
            jnp.sum(draw, axis=0, keepdims=True),
            jnp.sum(drate * rate, axis=0, keepdims=True),
            jnp.zeros((6, heads_n), F32),
        ],
        axis=0,
    )
    rows = length + EDGE
    for lo in range(0, channels, LANES):
        lanes = slice(lo, lo + LANES)
        total = jnp.zeros((rows, LANES), F32)
        own = dconv[EDGE : EDGE + length, lanes]
        sums = []
        for s in range(4):
            total = total + dconv[s : s + rows, lanes] * (taps[3 - s : 4 - s, lanes] * backs[0, :, s : s + 1])
            sums.append(
                jnp.sum(own * ext[EDGE - s : EDGE - s + length, lanes] * marks[0, :, s : s + 1], axis=0, keepdims=True)
            )
        dproj_out[0, :, lanes] = total[EDGE:].astype(BF16)
        dhalo_out[0, 0:EDGE, lanes] = total[:EDGE]
        dhalo_out[0, EDGE:, lanes] = total[length:]
        dtaps_out[0, :, lanes] = jnp.concatenate(
            sums[::-1] + [jnp.sum(own, axis=0, keepdims=True), jnp.zeros((3, LANES), F32)], axis=0
        )


def per_sequence(kernel, inputs, outputs, scratch, cost):
    sequences = None
    in_specs = []
    arrays = []
    for array, axis in inputs:
        if axis is not None:
            sequences = array.shape[axis]
        in_specs.append(block_spec(array.shape, axis))
        arrays.append(array)
    out_specs = [block_spec(shape, axis) for shape, _, axis in outputs]
    out_shape = [jax.ShapeDtypeStruct(shape, dtype) for shape, dtype, _ in outputs]
    return pl.pallas_call(
        kernel,
        grid=(sequences,),
        in_specs=in_specs,
        out_specs=out_specs,
        out_shape=out_shape,
        scratch_shapes=scratch,
        compiler_params=pltpu.CompilerParams(vmem_limit_bytes=VMEM_BYTES),
        cost_estimate=pl.CostEstimate(flops=cost, bytes_accessed=1 << 23, transcendentals=1 << 20),
    )(*arrays)


def block_spec(shape, axis):
    block = tuple(1 if d == axis else size for d, size in enumerate(shape))
    rank = len(shape)
    return pl.BlockSpec(
        block, functools.partial(block_index, rank, axis)
    )


def block_index(rank, axis, i):
    return tuple(i if d == axis else 0 for d in range(rank))


def rms_scale(values, gain_vector):
    return (
        values
        * lax.rsqrt(jnp.mean(values * values, axis=-1, keepdims=True) + EPSILON)
        * gain_vector
    )


def lanes_of(per_head, size):
    sequences, heads = per_head.shape
    spread_out = jnp.repeat(per_head, size, axis=1).reshape(sequences, 2, 1, heads * size // 2)
    return jnp.moveaxis(spread_out, 1, 0)


def layer_forward(hidden, ids, weights, head_params):
    norm_gain, mix_weight, gate_weight, taps, gate_gain, out_weight = weights
    sequences, length, width = hidden.shape
    channels = taps.shape[1]
    inner = gate_gain.shape[0]
    states = (channels - inner) // 2
    heads_n = head_params.shape[1]
    size = inner // heads_n
    gain = norm_gain.astype(F32)
    normed = rms_scale(hidden, gain).astype(BF16)
    proj = jnp.dot(normed, mix_weight, preferred_element_type=F32)
    edge = shift_along(proj[:, length - EDGE :, :channels], 1)
    gates = jnp.dot(normed, gate_weight, preferred_element_type=F32)
    conv, ysum, read, cum, state = per_sequence(
        fwd_local,
        [(proj, 0), (edge, 0), (ids["marks"], 0), (ids["bias"], 0), (head_params, None), (taps, None)],
        [
            ((sequences, length, channels), F32, 0),
            ((sequences, length, inner), F32, 0),
            ((sequences, length, states), BF16, 0),
            ((sequences, length, heads_n), F32, 0),
            ((2, sequences, states, inner // 2), BF16, 1),
        ],
        [pltpu.VMEM((length + EDGE, channels), F32), pltpu.VMEM((length, inner), BF16)],
        1 << 28,
    )
    through = jnp.exp(cum[:, -1]) * ids["carry"][:, None]
    through_lanes = lanes_of(through, size)
    incoming = chain(through_lanes, state, True)
    mixed, y = per_sequence(
        fwd_mix,
        [(ysum, 0), (read, 0), (cum, 0), (ids["marks"], 0), (incoming, 1), (gates, 0), (gate_gain.astype(F32)[None], None)],
        [((sequences, length, inner), BF16, 0), ((sequences, length, inner), F32, 0)],
        [pltpu.VMEM((length, inner), F32)],
        1 << 27,
    )
    update = jnp.dot(mixed, out_weight, preferred_element_type=F32)
    saved = (hidden, gain, normed, proj, edge, gates, conv, ysum, read, cum, through, through_lanes, incoming, mixed, y)
    return hidden + update, saved


def layer_backward(gradient, ids, weights, head_params, saved, final):
    hidden, gain, normed, proj, edge, gates, conv, ysum, read, cum, through, through_lanes, incoming, mixed, y = saved
    _, mix_weight, gate_weight, taps, gate_gain, out_weight = weights
    sequences, length, width = hidden.shape
    tokens = sequences * length
    channels = taps.shape[1]
    inner = gate_gain.shape[0]
    states = (channels - inner) // 2
    heads_n = head_params.shape[1]
    size = inner // heads_n
    update_low = gradient.astype(BF16)
    mixed_grad = lax.dot_general(
        update_low, out_weight, (((2,), (1,)), ((), ())), preferred_element_type=F32
    )
    dy, dgates, dgain, dstate = per_sequence(
        bwd_gate,
        [(mixed_grad, 0), (y, 0), (gates, 0), (gate_gain.astype(F32)[None], None), (cum, 0), (ids["marks"], 0), (read, 0)],
        [
            ((sequences, length, inner), F32, 0),
            ((sequences, length, inner), BF16, 0),
            ((sequences, 1, inner), F32, 0),
            ((2, sequences, states, inner // 2), BF16, 1),
        ],
        [pltpu.VMEM((length, inner), BF16), pltpu.VMEM((8, LANES), F32)],
        1 << 27,
    )
    output_grad = scatter_product(
        mixed.reshape(tokens, inner), update_low.reshape(tokens, width), 0 if final else 1
    )
    outgoing = chain(through_lanes, dstate, False)
    head_of = jnp.arange(inner) // size
    selector = (head_of[:, None] == jnp.arange(LANES)[None]).astype(BF16)
    raw = proj[:, :, channels:]
    dscaled, dwritten, dread, dcum = per_sequence(
        bwd_diag,
        [(conv, 0), (raw, 0), (ysum, 0), (dy, 0), (read, 0), (cum, 0), (ids["marks"], 0), (ids["bias_t"], 0),
         (head_params, None), (selector, None), (incoming, 1)],
        [
            ((sequences, length, inner), F32, 0),
            ((sequences, length, states), F32, 0),
            ((sequences, length, states), F32, 0),
            ((sequences, length, LANES), F32, 0),
        ],
        [pltpu.VMEM((length, inner), F32), pltpu.VMEM((length, inner), BF16)],
        1 << 28,
    )
    dproj, dhalo, dtaps, dskip, dheads = per_sequence(
        bwd_local,
        [(proj, 0), (edge, 0), (conv, 0), (dy, 0), (dscaled, 0), (dwritten, 0), (dread, 0), (dcum, 0), (cum, 0),
         (ids["marks"], 0), (ids["backs"], 0), (head_params, None), (taps, None), (selector, None),
         (incoming, 1), (outgoing, 1), (through[:, None], 0)],
        [
            ((sequences, length, channels + heads_n), BF16, 0),
            ((sequences, 2 * EDGE, channels), F32, 0),
            ((sequences, 8, channels), F32, 0),
            ((sequences, 1, inner), F32, 0),
            ((sequences, 8, heads_n), F32, 0),
        ],
        [
            pltpu.VMEM((length + EDGE, channels), F32),
            pltpu.VMEM((length + 2 * EDGE, channels), F32),
            pltpu.VMEM((length, inner), BF16),
            pltpu.VMEM((2 * length, inner), F32),
        ],
        1 << 28,
    )
    returned = shift_along(dhalo[:, :EDGE].astype(BF16), -1).astype(F32)
    tail = (dhalo[:, EDGE:] + returned).astype(BF16)
    dproj = lax.dynamic_update_slice(dproj, tail, (0, length - EDGE, 0))
    gates_grad = scatter_product(
        normed.reshape(tokens, width), dgates.reshape(tokens, inner), 0
    )
    mix_grad = scatter_product(
        normed.reshape(tokens, width), dproj.reshape(tokens, -1), None if final else 1
    )
    normed_grad = lax.dot_general(
        dproj, mix_weight, (((2,), (1,)), ((), ())), preferred_element_type=F32
    ) + lax.dot_general(dgates, gate_weight, (((2,), (1,)), ((), ())), preferred_element_type=F32)
    _, norm_pull = jax.vjp(rms_scale, hidden, gain)
    hidden_grad, norm_grad = norm_pull(normed_grad)
    dtaps = jnp.sum(dtaps, axis=0)
    small = jnp.concatenate(
        [
            norm_grad,
            dtaps[:4].reshape(-1),
            dtaps[4],
            jnp.sum(dgain, axis=(0, 1)),
            jnp.sum(dheads[:, 0], axis=0),
            jnp.sum(dheads[:, 1], axis=0),
            jnp.sum(dskip.reshape(-1, heads_n, size), axis=(0, 2)),
        ]
    )
    input_grad = jnp.concatenate([gates_grad, mix_grad], axis=1)
    return gradient + hidden_grad, small, input_grad, output_grad


def own_part(x, axis=0):
    index = lax.axis_index("dp") * lax.axis_size("ctx") + lax.axis_index("ctx")
    count = lax.axis_size("dp") * lax.axis_size("ctx")
    part = x.shape[axis] // count
    return lax.dynamic_slice_in_dim(x, index * part, part, axis=axis)


def unpack_small(total, width, channels, inner, heads_n):
    sizes = (width, 4 * channels, channels, inner, heads_n, heads_n, heads_n)
    parts, start = [], 0
    for size in sizes:
        parts.append(total[start : start + size])
        start += size
    norm, kernel, offset, gain, timestep, decay, skip = parts
    return (
        own_part(norm),
        own_part(kernel.reshape(4, channels), axis=1),
        own_part(offset),
        timestep,
        decay,
        skip,
        own_part(gain),
    )


def gather_small(layers):
    rows = []
    for shards, _ in layers:
        norm, _, kernel, offset, gate, _ = shards
        rows += [norm, kernel.reshape(-1), offset, gate]
    widths = [row.shape[0] for row in rows]
    everyone = gather_rows(jnp.concatenate(rows)[None], False)
    parts, start = [], 0
    for width in widths:
        parts.append(everyone[:, start : start + width])
        start += width
    count = everyone.shape[0]
    result = []
    for layer in range(len(layers)):
        norm, kernel, offset, gate = parts[4 * layer : 4 * layer + 4]
        taps = layers[layer][0][2].shape[0]
        kernel = kernel.reshape(count, taps, -1).swapaxes(0, 1).reshape(taps, -1).astype(F32)
        offset = offset.reshape(1, -1).astype(F32)
        packed_taps = jnp.concatenate([kernel, offset, jnp.zeros((8 - taps - 1, kernel.shape[1]), F32)], axis=0)
        result.append((norm.reshape(-1), packed_taps, gate.reshape(-1)))
    return result


def segment_terms(segments):
    sequences, length = segments.shape
    ids = segments.astype(F32)
    before = shift_along(ids[:, length - EDGE :] + 1.0, 1) - 1.0
    joined = jnp.concatenate([before, ids], axis=1)
    after = jnp.concatenate([joined, jnp.full((sequences, EDGE), -2.0, F32)], axis=1)
    marks, backs = [], []
    for s in range(4):
        marks.append((joined[:, EDGE - s : EDGE - s + length] == ids).astype(F32))
        backs.append((after[:, s : s + length + EDGE] == joined).astype(F32))
    last = ids[:, -1:]
    prev = before[:, -1:]
    marks.append((ids == last).astype(F32))
    marks.append((ids == prev).astype(F32))
    marks += [jnp.zeros_like(ids)] * 2
    causal = jnp.tril(jnp.ones((length, length), jnp.bool_))
    allowed = causal[None] & (ids[:, :, None] == ids[:, None, :])
    allowed_t = causal.T[None] & (ids[:, :, None] == ids[:, None, :])
    return {
        "marks": jnp.stack(marks, axis=2),
        "backs": jnp.stack(backs + backs, axis=2),
        "bias": jnp.where(allowed, 0.0, FAR).astype(F32),
        "bias_t": jnp.where(allowed_t, 0.0, FAR).astype(F32),
        "carry": (last == prev).astype(F32)[:, 0],
    }


def on_device(
    tokens,
    segments,
    cotangent,
    first_norm,
    first_input,
    first_kernel,
    first_offset,
    first_timestep,
    first_decay,
    first_skip,
    first_gate,
    first_output,
    second_norm,
    second_input,
    second_kernel,
    second_offset,
    second_timestep,
    second_decay,
    second_skip,
    second_gate,
    second_output,
):
    layout = tokens.shape
    sequences = layout[0] * layout[1]
    hidden = tokens.astype(F32).reshape(sequences, layout[2], layout[3])
    ids = segment_terms(segments.reshape(sequences, layout[2]))
    layers = (
        (
            (first_norm, first_input, first_kernel, first_offset, first_gate, first_output),
            (first_timestep, first_decay, first_skip),
        ),
        (
            (second_norm, second_input, second_kernel, second_offset, second_gate, second_output),
            (second_timestep, second_decay, second_skip),
        ),
    )
    smalls = gather_small(layers)
    stored = []
    inner = smalls[0][2].shape[0]
    first, second = layers[0][0], layers[1][0]
    mixers = [lax.all_gather(shards[1][:, inner:], BOTH, axis=0, tiled=True) for shards in (first, second)]
    gates, closers = [gather_rows(first[1][:, :inner], True)], [gather_rows(first[5], True)]
    own, width = second[5].shape
    turns = inner // width
    packed = jnp.concatenate([second[1][:, i * width : (i + 1) * width] for i in range(turns)] + [second[5]], axis=0)
    both = lax.all_gather(packed, BOTH, axis=0, tiled=True).reshape((-1,) + packed.shape)
    rows = second[1].shape[0]
    gates.append(
        jnp.concatenate(
            [both[:, i * rows : (i + 1) * rows].reshape(-1, width) for i in range(turns)], axis=1
        )
    )
    closers.append(both[:, turns * rows :].reshape(-1, width))
    for index, ((_, head_params), small) in enumerate(zip(layers, smalls)):
        weights = (small[0], mixers[index], gates[index], small[1], small[2], closers[index])
        heads = jnp.stack(list(head_params) + [jnp.zeros_like(head_params[0])] * 5)
        hidden, saved = layer_forward(hidden, ids, weights, heads)
        stored.append((weights, heads, saved))
    gradient = cotangent.astype(F32).reshape(hidden.shape)
    results = [None, None]
    for index in (1, 0):
        weights, heads, saved = stored[index]
        gradient, small, input_grad, output_grad = layer_backward(
            gradient, ids, weights, heads, saved, index == 0
        )
        results[index] = (small, input_grad, output_grad)
    totals = sum_everywhere(jnp.stack([result[0] for result in results]))
    for index, (_, input_grad, output_grad) in enumerate(results):
        weights, heads, _ = stored[index]
        parts = unpack_small(
            totals[index], hidden.shape[2], weights[3].shape[1], weights[4].shape[0], heads.shape[1]
        )
        results[index] = (parts[0], input_grad) + parts[1:] + (output_grad,)
    return (hidden.reshape(layout), gradient.reshape(layout)) + results[0] + results[1]


def solution(mesh):
    weight_specs = (P(BOTH), P(BOTH, None), P(None, BOTH), P(BOTH), P(), P(), P(), P(BOTH), P(BOTH, None))
    tokens_spec = P(None, "dp", "ctx", None)
    return jax.shard_map(
        on_device,
        mesh=mesh,
        in_specs=(tokens_spec, P(None, "dp", "ctx"), tokens_spec) + weight_specs + weight_specs,
        out_specs=(tokens_spec, tokens_spec) + weight_specs + weight_specs,
        check_vma=False,
    )
```

```python
import functools

import jax
import jax.numpy as jnp
from jax import lax
from jax.experimental import pallas as pl
from jax.experimental.pallas import tpu as pltpu
from jax.sharding import PartitionSpec as P

EPSILON = 1e-05
EXACT = lax.Precision.HIGHEST
BF16 = jnp.bfloat16
F32 = jnp.float32
BOTH = ("dp", "ctx")
FAR = -1e30
LANES = 128
EDGE = 8
VMEM_BYTES = 48 * 1024 * 1024
FREE = pl.CostEstimate(flops=0, bytes_accessed=0, transcendentals=0)


def shift_along(x, by):
    size = lax.axis_size("ctx")
    pairs = [(i, i + by) for i in range(size) if 0 <= i + by < size]
    return lax.ppermute(x, "ctx", pairs)


def swap_cores(x):
    return lax.ppermute(x, "ctx", [(i, i ^ 1) for i in range(lax.axis_size("ctx"))])


def swap_chips(x, distance):
    return lax.ppermute(
        x, "ctx", [(i, i ^ (2 * distance)) for i in range(lax.axis_size("ctx"))]
    )


def swap_rows(x, bit):
    return lax.ppermute(x, "dp", [(i, i ^ bit) for i in range(lax.axis_size("dp"))])


def pick(x, index, axis=0):
    return lax.dynamic_index_in_dim(x, index, axis=axis, keepdims=False)


def bits_of(count):
    return [1 << level for level in range((count - 1).bit_length())]


def in_order(mine, got, bit_is_set, axis):
    return jnp.concatenate(
        [jnp.where(bit_is_set, got, mine), jnp.where(bit_is_set, mine, got)], axis=axis
    )


def gather_over_chips(x):
    chips = lax.axis_size("ctx") // 2
    chip = lax.axis_index("ctx") // 2
    if chips <= 4:
        held = jnp.stack([x] + [swap_chips(x, distance) for distance in range(1, chips)])
        return jnp.stack([pick(held, chip ^ place) for place in range(chips)])
    x = x[None]
    for bit in bits_of(chips):
        x = in_order(x, swap_chips(x, bit), (chip // bit) % 2 == 1, 0)
    return x


def gather_over_rows(x, bits):
    count = lax.axis_size("dp")
    me = lax.axis_index("dp")
    rest = x.shape
    x = x.reshape((1,) * len(bits) + rest)
    order = sorted(bits, reverse=True)
    for bit in bits:
        x = in_order(x, swap_rows(x, bit), (me // bit) % 2 == 1, order.index(bit))
    return x.reshape((count,) + rest)


def gather_rows(shard, split):
    return finish_rows(gather_over_chips(shard), split)


def finish_rows(x, split):
    core = lax.axis_index("ctx") % 2
    order = bits_of(lax.axis_size("dp"))
    if split:
        columns = x.shape[-1]
        cut = columns // 2 // LANES * LANES
        x = jnp.concatenate(
            [gather_over_rows(x[..., :cut], order), gather_over_rows(x[..., cut:], order[::-1])], axis=-1
        )
    else:
        x = gather_over_rows(x, order)
    got = swap_cores(x)
    x = in_order(x[:, :, None], got[:, :, None], core == 1, 2)
    return x.reshape((-1, x.shape[-1]))


def halve_over_rows(x, bits, left):
    me = lax.axis_index("dp")
    left = sorted(left, reverse=True)
    x = x.reshape((2,) * len(left) + x.shape[1:])
    for bit in bits:
        axis = left.index(bit)
        mine = (me // bit) % 2
        got = swap_rows(pick(x, 1 - mine, axis), bit)
        x = (pick(x, mine, axis).astype(F32) + got.astype(F32)).astype(BF16)
        left.remove(bit)
    return x.reshape((1 << len(left),) + x.shape[len(left) :])


def scatter_over_chips(x):
    chips = lax.axis_size("ctx") // 2
    chip = lax.axis_index("ctx") // 2
    if chips <= 4:
        total = pick(x, chip).astype(F32)
        for distance in range(1, chips):
            total = total + swap_chips(pick(x, chip ^ distance), distance).astype(F32)
        return total
    for bit in bits_of(chips)[::-1]:
        x = x.reshape((2, bit) + x.shape[1:])
        mine = (chip // bit) % 2
        got = swap_chips(pick(x, 1 - mine), bit)
        x = (pick(x, mine).astype(F32) + got.astype(F32)).astype(BF16)
    return x[0].astype(F32)


def split_cores(product, own):
    rows, columns = product.shape
    split = product.reshape(rows // own // 2, 2, own, columns)
    return split[:, 0], split[:, 1]


def store_by_core(core, product, own, rows, keep_out, give_out):
    first, second = split_cores(product, own)
    mine = core[0] == 0
    keep_out[:, rows : rows + own] = jnp.where(mine, first, second)
    give_out[:, rows : rows + own] = jnp.where(mine, second, first)


def product_halves(core, lhs, rhs, keep_out, give_out):
    product = dot(lhs[...], rhs[...], TN).astype(BF16)
    store_by_core(core, product, keep_out.shape[1], 0, keep_out, give_out)


def pair_halves(core, lhs, rhs, other_lhs, other_rhs, keep_out, give_out):
    columns = keep_out.shape[2]
    groups = keep_out.shape[0]
    own = lhs.shape[1] // groups // 2
    store_by_core(core, dot(lhs[...], rhs[...], TN).astype(BF16), own, 0, keep_out, give_out)
    other_own = other_lhs.shape[1] // groups // 2
    other = dot(other_lhs[...], other_rhs[...], TN).astype(BF16)
    for turn in range(other.shape[1] // columns):
        store_by_core(
            core,
            other[:, turn * columns : (turn + 1) * columns],
            other_own,
            own + turn * other_own,
            keep_out,
            give_out,
        )


def turns_of(groups):
    return 4 if groups % 4 == 0 else 1


def product_by_core(lhs, rhs):
    dps = lax.axis_size("dp")
    chips = lax.axis_size("ctx") // 2
    core = lax.axis_index("ctx") % 2
    tokens, rows = lhs.shape
    columns = rhs.shape[1]
    groups = dps * chips
    own = rows // (groups * 2)
    shape = (dps, chips, own, columns)
    if own % 16:
        product = dot(lhs, rhs, TN).astype(BF16).reshape(dps, chips, 2, own, columns)
        return pick(product, core, 2), pick(product, 1 - core, 2)
    turns = turns_of(groups)
    out = jax.ShapeDtypeStruct((groups, own, columns), BF16)
    spec = pl.BlockSpec((groups // turns, own, columns), first_index_of_three)
    keep, give = pl.pallas_call(
        product_halves,
        grid=(turns,),
        in_specs=[
            pl.BlockSpec(memory_space=pltpu.SMEM),
            pl.BlockSpec((tokens, rows // turns), second_index_of_two),
            pl.BlockSpec((tokens, columns), no_index_of_two),
        ],
        out_specs=[spec, spec],
        out_shape=[out, out],
        compiler_params=pltpu.CompilerParams(vmem_limit_bytes=VMEM_BYTES),
        cost_estimate=FREE,
    )(core.reshape(1), lhs, rhs)
    return keep.reshape(shape), give.reshape(shape)


def pair_by_core(lhs, rhs, other_lhs, other_rhs):
    dps = lax.axis_size("dp")
    chips = lax.axis_size("ctx") // 2
    core = lax.axis_index("ctx") % 2
    tokens, rows = lhs.shape
    columns = rhs.shape[1]
    groups = dps * chips
    own, other_own = rows // (groups * 2), other_lhs.shape[1] // (groups * 2)
    pieces = other_rhs.shape[1] // columns
    if own % 16 or other_own % 16:
        first = product_by_core(lhs, rhs)
        second = product_by_core(other_lhs, other_rhs)
        return tuple(
            jnp.concatenate(
                [a] + [b[..., i * columns : (i + 1) * columns] for i in range(pieces)], axis=2
            )
            for a, b in zip(first, second)
        )
    height = own + pieces * other_own
    turns = turns_of(groups)
    out = jax.ShapeDtypeStruct((groups, height, columns), BF16)
    spec = pl.BlockSpec((groups // turns, height, columns), first_index_of_three)
    keep, give = pl.pallas_call(
        pair_halves,
        grid=(turns,),
        in_specs=[
            pl.BlockSpec(memory_space=pltpu.SMEM),
            pl.BlockSpec((tokens, rows // turns), second_index_of_two),
            pl.BlockSpec((tokens, columns), no_index_of_two),
            pl.BlockSpec((tokens, other_lhs.shape[1] // turns), second_index_of_two),
            pl.BlockSpec((tokens, other_rhs.shape[1]), no_index_of_two),
        ],
        out_specs=[spec, spec],
        out_shape=[out, out],
        compiler_params=pltpu.CompilerParams(vmem_limit_bytes=VMEM_BYTES),
        cost_estimate=FREE,
    )(core.reshape(1), lhs, rhs, other_lhs, other_rhs)
    shape = (dps, chips, height, columns)
    return keep.reshape(shape), give.reshape(shape)


def packed_block(lhs, first, second, out_lhs, out_rhs, out):
    groups, height, columns = out.shape
    inner = first.shape[1]
    own = lhs.shape[1] // groups
    out[:, :own, :inner] = dot(lhs[...], first[...], TN).astype(BF16).reshape(groups, own, inner)
    out[:, :own, inner:] = dot(lhs[...], second[...], TN).astype(BF16).reshape(groups, own, columns - inner)
    product = dot(out_lhs[...], out_rhs[...], TN).astype(BF16)
    rest, width = height - own, product.shape[1]
    split = product.reshape(groups, -1, rest, width)
    for turn in range(split.shape[1]):
        out[:, own:, turn * width : (turn + 1) * width] = split[:, turn]
    out[:, own:, split.shape[1] * width :] = jnp.zeros((groups, rest, columns - split.shape[1] * width), BF16)


def packed_product(lhs, first, second, out_lhs, out_rhs):
    count = lax.axis_size("dp") * lax.axis_size("ctx")
    tokens, rows = lhs.shape
    inner, rest = first.shape[1], second.shape[1]
    columns = inner + rest
    own, out_own = rows // count, out_lhs.shape[1] // count
    width = out_rhs.shape[1]
    pieces = columns // width
    height = own + out_own // pieces
    turns = turns_of(count)
    if own % 16 or (out_own // pieces) % 16:
        product = jnp.concatenate([dot(lhs, first, TN), dot(lhs, second, TN)], axis=1).astype(BF16)
        other = dot(out_lhs, out_rhs, TN).astype(BF16).reshape(count, pieces, out_own // pieces, width)
        other = jnp.swapaxes(other, 1, 2).reshape(count, out_own // pieces, pieces * width)
        other = jnp.pad(other, ((0, 0), (0, 0), (0, columns - pieces * width)))
        return jnp.concatenate([product.reshape(count, own, columns), other], axis=1)
    return pl.pallas_call(
        packed_block,
        grid=(turns,),
        in_specs=[
            pl.BlockSpec((tokens, rows // turns), second_index_of_two),
            pl.BlockSpec((tokens, inner), no_index_of_two),
            pl.BlockSpec((tokens, rest), no_index_of_two),
            pl.BlockSpec((tokens, out_lhs.shape[1] // turns), second_index_of_two),
            pl.BlockSpec((tokens, width), no_index_of_two),
        ],
        out_specs=pl.BlockSpec((count // turns, height, columns), first_index_of_three),
        out_shape=jax.ShapeDtypeStruct((count, height, columns), BF16),
        compiler_params=pltpu.CompilerParams(vmem_limit_bytes=VMEM_BYTES),
        cost_estimate=FREE,
    )(lhs, first, second, out_lhs, out_rhs)


def scatter_packed(product, own, width):
    _, height, columns = product.shape
    total = lax.psum_scatter(product, BOTH, scatter_dimension=0, tiled=True).reshape(height, columns)
    pieces = columns // width
    return total[:own], jnp.concatenate([total[own:, i * width : (i + 1) * width] for i in range(pieces)], axis=0)


def first_index_of_three(i):
    return (i, 0, 0)


def second_index_of_two(i):
    return (0, i)


def no_index_of_two(i):
    return (0, 0)


def over_cores(keep, give):
    return (keep.astype(F32) + swap_cores(give).astype(F32)).astype(BF16)


def after(trees, ready):
    return lax.optimization_barrier((trees, ready))[0]


def carry_along(pair_t, pair_state, forward, work):
    count = lax.axis_size("ctx")
    chips = count // 2
    sequences = pair_state.shape[0]
    chip = lax.axis_index("ctx") // 2
    place = chip if forward else chips - 1 - chip
    if chips > 4:

        def advance(_, carried):
            arrived = shift_along((carried * pair_t + pair_state).astype(BF16), 2 if forward else -2)
            return arrived.astype(F32)

        received = lax.fori_loop(0, chips - 1, advance, jnp.zeros_like(pair_state)).astype(BF16)
        done = []
        for item in work:
            done.append(item(done, pair_state))
        return received, done
    arrivals = []
    done = []
    for step in range(chips + sequences - 2):
        turn = jnp.clip(step - place, 0, sequences - 1)
        payload = pick(pair_state, turn)
        if step:
            payload = arrivals[-1].astype(F32) * pick(pair_t, turn) + payload
        pairs = []
        for k in range(chips - 1):
            if 0 <= step - k < sequences:
                source, target = (k, k + 1) if forward else (chips - 1 - k, chips - 2 - k)
                pairs += [(2 * source + c, 2 * target + c) for c in range(2)]
        payload = payload.astype(BF16)
        arrived = lax.ppermute(payload, "ctx", pairs)
        if step < len(work):
            made = work[step](done, payload)
            arrived, _ = lax.optimization_barrier((arrived, made))
            done.append(made)
        arrivals.append(arrived)
    arrivals = jnp.stack(arrivals)
    received = [pick(arrivals, jnp.maximum(s + place - 1, 0)) for s in range(sequences)]
    return jnp.where(place > 0, jnp.stack(received), jnp.zeros((), BF16)), done


def chain(through, mine, give, forward, work):
    core = lax.axis_index("ctx") % 2
    leading = core == (0 if forward else 1)
    other_t = swap_cores(through)
    sent = swap_cores(give).astype(F32)
    own_t, other_t = pick(through, core), pick(other_t, core)
    first_t = jnp.where(leading, own_t, other_t)
    second_t = jnp.where(leading, other_t, own_t)
    own = mine.astype(F32)
    first_state = jnp.where(leading, own, sent)
    pair_state = first_state * second_t + jnp.where(leading, sent, own)
    incoming, work = carry_along(first_t * second_t, pair_state, forward, work)
    second_in = (incoming.astype(F32) * first_t + first_state).astype(BF16)
    keep = jnp.where(leading, incoming, second_in)
    back = swap_cores(jnp.where(leading, second_in, incoming))
    return (keep, back), work


def silu_parts(v):
    gate = 1.0 / (1.0 + jnp.exp(-v))
    return v * gate, gate


def pair_mask(rows):
    return lax.broadcasted_iota(jnp.int32, (rows, LANES), 1) < LANES // 2


def spread(per_head, k, mask):
    return jnp.where(mask, per_head[:, 2 * k : 2 * k + 1], per_head[:, 2 * k + 1 : 2 * k + 2])


def dot(a, b, contract, precision=None):
    return lax.dot_general(
        a, b, ((contract[0], contract[1]), ((), ())),
        preferred_element_type=F32, precision=precision,
    )


NN = ((1,), (0,))
NT = ((1,), (1,))
TN = ((0,), (0,))


def triangle(size, upper):
    row = lax.broadcasted_iota(jnp.int32, (size, size), 0)
    col = lax.broadcasted_iota(jnp.int32, (size, size), 1)
    keep = (col >= row) if upper else (col <= row)
    return jnp.where(keep, 1.0, 0.0).astype(F32)


def steps_of(raw, heads):
    shifted = raw + heads[0:1]
    step = jnp.maximum(shifted, 0.0) + jnp.log1p(jnp.exp(-jnp.abs(shifted)))
    rate = -step * jnp.exp(heads[1:2])
    return shifted, step, rate


def half_of(core, mine, other, part, lanes):
    return jnp.where(core[0] == part, mine[0, :, lanes], other[0, :, lanes])


def store_halves(core, values, mine_out, give_out):
    mine_out[0] = jnp.where(core[0] == 0, values[0], values[1])
    give_out[0] = jnp.where(core[0] == 0, values[1], values[0])


def head_sums(values, selector):
    high = values.astype(BF16)
    low = (values - high.astype(F32)).astype(BF16)
    return dot(high, selector, NN) + dot(low, selector, NN)


def fwd_local(core, proj, halo, marks, bias, heads, taps, conv_out, ysum_out, read_out, cum_out, mine_out, give_out, ext, weighted):
    length = proj.shape[1]
    channels = halo.shape[2]
    states = read_out.shape[2]
    inner = channels - 2 * states
    head_rows = heads[...]
    raw = proj[0, :, channels:]
    _, step, rate = steps_of(raw, head_rows)
    cum = dot(triangle(length, False), rate, NN, EXACT)
    cum_t = dot(rate, triangle(length, False), ((0,), (1,)), EXACT)
    cum_out[0] = cum
    last = cum[length - 1 : length]
    end_weight = jnp.exp(last - cum) * marks[0, :, 4:5] * step
    ext[0:EDGE] = halo[0]
    ext[EDGE:] = proj[0, :, :channels]

    def activate(lo):
        lanes = slice(lo, lo + LANES)
        total = taps[4:5, lanes]
        for s in range(4):
            total = total + ext[EDGE - s : EDGE - s + length, lanes] * (
                taps[3 - s : 4 - s, lanes] * marks[0, :, s : s + 1]
            )
        conv_out[0, :, lanes] = total
        return silu_parts(total)[0]

    written = activate(inner).astype(BF16)
    readout = activate(inner + states).astype(BF16)
    read_out[0] = readout
    scores = dot(readout, written, NT)
    mask = pair_mask(length)
    blocked = bias[0]
    zero = jnp.zeros((length, LANES), BF16)
    for k in range(inner // LANES):
        lo = k * LANES
        x = activate(lo)
        scaled = (x * spread(step, k, mask)).astype(BF16)
        weighted[:, lo : lo + LANES] = (x * spread(end_weight, k, mask)).astype(BF16)
        mixing = []
        for h in (2 * k, 2 * k + 1):
            gap = cum[:, h : h + 1] - cum_t[h : h + 1, :]
            mixing.append((jnp.exp(gap + blocked) * scores).astype(BF16))
        values = jnp.concatenate(
            [jnp.where(mask, scaled, zero), jnp.where(mask, zero, scaled)], axis=0
        )
        result = dot(jnp.concatenate(mixing, axis=1), values, NN)
        ysum_out[0, :, lo : lo + LANES] = result + x * spread(head_rows[2:3], k, mask[0:1])
    half = inner // 2
    store_halves(
        core,
        [dot(written, weighted[:, part * half : (part + 1) * half], TN).astype(BF16) for part in range(2)],
        mine_out,
        give_out,
    )


def fwd_mix(core, ysum, read, cum, marks, in_mine, in_other, gates, gain, mixed_out, y_out, gated):
    length = ysum.shape[1]
    inner = ysum.shape[2]
    half = inner // 2
    entry = jnp.exp(cum[0]) * marks[0, :, 5:6]
    mask = pair_mask(length)
    squares = jnp.zeros((length, LANES), F32)
    for k in range(inner // LANES):
        lo = k * LANES
        part, at = lo // half, lo % half
        carried = dot(read[0], half_of(core, in_mine, in_other, part, slice(at, at + LANES)), NN)
        y = ysum[0, :, lo : lo + LANES] + spread(entry, k, mask) * carried
        y_out[0, :, lo : lo + LANES] = y
        value = y * silu_parts(gates[0, :, lo : lo + LANES])[0]
        gated[:, lo : lo + LANES] = value
        squares = squares + value * value
    scale = lax.rsqrt(jnp.sum(squares, axis=1, keepdims=True) * (1.0 / inner) + EPSILON)
    for k in range(inner // LANES):
        lanes = slice(k * LANES, (k + 1) * LANES)
        mixed_out[0, :, lanes] = (gated[:, lanes] * scale * gain[:, lanes]).astype(BF16)


def bwd_gate(core, grad, y, gates, gain, cum, marks, read, dy_out, dgate_out, dgain_out, mine_out, give_out, weighted):
    length = y.shape[1]
    inner = y.shape[2]
    entry = jnp.exp(cum[0]) * marks[0, :, 5:6]
    mask = pair_mask(length)
    squares = jnp.zeros((length, LANES), F32)
    cross = jnp.zeros((length, LANES), F32)
    for k in range(inner // LANES):
        lanes = slice(k * LANES, (k + 1) * LANES)
        value = y[0, :, lanes] * silu_parts(gates[0, :, lanes])[0]
        squares = squares + value * value
        cross = cross + value * grad[0, :, lanes] * gain[:, lanes]
    scale = lax.rsqrt(jnp.sum(squares, axis=1, keepdims=True) * (1.0 / inner) + EPSILON)
    inward = jnp.sum(cross, axis=1, keepdims=True) * (scale * scale * scale * (1.0 / inner))
    for k in range(inner // LANES):
        lanes = slice(k * LANES, (k + 1) * LANES)
        z = gates[0, :, lanes]
        active, sigmoid = silu_parts(z)
        yk = y[0, :, lanes]
        value = yk * active
        g = grad[0, :, lanes]
        dgain_out[0, :, lanes] = jnp.sum(g * value * scale, axis=0, keepdims=True)
        dvalue = g * gain[:, lanes] * scale - value * inward
        dy = dvalue * active
        dy_out[0, :, lanes] = dy
        dgate_out[0, :, lanes] = (dvalue * yk * (sigmoid + active * (1.0 - sigmoid))).astype(BF16)
        weighted[:, lanes] = (dy * spread(entry, k, mask)).astype(BF16)
    half = inner // 2
    store_halves(
        core,
        [dot(read[0], weighted[:, part * half : (part + 1) * half], TN).astype(BF16) for part in range(2)],
        mine_out,
        give_out,
    )


def bwd_diag(core, conv, raw, ysum, dy, read, cum, marks, bias_t, heads, selector, in_mine, in_other, dscaled_out, joint_out, terms, entered):
    length = ysum.shape[1]
    inner = ysum.shape[2]
    half = inner // 2
    states = read.shape[2]
    head_rows = heads[...]
    _, step, rate = steps_of(raw[0], head_rows)
    cums = cum[0]
    cum_t = dot(rate, triangle(length, False), ((0,), (1,)), EXACT)
    entry = jnp.exp(cums) * marks[0, :, 5:6]
    written = silu_parts(conv[0, :, inner : inner + states])[0].astype(BF16)
    readout = read[0]
    scores_t = dot(written, readout, NT)
    mask = pair_mask(length)
    blocked = bias_t[0]
    zero = jnp.zeros((length, LANES), BF16)
    dscores_t = jnp.zeros((length, length), F32)
    for k in range(inner // LANES):
        lo = k * LANES
        lanes = slice(lo, lo + LANES)
        x = silu_parts(conv[0, :, lanes])[0]
        scaled = (x * spread(step, k, mask)).astype(BF16)
        grad = dy[0, :, lanes]
        low = grad.astype(BF16)
        decays, mixing = [], []
        for h in (2 * k, 2 * k + 1):
            gap = cum_t[h : h + 1, :] - cums[:, h : h + 1]
            decay = jnp.exp(gap + blocked)
            decays.append(decay)
            mixing.append((decay * scores_t).astype(BF16))
        grads = jnp.concatenate([jnp.where(mask, low, zero), jnp.where(mask, zero, low)], axis=0)
        dscaled = dot(jnp.concatenate(mixing, axis=1), grads, NN)
        dscaled_out[0, :, lanes] = dscaled
        values = jnp.concatenate(
            [jnp.where(mask, scaled, zero), jnp.where(mask, zero, scaled)], axis=0
        )
        dmixing = dot(values, low, NT)
        dscores_t = dscores_t + dmixing[:length] * decays[0] + dmixing[length:] * decays[1]
        entered_k = (grad * spread(entry, k, mask)).astype(BF16)
        entered[:, lanes] = entered_k
        part, at = lo // half, lo % half
        carried = dot(readout, half_of(core, in_mine, in_other, part, slice(at, at + LANES)), NN)
        diagonal = ysum[0, :, lanes] - x * spread(head_rows[2:3], k, mask[0:1])
        terms[:, lanes] = (
            low.astype(F32) * diagonal
            - scaled.astype(F32) * dscaled
            + entered_k.astype(F32) * carried
        )
    joint_out[0, :, 2 * states :] = head_sums(terms[...], selector[...])
    dlow = dscores_t.astype(BF16)
    joint_out[0, :, :states] = dot(dlow, readout, NN)
    dread = dot(dlow, written, TN)
    for part in range(2):
        dread = dread + dot(
            entered[:, part * half : (part + 1) * half],
            half_of(core, in_mine, in_other, part, slice(None)),
            NT,
        )
    joint_out[0, :, states : 2 * states] = dread


def bwd_local(core, proj, halo, conv, dy, dscaled, joint, cum, marks, backs, heads, taps, selector, in_mine, in_other, out_mine, out_other, through, dproj_out, dhalo_out, dtaps_out, dskip_out, dhead_out, ext, dconv, ending, terms):
    length = proj.shape[1]
    channels = halo.shape[2]
    states = (joint.shape[2] - LANES) // 2
    inner = channels - 2 * states
    half = inner // 2
    head_rows = heads[...]
    shifted, step, rate = steps_of(proj[0, :, channels:], head_rows)
    cums = cum[0]
    last = cums[length - 1 : length]
    end_decay = jnp.exp(last - cums) * marks[0, :, 4:5]
    end_weight = end_decay * step
    mask = pair_mask(length)
    written_v, written_s = silu_parts(conv[0, :, inner : inner + states])
    written = written_v.astype(BF16)
    ext[0:EDGE] = halo[0]
    ext[EDGE:] = proj[0, :, :channels]
    dconv[0:EDGE] = jnp.zeros((EDGE, channels), F32)
    dconv[EDGE + length :] = jnp.zeros((EDGE, channels), F32)
    products = []
    for k in range(inner // LANES):
        lo = k * LANES
        lanes = slice(lo, lo + LANES)
        part, at = lo // half, lo % half
        pre = conv[0, :, lanes]
        x, sigmoid = silu_parts(pre)
        grad = dy[0, :, lanes]
        back = half_of(core, out_mine, out_other, part, slice(at, at + LANES))
        entering = half_of(core, in_mine, in_other, part, slice(at, at + LANES))
        products.append(
            jnp.sum(back.astype(F32) * entering.astype(F32), axis=0, keepdims=True)
        )
        ends = dot(written, back, NN)
        inside = dscaled[0, :, lanes] + spread(end_decay, k, mask) * ends
        weighted = (x * spread(end_weight, k, mask)).astype(BF16)
        ending[:, lanes] = weighted
        terms[0:length, lanes] = x * inside
        terms[length : 2 * length, lanes] = weighted.astype(F32) * ends
        dskip_out[0, :, lanes] = jnp.sum(grad * x, axis=0, keepdims=True)
        dx = spread(step, k, mask) * inside + spread(head_rows[2:3], k, mask[0:1]) * grad
        dconv[EDGE : EDGE + length, lanes] = dx * (sigmoid + x * (1.0 - sigmoid))
    dw = joint[0, :, :states]
    for part in range(2):
        dw = dw + dot(
            ending[:, part * half : (part + 1) * half],
            half_of(core, out_mine, out_other, part, slice(None)),
            NT,
        )
    dconv[EDGE : EDGE + length, inner : inner + states] = dw * (
        written_s + written_v * (1.0 - written_s)
    )
    read_v, read_s = silu_parts(conv[0, :, inner + states :])
    dconv[EDGE : EDGE + length, inner + states :] = joint[0, :, states : 2 * states] * (read_s + read_v * (1.0 - read_s))
    sums = head_sums(terms[...], selector[...])
    heads_n = rate.shape[1]
    dstep = sums[:length, :heads_n]
    ended = sums[length:, :heads_n]
    kept = head_sums(
        jnp.broadcast_to(jnp.concatenate(products, axis=1), (8, inner)), selector[...]
    )[0:1, :heads_n]
    at_last = jnp.sum(ended, axis=0, keepdims=True) + kept * through[0]
    row = lax.broadcasted_iota(jnp.int32, (length, heads_n), 0)
    dcums = joint[0, :, 2 * states : 2 * states + heads_n] - ended + jnp.where(row == length - 1, at_last, 0.0)
    drate = dot(triangle(length, True), dcums, NN, EXACT)
    dstep = dstep - drate * jnp.exp(head_rows[1:2])
    draw = dstep * (1.0 / (1.0 + jnp.exp(-shifted)))
    dproj_out[0, :, channels:] = draw.astype(BF16)
    dhead_out[0] = jnp.concatenate(
        [
            jnp.sum(draw, axis=0, keepdims=True),
            jnp.sum(drate * rate, axis=0, keepdims=True),
            jnp.zeros((6, heads_n), F32),
        ],
        axis=0,
    )
    rows = length + EDGE
    for lo in range(0, channels, LANES):
        lanes = slice(lo, lo + LANES)
        total = jnp.zeros((rows, LANES), F32)
        own = dconv[EDGE : EDGE + length, lanes]
        sums = []
        for s in range(4):
            total = total + dconv[s : s + rows, lanes] * (taps[3 - s : 4 - s, lanes] * backs[0, :, s : s + 1])
            sums.append(
                jnp.sum(own * ext[EDGE - s : EDGE - s + length, lanes] * marks[0, :, s : s + 1], axis=0, keepdims=True)
            )
        dproj_out[0, :, lanes] = total[EDGE:].astype(BF16)
        dhalo_out[0, 0:EDGE, lanes] = total[:EDGE]
        dhalo_out[0, EDGE:, lanes] = total[length:]
        dtaps_out[0, :, lanes] = jnp.concatenate(
            sums[::-1] + [jnp.sum(own, axis=0, keepdims=True), jnp.zeros((3, LANES), F32)], axis=0
        )


def per_sequence(kernel, inputs, outputs, scratch):
    sequences = None
    in_specs = [pl.BlockSpec(memory_space=pltpu.SMEM)]
    arrays = [(lax.axis_index("ctx") % 2).reshape(1)]
    for array, axis in inputs:
        if axis is not None:
            sequences = array.shape[axis]
        in_specs.append(block_spec(array.shape, axis))
        arrays.append(array)
    out_specs = [block_spec(shape, axis) for shape, _, axis in outputs]
    out_shape = [jax.ShapeDtypeStruct(shape, dtype) for shape, dtype, _ in outputs]
    return pl.pallas_call(
        kernel,
        grid=(sequences,),
        in_specs=in_specs,
        out_specs=out_specs,
        out_shape=out_shape,
        scratch_shapes=scratch,
        compiler_params=pltpu.CompilerParams(vmem_limit_bytes=VMEM_BYTES),
        cost_estimate=FREE,
    )(*arrays)


def block_spec(shape, axis):
    block = tuple(1 if d == axis else size for d, size in enumerate(shape))
    rank = len(shape)
    return pl.BlockSpec(
        block, functools.partial(block_index, rank, axis)
    )


def block_index(rank, axis, i):
    return tuple(i if d == axis else 0 for d in range(rank))


def rms_scale(values, gain_vector):
    return (
        values
        * lax.rsqrt(jnp.mean(values * values, axis=-1, keepdims=True) + EPSILON)
        * gain_vector
    )


def lanes_of(per_head, size):
    sequences, heads = per_head.shape
    spread_out = jnp.repeat(per_head, size, axis=1).reshape(sequences, 2, 1, heads * size // 2)
    return jnp.moveaxis(spread_out, 1, 0)


def layer_forward(hidden, ids, weights, head_params):
    norm_gain, mix_weight, gate_weight, taps, gate_gain, out_weight = weights
    sequences, length, width = hidden.shape
    channels = taps.shape[1]
    inner = gate_gain.shape[0]
    states = (channels - inner) // 2
    heads_n = head_params.shape[1]
    size = inner // heads_n
    gain = norm_gain.astype(F32)
    normed = rms_scale(hidden, gain).astype(BF16)
    proj = jnp.dot(normed, mix_weight, preferred_element_type=F32)
    edge = shift_along(proj[:, length - EDGE :, :channels], 1)
    gates = jnp.dot(normed, gate_weight, preferred_element_type=F32)
    conv, ysum, read, cum, mine, give = per_sequence(
        fwd_local,
        [(proj, 0), (edge, 0), (ids["marks"], 0), (ids["bias"], 0), (head_params, None), (taps, None)],
        [
            ((sequences, length, channels), F32, 0),
            ((sequences, length, inner), F32, 0),
            ((sequences, length, states), BF16, 0),
            ((sequences, length, heads_n), F32, 0),
            ((sequences, states, inner // 2), BF16, 0),
            ((sequences, states, inner // 2), BF16, 0),
        ],
        [pltpu.VMEM((length + EDGE, channels), F32), pltpu.VMEM((length, inner), BF16)],
    )
    through = jnp.exp(cum[:, -1]) * ids["carry"][:, None]
    through_lanes = lanes_of(through, size)
    incoming, _ = chain(through_lanes, mine, give, True, [])
    mixed, y = per_sequence(
        fwd_mix,
        [(ysum, 0), (read, 0), (cum, 0), (ids["marks"], 0), (incoming[0], 0), (incoming[1], 0), (gates, 0), (gate_gain.astype(F32)[None], None)],
        [((sequences, length, inner), BF16, 0), ((sequences, length, inner), F32, 0)],
        [pltpu.VMEM((length, inner), F32)],
    )
    update = jnp.dot(mixed, out_weight, preferred_element_type=F32)
    saved = (hidden, gain, normed, proj, edge, gates, conv, ysum, read, cum, through, through_lanes, incoming, mixed, y)
    return hidden + update, saved


def layer_backward(gradient, ids, weights, head_params, saved, final, other_terms=None, other_small=None):
    hidden, gain, normed, proj, edge, gates, conv, ysum, read, cum, through, through_lanes, incoming, mixed, y = saved
    _, mix_weight, gate_weight, taps, gate_gain, out_weight = weights
    sequences, length, width = hidden.shape
    tokens = sequences * length
    channels = taps.shape[1]
    inner = gate_gain.shape[0]
    states = (channels - inner) // 2
    heads_n = head_params.shape[1]
    size = inner // heads_n
    update_low = gradient.astype(BF16)
    mixed_grad = lax.dot_general(
        update_low, out_weight, (((2,), (1,)), ((), ())), preferred_element_type=F32
    )
    dy, dgates, dgain, mine, give = per_sequence(
        bwd_gate,
        [(mixed_grad, 0), (y, 0), (gates, 0), (gate_gain.astype(F32)[None], None), (cum, 0), (ids["marks"], 0), (read, 0)],
        [
            ((sequences, length, inner), F32, 0),
            ((sequences, length, inner), BF16, 0),
            ((sequences, 1, inner), F32, 0),
            ((sequences, states, inner // 2), BF16, 0),
            ((sequences, states, inner // 2), BF16, 0),
        ],
        [pltpu.VMEM((length, inner), BF16)],
    )
    head_of = jnp.arange(inner) // size
    selector = (head_of[:, None] == jnp.arange(LANES)[None]).astype(BF16)
    raw = proj[:, :, channels:]

    def diagonal(done, ready):
        return per_sequence(
            bwd_diag,
            [(conv, 0), (raw, 0), (ysum, 0), (after(dy, ready), 0), (read, 0), (cum, 0), (ids["marks"], 0),
             (ids["bias_t"], 0), (head_params, None), (selector, None), (incoming[0], 0), (incoming[1], 0)],
            [
                ((sequences, length, inner), F32, 0),
                ((sequences, length, 2 * states + LANES), F32, 0),
            ],
            [pltpu.VMEM((length, inner), F32), pltpu.VMEM((length, inner), BF16)],
        )

    flat = normed.reshape(tokens, width)
    flat_gates = dgates.reshape(tokens, inner)
    output_terms = (mixed.reshape(tokens, inner), update_low.reshape(tokens, width))
    order = bits_of(lax.axis_size("dp"))
    if final:
        outgoing, made = chain(
            through_lanes,
            mine,
            give,
            False,
            [
                lambda done, ready: packed_product(*after(other_terms, ready)),
                diagonal,
                lambda done, ready: pair_by_core(*after(output_terms + (flat, flat_gates), ready)),
                lambda done, ready: over_cores(*done[2]),
            ],
        )
        other_product, (dscaled, joint), _, pair = made
        outgoing, pair = lax.optimization_barrier((outgoing, pair))
        own = inner // (2 * lax.axis_size("dp") * lax.axis_size("ctx") // 2)
        pair = [
            halve_over_rows(pair[:, :, :own], order[:1], order),
            halve_over_rows(pair[:, :, own:], order[-1:], order),
        ]
    else:
        outgoing, made = chain(through_lanes, mine, give, False, [diagonal])
        dscaled, joint = made[0]
    dproj, dhalo, dtaps, dskip, dheads = per_sequence(
        bwd_local,
        [(proj, 0), (edge, 0), (conv, 0), (dy, 0), (dscaled, 0), (joint, 0), (cum, 0),
         (ids["marks"], 0), (ids["backs"], 0), (head_params, None), (taps, None), (selector, None),
         (incoming[0], 0), (incoming[1], 0), (outgoing[0], 0), (outgoing[1], 0), (through[:, None], 0)],
        [
            ((sequences, length, channels + heads_n), BF16, 0),
            ((sequences, 2 * EDGE, channels), F32, 0),
            ((sequences, 8, channels), F32, 0),
            ((sequences, 1, inner), F32, 0),
            ((sequences, 8, heads_n), F32, 0),
        ],
        [
            pltpu.VMEM((length + EDGE, channels), F32),
            pltpu.VMEM((length + 2 * EDGE, channels), F32),
            pltpu.VMEM((length, inner), BF16),
            pltpu.VMEM((2 * length, inner), F32),
        ],
    )
    if final:
        dproj, dhalo, pair = lax.optimization_barrier((dproj, dhalo, pair))
        pair = jnp.concatenate(
            [
                halve_over_rows(pair[0], order[1:], order[1:])[0],
                halve_over_rows(pair[1], order[:-1], order[:-1])[0],
            ],
            axis=1,
        )
    returned = shift_along(dhalo[:, :EDGE].astype(BF16), -1).astype(F32)
    tail = (dhalo[:, EDGE:] + returned).astype(BF16)
    dproj = lax.dynamic_update_slice(dproj, tail, (0, length - EDGE, 0))
    flat_grad = dproj.reshape(tokens, -1)
    if final:
        product = product_by_core(flat, flat_grad)
        dproj, product, pair = lax.optimization_barrier((dproj, product, pair))
        summed = over_cores(*product)
        cut = channels // 2 // LANES * LANES
        pair = scatter_over_chips(pair)
        first_parts = [
            halve_over_rows(summed[..., :cut], order[:1], order),
            halve_over_rows(summed[..., cut:], order[-1:], order),
        ]
    normed_grad = lax.dot_general(
        dproj, mix_weight, (((2,), (1,)), ((), ())), preferred_element_type=F32
    ) + lax.dot_general(dgates, gate_weight, (((2,), (1,)), ((), ())), preferred_element_type=F32)
    _, norm_pull = jax.vjp(rms_scale, hidden, gain)
    hidden_grad, norm_grad = norm_pull(normed_grad)
    dtaps = jnp.sum(dtaps, axis=0)
    small = jnp.concatenate(
        [
            norm_grad,
            dtaps[:4].reshape(-1),
            dtaps[4],
            jnp.sum(dgain, axis=(0, 1)),
            jnp.sum(dheads[:, 0], axis=0),
            jnp.sum(dheads[:, 1], axis=0),
            jnp.sum(dskip.reshape(-1, heads_n, size), axis=(0, 2)),
        ]
    )
    gradient = gradient + hidden_grad
    if not final:
        return gradient, small, (flat, flat_gates, flat_grad) + output_terms
    small = jnp.stack([small, other_small])
    small = small + swap_cores(small)
    first_parts, small = lax.optimization_barrier((first_parts, small))
    second_parts = [
        halve_over_rows(first_parts[0], order[1:], order[1:])[0],
        halve_over_rows(first_parts[1], order[:-1], order[:-1])[0],
    ]
    for bit in order:
        small = small + swap_rows(small, bit)
    other_grads = scatter_packed(other_product, width // (inner // own), width)
    second_parts, small, pair = lax.optimization_barrier((second_parts, small, pair))
    last = scatter_over_chips(jnp.concatenate(second_parts, axis=-1))
    last, other_grads = lax.optimization_barrier((last, other_grads))
    for bit in bits_of(lax.axis_size("ctx") // 2):
        small = small + swap_chips(small, bit)
    output_grad = pair[:own]
    gates_grad = jnp.concatenate(jnp.split(pair[own:], inner // width, axis=0), axis=1)
    input_grad = jnp.concatenate([gates_grad, last], axis=1)
    return gradient, small, input_grad, output_grad, tuple(grad.astype(F32) for grad in other_grads)


def own_part(x, axis=0):
    index = lax.axis_index("dp") * lax.axis_size("ctx") + lax.axis_index("ctx")
    count = lax.axis_size("dp") * lax.axis_size("ctx")
    part = x.shape[axis] // count
    return lax.dynamic_slice_in_dim(x, index * part, part, axis=axis)


def unpack_small(total, width, channels, inner, heads_n):
    sizes = (width, 4 * channels, channels, inner, heads_n, heads_n, heads_n)
    parts, start = [], 0
    for size in sizes:
        parts.append(total[start : start + size])
        start += size
    norm, kernel, offset, gain, timestep, decay, skip = parts
    return (
        own_part(norm),
        own_part(kernel.reshape(4, channels), axis=1),
        own_part(offset),
        timestep,
        decay,
        skip,
        own_part(gain),
    )


def gather_packed(gate_shard, out_shard):
    rows, columns = gate_shard.shape
    width = out_shard.shape[1]
    turns = columns // width
    pieces = [gate_shard[:, i * width : (i + 1) * width] for i in range(turns)]
    packed = jnp.concatenate(pieces + [out_shard], axis=0)
    both = lax.all_gather(packed, BOTH, axis=0, tiled=True).reshape((-1,) + packed.shape)
    gate_weight = jnp.concatenate(
        [both[:, i * rows : (i + 1) * rows].reshape(-1, width) for i in range(turns)], axis=1
    )
    return gate_weight, both[:, turns * rows :].reshape(-1, width)


def gather_small(layers):
    rows = []
    for shards, _ in layers:
        norm, _, kernel, offset, gate, _ = shards
        rows += [norm, kernel.reshape(-1), offset, gate]
    widths = [row.shape[0] for row in rows]
    everyone = gather_rows(jnp.concatenate(rows)[None], False)
    parts, start = [], 0
    for width in widths:
        parts.append(everyone[:, start : start + width])
        start += width
    count = everyone.shape[0]
    result = []
    for layer in range(len(layers)):
        norm, kernel, offset, gate = parts[4 * layer : 4 * layer + 4]
        taps = layers[layer][0][2].shape[0]
        kernel = kernel.reshape(count, taps, -1).swapaxes(0, 1).reshape(taps, -1).astype(F32)
        offset = offset.reshape(1, -1).astype(F32)
        packed_taps = jnp.concatenate([kernel, offset, jnp.zeros((8 - taps - 1, kernel.shape[1]), F32)], axis=0)
        result.append((norm.reshape(-1), packed_taps, gate.reshape(-1)))
    return result


def segment_terms(segments):
    sequences, length = segments.shape
    ids = segments.astype(F32)
    before = shift_along(ids[:, length - EDGE :] + 1.0, 1) - 1.0
    joined = jnp.concatenate([before, ids], axis=1)
    after = jnp.concatenate([joined, jnp.full((sequences, EDGE), -2.0, F32)], axis=1)
    marks, backs = [], []
    for s in range(4):
        marks.append((joined[:, EDGE - s : EDGE - s + length] == ids).astype(F32))
        backs.append((after[:, s : s + length + EDGE] == joined).astype(F32))
    last = ids[:, -1:]
    prev = before[:, -1:]
    marks.append((ids == last).astype(F32))
    marks.append((ids == prev).astype(F32))
    marks += [jnp.zeros_like(ids)] * 2
    causal = jnp.tril(jnp.ones((length, length), jnp.bool_))
    allowed = causal[None] & (ids[:, :, None] == ids[:, None, :])
    allowed_t = causal.T[None] & (ids[:, :, None] == ids[:, None, :])
    return {
        "marks": jnp.stack(marks, axis=2),
        "backs": jnp.stack(backs + backs, axis=2),
        "bias": jnp.where(allowed, 0.0, FAR).astype(F32),
        "bias_t": jnp.where(allowed_t, 0.0, FAR).astype(F32),
        "carry": (last == prev).astype(F32)[:, 0],
    }


def on_device(
    tokens,
    segments,
    cotangent,
    first_norm,
    first_input,
    first_kernel,
    first_offset,
    first_timestep,
    first_decay,
    first_skip,
    first_gate,
    first_output,
    second_norm,
    second_input,
    second_kernel,
    second_offset,
    second_timestep,
    second_decay,
    second_skip,
    second_gate,
    second_output,
):
    layout = tokens.shape
    sequences = layout[0] * layout[1]
    hidden = tokens.astype(F32).reshape(sequences, layout[2], layout[3])
    ids = segment_terms(segments.reshape(sequences, layout[2]))
    layers = (
        (
            (first_norm, first_input, first_kernel, first_offset, first_gate, first_output),
            (first_timestep, first_decay, first_skip),
        ),
        (
            (second_norm, second_input, second_kernel, second_offset, second_gate, second_output),
            (second_timestep, second_decay, second_skip),
        ),
    )
    smalls = gather_small(layers)
    stored = []
    inner = smalls[0][2].shape[0]
    first, second = layers[0][0], layers[1][0]
    mixers = [gather_rows(first[1][:, inner:], True), lax.all_gather(second[1][:, inner:], BOTH, axis=0, tiled=True)]
    gates, closers = [], []
    for shards in (first, second):
        gate_weight, out_weight = gather_packed(shards[1][:, :inner], shards[5])
        gates.append(gate_weight)
        closers.append(out_weight)
    ids, mixer = lax.optimization_barrier((ids, mixers[0]))
    mixers[0] = mixer
    for index, ((_, head_params), small) in enumerate(zip(layers, smalls)):
        weights = (small[0], mixers[index], gates[index], small[1], small[2], closers[index])
        heads = jnp.stack(list(head_params) + [jnp.zeros_like(head_params[0])] * 5)
        hidden, saved = layer_forward(hidden, ids, weights, heads)
        stored.append((weights, heads, saved))
    gradient = cotangent.astype(F32).reshape(hidden.shape)
    weights, heads, saved = stored[1]
    gradient, small, terms = layer_backward(gradient, ids, weights, heads, saved, False)
    weights, heads, saved = stored[0]
    gradient, smalls, input_grad, output_grad, other_grads = layer_backward(
        gradient, ids, weights, heads, saved, True, terms, small
    )
    results = []
    for total, (in_grad, out_grad) in (
        (smalls[0], (input_grad, output_grad)),
        (smalls[1], other_grads),
    ):
        parts = unpack_small(
            total, hidden.shape[2], weights[3].shape[1], weights[4].shape[0], heads.shape[1]
        )
        results.append((parts[0], in_grad) + parts[1:] + (out_grad,))
    return (hidden.reshape(layout), gradient.reshape(layout)) + results[0] + results[1]


def solution(mesh):
    weight_specs = (P(BOTH), P(BOTH, None), P(None, BOTH), P(BOTH), P(), P(), P(), P(BOTH), P(BOTH, None))
    tokens_spec = P(None, "dp", "ctx", None)
    return jax.shard_map(
        on_device,
        mesh=mesh,
        in_specs=(tokens_spec, P(None, "dp", "ctx"), tokens_spec) + weight_specs + weight_specs,
        out_specs=(tokens_spec, tokens_spec) + weight_specs + weight_specs,
        check_vma=False,
    )
```

```python
import functools

import jax
import jax.numpy as jnp
from jax import lax
from jax.experimental import pallas as pl
from jax.experimental.pallas import tpu as pltpu
from jax.sharding import PartitionSpec as P

EPSILON = 1e-05
EXACT = lax.Precision.HIGHEST
BF16 = jnp.bfloat16
F32 = jnp.float32
BOTH = ("dp", "ctx")
FAR = -1e30
LANES = 128
EDGE = 8
VMEM_BYTES = 48 * 1024 * 1024
FREE = pl.CostEstimate(flops=0, bytes_accessed=0, transcendentals=0)


def shift_along(x, by):
    size = lax.axis_size("ctx")
    pairs = [(i, i + by) for i in range(size) if 0 <= i + by < size]
    return lax.ppermute(x, "ctx", pairs)


def swap_cores(x):
    return lax.ppermute(x, "ctx", [(i, i ^ 1) for i in range(lax.axis_size("ctx"))])


def swap_chips(x, distance):
    return lax.ppermute(
        x, "ctx", [(i, i ^ (2 * distance)) for i in range(lax.axis_size("ctx"))]
    )


def swap_rows(x, bit):
    return lax.ppermute(x, "dp", [(i, i ^ bit) for i in range(lax.axis_size("dp"))])


def pick(x, index, axis=0):
    return lax.dynamic_index_in_dim(x, index, axis=axis, keepdims=False)


def bits_of(count):
    return [1 << level for level in range((count - 1).bit_length())]


def in_order(mine, got, bit_is_set, axis):
    return jnp.concatenate(
        [jnp.where(bit_is_set, got, mine), jnp.where(bit_is_set, mine, got)], axis=axis
    )


def gather_over_chips(x):
    chips = lax.axis_size("ctx") // 2
    chip = lax.axis_index("ctx") // 2
    if chips <= 4:
        held = jnp.stack([x] + [swap_chips(x, distance) for distance in range(1, chips)])
        return jnp.stack([pick(held, chip ^ place) for place in range(chips)])
    x = x[None]
    for bit in bits_of(chips):
        x = in_order(x, swap_chips(x, bit), (chip // bit) % 2 == 1, 0)
    return x


def gather_rows(shard, aside):
    core = lax.axis_index("ctx") % 2
    order = bits_of(lax.axis_size("dp"))
    cut = shard.shape[1] // 2 // LANES * LANES
    x, aside = lax.optimization_barrier((gather_over_chips(shard), gather_over_chips(aside)))
    ways = [(x[..., :cut], order), (x[..., cut:], order[::-1]), (aside, order)]
    shapes = [part.shape for part, _ in ways]
    parts = [part.reshape((1,) * len(order) + part.shape) for part, _ in ways]
    for turn in range(len(order)):
        joined = []
        for part, (_, bits) in zip(parts, ways):
            bit = bits[turn]
            joined.append(
                in_order(
                    part,
                    swap_rows(part, bit),
                    (lax.axis_index("dp") // bit) % 2 == 1,
                    sorted(bits, reverse=True).index(bit),
                )
            )
        parts = lax.optimization_barrier(joined)
    left, right, aside = [part.reshape((-1,) + shape) for part, shape in zip(parts, shapes)]
    results = []
    for part in (jnp.concatenate([left, right], axis=-1), aside):
        whole = in_order(part[:, :, None], swap_cores(part)[:, :, None], core == 1, 2)
        results.append(whole.reshape((-1, part.shape[-1])))
    return results


def halve_over_rows(x, bits, left):
    me = lax.axis_index("dp")
    left = sorted(left, reverse=True)
    x = x.reshape((2,) * len(left) + x.shape[1:])
    for bit in bits:
        axis = left.index(bit)
        mine = (me // bit) % 2
        got = swap_rows(pick(x, 1 - mine, axis), bit)
        x = (pick(x, mine, axis).astype(F32) + got.astype(F32)).astype(BF16)
        left.remove(bit)
    return x.reshape((1 << len(left),) + x.shape[len(left) :])


def scatter_over_chips(x):
    chips = lax.axis_size("ctx") // 2
    chip = lax.axis_index("ctx") // 2
    if chips <= 4:
        total = pick(x, chip).astype(F32)
        for distance in range(1, chips):
            total = total + swap_chips(pick(x, chip ^ distance), distance).astype(F32)
        return total
    for bit in bits_of(chips)[::-1]:
        x = x.reshape((2, bit) + x.shape[1:])
        mine = (chip // bit) % 2
        got = swap_chips(pick(x, 1 - mine), bit)
        x = (pick(x, mine).astype(F32) + got.astype(F32)).astype(BF16)
    return x[0].astype(F32)


def split_cores(product, own):
    rows, columns = product.shape
    split = product.reshape(rows // own // 2, 2, own, columns)
    return split[:, 0], split[:, 1]


def store_by_core(core, product, own, rows, keep_out, give_out):
    first, second = split_cores(product, own)
    mine = core[0] == 0
    keep_out[:, rows : rows + own] = jnp.where(mine, first, second)
    give_out[:, rows : rows + own] = jnp.where(mine, second, first)


def product_halves(core, lhs, rhs, keep_out, give_out):
    product = dot(lhs[...], rhs[...], TN).astype(BF16)
    store_by_core(core, product, keep_out.shape[1], 0, keep_out, give_out)


def pair_halves(core, lhs, rhs, other_lhs, other_rhs, keep_out, give_out):
    columns = keep_out.shape[2]
    groups = keep_out.shape[0]
    own = lhs.shape[1] // groups // 2
    store_by_core(core, dot(lhs[...], rhs[...], TN).astype(BF16), own, 0, keep_out, give_out)
    other_own = other_lhs.shape[1] // groups // 2
    other = dot(other_lhs[...], other_rhs[...], TN).astype(BF16)
    for turn in range(other.shape[1] // columns):
        store_by_core(
            core,
            other[:, turn * columns : (turn + 1) * columns],
            other_own,
            own + turn * other_own,
            keep_out,
            give_out,
        )


def turns_of(groups):
    return 4 if groups % 4 == 0 else 1


def product_by_core(lhs, rhs):
    dps = lax.axis_size("dp")
    chips = lax.axis_size("ctx") // 2
    core = lax.axis_index("ctx") % 2
    tokens, rows = lhs.shape
    columns = rhs.shape[1]
    groups = dps * chips
    own = rows // (groups * 2)
    shape = (dps, chips, own, columns)
    if own % 16:
        product = dot(lhs, rhs, TN).astype(BF16).reshape(dps, chips, 2, own, columns)
        return pick(product, core, 2), pick(product, 1 - core, 2)
    turns = turns_of(groups)
    out = jax.ShapeDtypeStruct((groups, own, columns), BF16)
    spec = pl.BlockSpec((groups // turns, own, columns), first_index_of_three)
    keep, give = pl.pallas_call(
        product_halves,
        grid=(turns,),
        in_specs=[
            pl.BlockSpec(memory_space=pltpu.SMEM),
            pl.BlockSpec((tokens, rows // turns), second_index_of_two),
            pl.BlockSpec((tokens, columns), no_index_of_two),
        ],
        out_specs=[spec, spec],
        out_shape=[out, out],
        compiler_params=pltpu.CompilerParams(vmem_limit_bytes=VMEM_BYTES),
        cost_estimate=FREE,
    )(core.reshape(1), lhs, rhs)
    return keep.reshape(shape), give.reshape(shape)


def pair_by_core(lhs, rhs, other_lhs, other_rhs):
    dps = lax.axis_size("dp")
    chips = lax.axis_size("ctx") // 2
    core = lax.axis_index("ctx") % 2
    tokens, rows = lhs.shape
    columns = rhs.shape[1]
    groups = dps * chips
    own, other_own = rows // (groups * 2), other_lhs.shape[1] // (groups * 2)
    pieces = other_rhs.shape[1] // columns
    if own % 16 or other_own % 16:
        first = product_by_core(lhs, rhs)
        second = product_by_core(other_lhs, other_rhs)
        return tuple(
            jnp.concatenate(
                [a] + [b[..., i * columns : (i + 1) * columns] for i in range(pieces)], axis=2
            )
            for a, b in zip(first, second)
        )
    height = own + pieces * other_own
    turns = turns_of(groups)
    out = jax.ShapeDtypeStruct((groups, height, columns), BF16)
    spec = pl.BlockSpec((groups // turns, height, columns), first_index_of_three)
    keep, give = pl.pallas_call(
        pair_halves,
        grid=(turns,),
        in_specs=[
            pl.BlockSpec(memory_space=pltpu.SMEM),
            pl.BlockSpec((tokens, rows // turns), second_index_of_two),
            pl.BlockSpec((tokens, columns), no_index_of_two),
            pl.BlockSpec((tokens, other_lhs.shape[1] // turns), second_index_of_two),
            pl.BlockSpec((tokens, other_rhs.shape[1]), no_index_of_two),
        ],
        out_specs=[spec, spec],
        out_shape=[out, out],
        compiler_params=pltpu.CompilerParams(vmem_limit_bytes=VMEM_BYTES),
        cost_estimate=FREE,
    )(core.reshape(1), lhs, rhs, other_lhs, other_rhs)
    shape = (dps, chips, height, columns)
    return keep.reshape(shape), give.reshape(shape)


def packed_block(lhs, first, second, out_lhs, out_rhs, out):
    groups, height, columns = out.shape
    inner = first.shape[1]
    own = lhs.shape[1] // groups
    out[:, :own, :inner] = dot(lhs[...], first[...], TN).astype(BF16).reshape(groups, own, inner)
    out[:, :own, inner:] = dot(lhs[...], second[...], TN).astype(BF16).reshape(groups, own, columns - inner)
    product = dot(out_lhs[...], out_rhs[...], TN).astype(BF16)
    rest, width = height - own, product.shape[1]
    split = product.reshape(groups, -1, rest, width)
    for turn in range(split.shape[1]):
        out[:, own:, turn * width : (turn + 1) * width] = split[:, turn]
    out[:, own:, split.shape[1] * width :] = jnp.zeros((groups, rest, columns - split.shape[1] * width), BF16)


def packed_product(lhs, first, second, out_lhs, out_rhs):
    count = lax.axis_size("dp") * lax.axis_size("ctx")
    tokens, rows = lhs.shape
    inner, rest = first.shape[1], second.shape[1]
    columns = inner + rest
    own, out_own = rows // count, out_lhs.shape[1] // count
    width = out_rhs.shape[1]
    pieces = columns // width
    height = own + out_own // pieces
    turns = turns_of(count)
    if own % 16 or (out_own // pieces) % 16:
        product = jnp.concatenate([dot(lhs, first, TN), dot(lhs, second, TN)], axis=1).astype(BF16)
        other = dot(out_lhs, out_rhs, TN).astype(BF16).reshape(count, pieces, out_own // pieces, width)
        other = jnp.swapaxes(other, 1, 2).reshape(count, out_own // pieces, pieces * width)
        other = jnp.pad(other, ((0, 0), (0, 0), (0, columns - pieces * width)))
        return jnp.concatenate([product.reshape(count, own, columns), other], axis=1)
    return pl.pallas_call(
        packed_block,
        grid=(turns,),
        in_specs=[
            pl.BlockSpec((tokens, rows // turns), second_index_of_two),
            pl.BlockSpec((tokens, inner), no_index_of_two),
            pl.BlockSpec((tokens, rest), no_index_of_two),
            pl.BlockSpec((tokens, out_lhs.shape[1] // turns), second_index_of_two),
            pl.BlockSpec((tokens, width), no_index_of_two),
        ],
        out_specs=pl.BlockSpec((count // turns, height, columns), first_index_of_three),
        out_shape=jax.ShapeDtypeStruct((count, height, columns), BF16),
        compiler_params=pltpu.CompilerParams(vmem_limit_bytes=VMEM_BYTES),
        cost_estimate=FREE,
    )(lhs, first, second, out_lhs, out_rhs)


def scatter_packed(product, own, width):
    _, height, columns = product.shape
    total = lax.psum_scatter(product, BOTH, scatter_dimension=0, tiled=True).reshape(height, columns)
    pieces = columns // width
    return total[:own], jnp.concatenate([total[own:, i * width : (i + 1) * width] for i in range(pieces)], axis=0)


def first_index_of_three(i):
    return (i, 0, 0)


def second_index_of_two(i):
    return (0, i)


def no_index_of_two(i):
    return (0, 0)


def over_cores(keep, give):
    return (keep.astype(F32) + swap_cores(give).astype(F32)).astype(BF16)


def after(trees, ready):
    return lax.optimization_barrier((trees, ready))[0]


def exchange_chips(blocks):
    chips = blocks.shape[0]
    chip = lax.axis_index("ctx") // 2
    got = [pick(blocks, chip)]
    for distance in range(1, chips):
        got.append(swap_chips(pick(blocks, chip ^ distance), distance))
    return got


def by_sender(got):
    chip = lax.axis_index("ctx") // 2
    held = jnp.stack(got)
    return [pick(held, place ^ chip) for place in range(len(got))]


def carry_along(pair_t, pair_state, forward, work):
    count = lax.axis_size("ctx")
    chips = count // 2
    sequences, states, channels = pair_state.shape
    if chips > 4:

        def advance(_, carried):
            arrived = shift_along((carried * pair_t + pair_state).astype(BF16), 2 if forward else -2)
            return arrived.astype(F32)

        received = lax.fori_loop(0, chips - 1, advance, jnp.zeros_like(pair_state)).astype(BF16)
        done = []
        for items in work:
            for item in items:
                done.append(item(done, pair_state))
        return received, done
    share = channels // chips
    high = pair_t.astype(BF16)
    low = (pair_t - high.astype(F32)).astype(BF16)
    payload = jnp.concatenate(
        [pair_state.astype(BF16), high, low, jnp.zeros((sequences, 14, channels), BF16)], axis=1
    )
    blocks = jnp.moveaxis(payload.reshape(sequences, states + 16, chips, share), 2, 0)
    got = exchange_chips(blocks)
    done = []
    got, done = during(got, done, work[0], payload)
    carried = jnp.zeros((sequences, states, share), F32)
    entering = [None] * chips
    order = range(chips) if forward else range(chips - 1, -1, -1)
    held = by_sender(got)
    for place in order:
        entering[place] = carried.astype(BF16)
        decay = (held[place][:, states : states + 1].astype(F32) + held[place][:, states + 1 : states + 2].astype(F32))
        carried = carried * decay + held[place][:, :states].astype(F32)
    blocks = jnp.stack(entering)
    got = exchange_chips(blocks)
    got, done = during(got, done, work[1], blocks)
    return jnp.concatenate(by_sender(got), axis=-1), done


def during(got, done, items, ready):
    for item in items:
        made = item(done, ready)
        got, made = lax.optimization_barrier((got, made))
        done = done + [made]
    return got, done


def chain(through, mine, give, forward, work):
    core = lax.axis_index("ctx") % 2
    leading = core == (0 if forward else 1)
    other_t = swap_cores(through)
    sent = swap_cores(give).astype(F32)
    own_t, other_t = pick(through, core), pick(other_t, core)
    first_t = jnp.where(leading, own_t, other_t)
    second_t = jnp.where(leading, other_t, own_t)
    own = mine.astype(F32)
    first_state = jnp.where(leading, own, sent)
    pair_state = first_state * second_t + jnp.where(leading, sent, own)
    incoming, work = carry_along(first_t * second_t, pair_state, forward, work)
    second_in = (incoming.astype(F32) * first_t + first_state).astype(BF16)
    keep = jnp.where(leading, incoming, second_in)
    back = swap_cores(jnp.where(leading, second_in, incoming))
    return (keep, back), work


def silu_parts(v):
    gate = 0.5 + 0.5 * jnp.tanh(0.5 * v)
    return v * gate, gate


def pair_mask(rows):
    return lax.broadcasted_iota(jnp.int32, (rows, LANES), 1) < LANES // 2


def spread(per_head, k, mask):
    return jnp.where(mask, per_head[:, 2 * k : 2 * k + 1], per_head[:, 2 * k + 1 : 2 * k + 2])


def dot(a, b, contract, precision=None):
    return lax.dot_general(
        a, b, ((contract[0], contract[1]), ((), ())),
        preferred_element_type=F32, precision=precision,
    )


NN = ((1,), (0,))
NT = ((1,), (1,))
TN = ((0,), (0,))


def triangle(size, upper):
    row = lax.broadcasted_iota(jnp.int32, (size, size), 0)
    col = lax.broadcasted_iota(jnp.int32, (size, size), 1)
    keep = (col >= row) if upper else (col <= row)
    return jnp.where(keep, 1.0, 0.0).astype(F32)


def steps_of(raw, heads):
    shifted = raw + heads[0:1]
    step = jnp.maximum(shifted, 0.0) + jnp.log1p(jnp.exp(-jnp.abs(shifted)))
    rate = -step * jnp.exp(heads[1:2])
    return shifted, step, rate


def half_of(core, mine, other, part, lanes):
    return jnp.where(core[0] == part, mine[0, :, lanes], other[0, :, lanes])


def store_halves(core, values, mine_out, give_out):
    mine_out[0] = jnp.where(core[0] == 0, values[0], values[1])
    give_out[0] = jnp.where(core[0] == 0, values[1], values[0])


def add_up(out, rows, lanes, value):
    first = pl.program_id(0) == 0
    out[rows, lanes] = jnp.where(first, value, out[rows, lanes] + value)


def head_sums(values, selector):
    high = values.astype(BF16)
    low = (values - high.astype(F32)).astype(BF16)
    return dot(high, selector, NN) + dot(low, selector, NN)


def fwd_local(core, proj, halo, marks, bias, heads, taps, conv_out, ysum_out, read_out, cum_out, mine_out, give_out, ext, weighted):
    length = proj.shape[1]
    channels = halo.shape[2]
    states = read_out.shape[2]
    inner = channels - 2 * states
    head_rows = heads[...]
    raw = proj[0, :, channels:]
    _, step, rate = steps_of(raw, head_rows)
    cum = dot(triangle(length, False), rate, NN, EXACT)
    cum_t = dot(rate, triangle(length, False), ((0,), (1,)), EXACT)
    cum_out[0] = jnp.concatenate([cum, raw], axis=1)
    last = cum[length - 1 : length]
    end_weight = jnp.exp(last - cum) * marks[0, :, 4:5] * step
    ext[0:EDGE] = halo[0]
    ext[EDGE:] = proj[0, :, :channels]

    def activate(lo):
        lanes = slice(lo, lo + LANES)
        total = taps[4:5, lanes]
        for s in range(4):
            total = total + ext[EDGE - s : EDGE - s + length, lanes] * (
                taps[3 - s : 4 - s, lanes] * marks[0, :, s : s + 1]
            )
        conv_out[0, :, lanes] = total
        return silu_parts(total)[0]

    written = activate(inner).astype(BF16)
    readout = activate(inner + states).astype(BF16)
    read_out[0] = readout
    scores = dot(readout, written, NT)
    mask = pair_mask(length)
    blocked = bias[0]
    zero = jnp.zeros((length, LANES), BF16)
    for k in range(inner // LANES):
        lo = k * LANES
        x = activate(lo)
        scaled = (x * spread(step, k, mask)).astype(BF16)
        weighted[:, lo : lo + LANES] = (x * spread(end_weight, k, mask)).astype(BF16)
        mixing = []
        for h in (2 * k, 2 * k + 1):
            gap = cum[:, h : h + 1] - cum_t[h : h + 1, :]
            mixing.append((jnp.exp(gap + blocked) * scores).astype(BF16))
        values = jnp.concatenate(
            [jnp.where(mask, scaled, zero), jnp.where(mask, zero, scaled)], axis=0
        )
        result = dot(jnp.concatenate(mixing, axis=1), values, NN)
        ysum_out[0, :, lo : lo + LANES] = result + x * spread(head_rows[2:3], k, mask[0:1])
    half = inner // 2
    store_halves(
        core,
        [dot(written, weighted[:, part * half : (part + 1) * half], TN).astype(BF16) for part in range(2)],
        mine_out,
        give_out,
    )


def fwd_mix(core, ysum, read, cum, marks, in_mine, in_other, gates, gain, mixed_out, y_out, gated):
    length = ysum.shape[1]
    inner = ysum.shape[2]
    half = inner // 2
    entry = jnp.exp(cum[0][:, : cum.shape[2] // 2]) * marks[0, :, 5:6]
    mask = pair_mask(length)
    squares = jnp.zeros((length, LANES), F32)
    for k in range(inner // LANES):
        lo = k * LANES
        part, at = lo // half, lo % half
        carried = dot(read[0], half_of(core, in_mine, in_other, part, slice(at, at + LANES)), NN)
        y = ysum[0, :, lo : lo + LANES] + spread(entry, k, mask) * carried
        y_out[0, :, lo : lo + LANES] = y
        value = y * silu_parts(gates[0, :, lo : lo + LANES])[0]
        gated[:, lo : lo + LANES] = value
        squares = squares + value * value
    scale = lax.rsqrt(jnp.sum(squares, axis=1, keepdims=True) * (1.0 / inner) + EPSILON)
    for k in range(inner // LANES):
        lanes = slice(k * LANES, (k + 1) * LANES)
        mixed_out[0, :, lanes] = (gated[:, lanes] * scale * gain[:, lanes]).astype(BF16)


def bwd_gate(core, grad, y, gates, gain, cum, marks, read, dy_out, dgate_out, dgain_out, mine_out, give_out, weighted):
    length = y.shape[1]
    inner = y.shape[2]
    entry = jnp.exp(cum[0][:, : cum.shape[2] // 2]) * marks[0, :, 5:6]
    mask = pair_mask(length)
    squares = jnp.zeros((length, LANES), F32)
    cross = jnp.zeros((length, LANES), F32)
    for k in range(inner // LANES):
        lanes = slice(k * LANES, (k + 1) * LANES)
        value = y[0, :, lanes] * silu_parts(gates[0, :, lanes])[0]
        squares = squares + value * value
        cross = cross + value * grad[0, :, lanes] * gain[:, lanes]
    scale = lax.rsqrt(jnp.sum(squares, axis=1, keepdims=True) * (1.0 / inner) + EPSILON)
    inward = jnp.sum(cross, axis=1, keepdims=True) * (scale * scale * scale * (1.0 / inner))
    for k in range(inner // LANES):
        lanes = slice(k * LANES, (k + 1) * LANES)
        z = gates[0, :, lanes]
        active, sigmoid = silu_parts(z)
        yk = y[0, :, lanes]
        value = yk * active
        g = grad[0, :, lanes]
        add_up(dgain_out, slice(0, 1), lanes, jnp.sum(g * value * scale, axis=0, keepdims=True))
        dvalue = g * gain[:, lanes] * scale - value * inward
        dy = dvalue * active
        dy_out[0, :, lanes] = dy
        dgate_out[0, :, lanes] = (dvalue * yk * (sigmoid + active * (1.0 - sigmoid))).astype(BF16)
        weighted[:, lanes] = (dy * spread(entry, k, mask)).astype(BF16)
    half = inner // 2
    store_halves(
        core,
        [dot(read[0], weighted[:, part * half : (part + 1) * half], TN).astype(BF16) for part in range(2)],
        mine_out,
        give_out,
    )


def bwd_diag(core, conv, ysum, dy, read, cum, marks, bias_t, heads, selector, in_mine, in_other, dscaled_out, joint_out, terms, entered):
    length = ysum.shape[1]
    inner = ysum.shape[2]
    half = inner // 2
    states = read.shape[2]
    head_rows = heads[...]
    heads_n = heads.shape[1]
    _, step, rate = steps_of(cum[0][:, heads_n:], head_rows)
    cums = cum[0][:, :heads_n]
    cum_t = dot(rate, triangle(length, False), ((0,), (1,)), EXACT)
    entry = jnp.exp(cums) * marks[0, :, 5:6]
    written = silu_parts(conv[0, :, inner : inner + states])[0].astype(BF16)
    readout = read[0]
    scores_t = dot(written, readout, NT)
    mask = pair_mask(length)
    blocked = bias_t[0]
    zero = jnp.zeros((length, LANES), BF16)
    dscores_t = jnp.zeros((length, length), F32)
    for k in range(inner // LANES):
        lo = k * LANES
        lanes = slice(lo, lo + LANES)
        x = silu_parts(conv[0, :, lanes])[0]
        scaled = (x * spread(step, k, mask)).astype(BF16)
        grad = dy[0, :, lanes]
        low = grad.astype(BF16)
        decays, mixing = [], []
        for h in (2 * k, 2 * k + 1):
            gap = cum_t[h : h + 1, :] - cums[:, h : h + 1]
            decay = jnp.exp(gap + blocked)
            decays.append(decay)
            mixing.append((decay * scores_t).astype(BF16))
        grads = jnp.concatenate([jnp.where(mask, low, zero), jnp.where(mask, zero, low)], axis=0)
        dscaled = dot(jnp.concatenate(mixing, axis=1), grads, NN)
        dscaled_out[0, :, lanes] = dscaled
        values = jnp.concatenate(
            [jnp.where(mask, scaled, zero), jnp.where(mask, zero, scaled)], axis=0
        )
        dmixing = dot(values, low, NT)
        dscores_t = dscores_t + dmixing[:length] * decays[0] + dmixing[length:] * decays[1]
        entered_k = (grad * spread(entry, k, mask)).astype(BF16)
        entered[:, lanes] = entered_k
        part, at = lo // half, lo % half
        carried = dot(readout, half_of(core, in_mine, in_other, part, slice(at, at + LANES)), NN)
        diagonal = ysum[0, :, lanes] - x * spread(head_rows[2:3], k, mask[0:1])
        terms[:, lanes] = (
            low.astype(F32) * diagonal
            - scaled.astype(F32) * dscaled
            + entered_k.astype(F32) * carried
        )
    joint_out[0, :, 2 * states :] = head_sums(terms[...], selector[...])
    dlow = dscores_t.astype(BF16)
    joint_out[0, :, :states] = dot(dlow, readout, NN)
    dread = dot(dlow, written, TN)
    for part in range(2):
        dread = dread + dot(
            entered[:, part * half : (part + 1) * half],
            half_of(core, in_mine, in_other, part, slice(None)),
            NT,
        )
    joint_out[0, :, states : 2 * states] = dread


def bwd_local(core, proj, halo, conv, dy, dscaled, joint, cum, marks, backs, heads, taps, selector, in_mine, in_other, out_mine, out_other, through, dproj_out, dhalo_out, dtaps_out, dhead_out, ext, dconv, ending, terms):
    length = proj.shape[1]
    channels = halo.shape[2]
    states = (joint.shape[2] - LANES) // 2
    inner = channels - 2 * states
    half = inner // 2
    head_rows = heads[...]
    heads_n = heads.shape[1]
    shifted, step, rate = steps_of(cum[0][:, heads_n:], head_rows)
    cums = cum[0][:, :heads_n]
    last = cums[length - 1 : length]
    end_decay = jnp.exp(last - cums) * marks[0, :, 4:5]
    end_weight = end_decay * step
    mask = pair_mask(length)
    written_v, written_s = silu_parts(conv[0, :, inner : inner + states])
    written = written_v.astype(BF16)
    ext[0:EDGE] = halo[0]
    ext[EDGE:] = proj[0, :, :channels]
    dconv[0:EDGE] = jnp.zeros((EDGE, channels), F32)
    dconv[EDGE + length :] = jnp.zeros((EDGE, channels), F32)
    products, skips = [], []
    for k in range(inner // LANES):
        lo = k * LANES
        lanes = slice(lo, lo + LANES)
        part, at = lo // half, lo % half
        pre = conv[0, :, lanes]
        x, sigmoid = silu_parts(pre)
        grad = dy[0, :, lanes]
        back = half_of(core, out_mine, out_other, part, slice(at, at + LANES))
        entering = half_of(core, in_mine, in_other, part, slice(at, at + LANES))
        products.append(
            jnp.sum(back.astype(F32) * entering.astype(F32), axis=0, keepdims=True)
        )
        ends = dot(written, back, NN)
        inside = dscaled[0, :, lanes] + spread(end_decay, k, mask) * ends
        weighted = (x * spread(end_weight, k, mask)).astype(BF16)
        ending[:, lanes] = weighted
        terms[0:length, lanes] = x * inside
        terms[length : 2 * length, lanes] = weighted.astype(F32) * ends
        skips.append(jnp.sum(grad * x, axis=0, keepdims=True))
        dx = spread(step, k, mask) * inside + spread(head_rows[2:3], k, mask[0:1]) * grad
        dconv[EDGE : EDGE + length, lanes] = dx * (sigmoid + x * (1.0 - sigmoid))
    dw = joint[0, :, :states]
    for part in range(2):
        dw = dw + dot(
            ending[:, part * half : (part + 1) * half],
            half_of(core, out_mine, out_other, part, slice(None)),
            NT,
        )
    dconv[EDGE : EDGE + length, inner : inner + states] = dw * (
        written_s + written_v * (1.0 - written_s)
    )
    read_v, read_s = silu_parts(conv[0, :, inner + states :])
    dconv[EDGE : EDGE + length, inner + states :] = joint[0, :, states : 2 * states] * (read_s + read_v * (1.0 - read_s))
    sums = head_sums(terms[...], selector[...])
    dstep = sums[:length, :heads_n]
    ended = sums[length:, :heads_n]
    lane_sums = jnp.concatenate(
        [jnp.concatenate(products, axis=1), jnp.concatenate(skips, axis=1), jnp.zeros((6, inner), F32)], axis=0
    )
    by_head = head_sums(lane_sums, selector[...])[:, :heads_n]
    kept = by_head[0:1]
    at_last = jnp.sum(ended, axis=0, keepdims=True) + kept * through[0]
    row = lax.broadcasted_iota(jnp.int32, (length, heads_n), 0)
    dcums = joint[0, :, 2 * states : 2 * states + heads_n] - ended + jnp.where(row == length - 1, at_last, 0.0)
    drate = dot(triangle(length, True), dcums, NN, EXACT)
    dstep = dstep - drate * jnp.exp(head_rows[1:2])
    draw = dstep * (1.0 / (1.0 + jnp.exp(-shifted)))
    dproj_out[0, :, channels:] = draw.astype(BF16)
    add_up(
        dhead_out,
        slice(None),
        slice(None),
        jnp.concatenate(
            [
                jnp.sum(draw, axis=0, keepdims=True),
                jnp.sum(drate * rate, axis=0, keepdims=True),
                by_head[1:2],
                jnp.zeros((5, heads_n), F32),
            ],
            axis=0,
        ),
    )
    rows = length + EDGE
    for lo in range(0, channels, LANES):
        lanes = slice(lo, lo + LANES)
        total = jnp.zeros((rows, LANES), F32)
        own = dconv[EDGE : EDGE + length, lanes]
        sums = []
        for s in range(4):
            total = total + dconv[s : s + rows, lanes] * (taps[3 - s : 4 - s, lanes] * backs[0, :, s : s + 1])
            sums.append(
                jnp.sum(own * ext[EDGE - s : EDGE - s + length, lanes] * marks[0, :, s : s + 1], axis=0, keepdims=True)
            )
        dproj_out[0, :, lanes] = total[EDGE:].astype(BF16)
        dhalo_out[0, 0:EDGE, lanes] = total[:EDGE]
        dhalo_out[0, EDGE:, lanes] = total[length:]
        sums = sums[::-1] + [jnp.sum(own, axis=0, keepdims=True), jnp.zeros((3, LANES), F32)]
        add_up(dtaps_out, slice(None), lanes, jnp.concatenate(sums, axis=0))


def per_sequence(kernel, inputs, outputs, scratch):
    sequences = None
    in_specs = [pl.BlockSpec(memory_space=pltpu.SMEM)]
    arrays = [(lax.axis_index("ctx") % 2).reshape(1)]
    for array, axis in inputs:
        if axis is not None:
            sequences = array.shape[axis]
        in_specs.append(block_spec(array.shape, axis))
        arrays.append(array)
    out_specs = [block_spec(shape, axis) for shape, _, axis in outputs]
    out_shape = [jax.ShapeDtypeStruct(shape, dtype) for shape, dtype, _ in outputs]
    return pl.pallas_call(
        kernel,
        grid=(sequences,),
        in_specs=in_specs,
        out_specs=out_specs,
        out_shape=out_shape,
        scratch_shapes=scratch,
        compiler_params=pltpu.CompilerParams(vmem_limit_bytes=VMEM_BYTES),
        cost_estimate=FREE,
    )(*arrays)


def block_spec(shape, axis):
    block = tuple(1 if d == axis else size for d, size in enumerate(shape))
    rank = len(shape)
    return pl.BlockSpec(
        block, functools.partial(block_index, rank, axis)
    )


def block_index(rank, axis, i):
    return tuple(i if d == axis else 0 for d in range(rank))


def rms_scale(values, gain_vector):
    return (
        values
        * lax.rsqrt(jnp.mean(values * values, axis=-1, keepdims=True) + EPSILON)
        * gain_vector
    )


def lanes_of(per_head, size):
    sequences, heads = per_head.shape
    spread_out = jnp.repeat(per_head, size, axis=1).reshape(sequences, 2, 1, heads * size // 2)
    return jnp.moveaxis(spread_out, 1, 0)


def layer_forward(hidden, ids, small, mix_weight, wave, later, head_params):
    norm_gain, taps, gate_gain = small
    sequences, length, width = hidden.shape
    channels = taps.shape[1]
    inner = gate_gain.shape[0]
    states = (channels - inner) // 2
    heads_n = head_params.shape[1]
    size = inner // heads_n
    gain = norm_gain.astype(F32)
    normed = rms_scale(hidden, gain).astype(BF16)
    proj = jnp.dot(normed, mix_weight, preferred_element_type=F32)
    edge = shift_along(proj[:, length - EDGE :, :channels], 1)
    conv, ysum, read, cum, mine, give = per_sequence(
        fwd_local,
        [(proj, 0), (edge, 0), (ids["marks"], 0), (ids["bias"], 0), (head_params, None), (taps, None)],
        [
            ((sequences, length, channels), F32, 0),
            ((sequences, length, inner), F32, 0),
            ((sequences, length, states), BF16, 0),
            ((sequences, length, 2 * heads_n), F32, 0),
            ((sequences, states, inner // 2), BF16, 0),
            ((sequences, states, inner // 2), BF16, 0),
        ],
        [pltpu.VMEM((length + EDGE, channels), F32), pltpu.VMEM((length, inner), BF16)],
    )
    through = jnp.exp(cum[:, -1, :heads_n]) * ids["carry"][:, None]
    through_lanes = lanes_of(through, size)
    packed, shapes = wave
    following_wave = None
    if later:
        following_wave = (gather_packed(after(later, mine)), [shard.shape for shard in later])
    arrived = lambda done, ready: unpack(after(packed, ready), shapes)[:2]
    used = lambda done, ready: [jnp.dot(normed, done[0][1], preferred_element_type=F32)] + unpack(
        after(packed, ready), shapes
    )[2:]
    incoming, made = chain(
        through_lanes, mine, give, True, [[arrived], [used]] if later else [[], [arrived, used]]
    )
    (out_weight, gate_weight), (gates, *following) = made
    weights = (norm_gain, mix_weight, gate_weight, taps, gate_gain, out_weight)
    mixed, y = per_sequence(
        fwd_mix,
        [(ysum, 0), (read, 0), (cum, 0), (ids["marks"], 0), (incoming[0], 0), (incoming[1], 0), (gates, 0), (gate_gain.astype(F32)[None], None)],
        [((sequences, length, inner), BF16, 0), ((sequences, length, inner), F32, 0)],
        [pltpu.VMEM((length, inner), F32)],
    )
    update = jnp.dot(mixed, out_weight, preferred_element_type=F32)
    saved = (hidden, gain, normed, proj, edge, gates, conv, ysum, read, cum, through, through_lanes, incoming, mixed, y)
    return hidden + update, weights, following, following_wave, saved


def layer_backward(gradient, ids, weights, head_params, saved, final, other_terms=None, other_small=None):
    hidden, gain, normed, proj, edge, gates, conv, ysum, read, cum, through, through_lanes, incoming, mixed, y = saved
    _, mix_weight, gate_weight, taps, gate_gain, out_weight = weights
    sequences, length, width = hidden.shape
    tokens = sequences * length
    channels = taps.shape[1]
    inner = gate_gain.shape[0]
    states = (channels - inner) // 2
    heads_n = head_params.shape[1]
    size = inner // heads_n
    update_low = gradient.astype(BF16)
    mixed_grad = lax.dot_general(
        update_low, out_weight, (((2,), (1,)), ((), ())), preferred_element_type=F32
    )
    dy, dgates, dgain, mine, give = per_sequence(
        bwd_gate,
        [(mixed_grad, 0), (y, 0), (gates, 0), (gate_gain.astype(F32)[None], None), (cum, 0), (ids["marks"], 0), (read, 0)],
        [
            ((sequences, length, inner), F32, 0),
            ((sequences, length, inner), BF16, 0),
            ((8, inner), F32, None),
            ((sequences, states, inner // 2), BF16, 0),
            ((sequences, states, inner // 2), BF16, 0),
        ],
        [pltpu.VMEM((length, inner), BF16)],
    )
    head_of = jnp.arange(inner) // size
    selector = (head_of[:, None] == jnp.arange(LANES)[None]).astype(BF16)

    def diagonal(done, ready):
        return per_sequence(
            bwd_diag,
            [(conv, 0), (ysum, 0), (after(dy, ready), 0), (read, 0), (cum, 0), (ids["marks"], 0),
             (ids["bias_t"], 0), (head_params, None), (selector, None), (incoming[0], 0), (incoming[1], 0)],
            [
                ((sequences, length, inner), F32, 0),
                ((sequences, length, 2 * states + LANES), F32, 0),
            ],
            [pltpu.VMEM((length, inner), F32), pltpu.VMEM((length, inner), BF16)],
        )

    flat = normed.reshape(tokens, width)
    flat_gates = dgates.reshape(tokens, inner)
    output_terms = (mixed.reshape(tokens, inner), update_low.reshape(tokens, width))
    order = bits_of(lax.axis_size("dp"))
    if final:
        other_product = packed_product(*after(other_terms, mine))
        outgoing, made = chain(
            through_lanes,
            mine,
            give,
            False,
            [
                [diagonal, lambda done, ready: pair_by_core(*after(output_terms + (flat, flat_gates), ready))],
                [lambda done, ready: over_cores(*done[1])],
            ],
        )
        (dscaled, joint), _, pair = made
        outgoing, pair = lax.optimization_barrier((outgoing, pair))
        own = inner // (2 * lax.axis_size("dp") * lax.axis_size("ctx") // 2)
        pair = [
            halve_over_rows(pair[:, :, :own], order[:1], order),
            halve_over_rows(pair[:, :, own:], order[-1:], order),
        ]
    else:
        outgoing, made = chain(through_lanes, mine, give, False, [[diagonal], []])
        dscaled, joint = made[0]
    dproj, dhalo, dtaps, dheads = per_sequence(
        bwd_local,
        [(proj, 0), (edge, 0), (conv, 0), (dy, 0), (dscaled, 0), (joint, 0), (cum, 0),
         (ids["marks"], 0), (ids["backs"], 0), (head_params, None), (taps, None), (selector, None),
         (incoming[0], 0), (incoming[1], 0), (outgoing[0], 0), (outgoing[1], 0), (through[:, None], 0)],
        [
            ((sequences, length, channels + heads_n), BF16, 0),
            ((sequences, 2 * EDGE, channels), F32, 0),
            ((8, channels), F32, None),
            ((8, heads_n), F32, None),
        ],
        [
            pltpu.VMEM((length + EDGE, channels), F32),
            pltpu.VMEM((length + 2 * EDGE, channels), F32),
            pltpu.VMEM((length, inner), BF16),
            pltpu.VMEM((2 * length, inner), F32),
        ],
    )
    if final:
        dproj, dhalo, pair = lax.optimization_barrier((dproj, dhalo, pair))
        pair = jnp.concatenate(
            [
                halve_over_rows(pair[0], order[1:], order[1:])[0],
                halve_over_rows(pair[1], order[:-1], order[:-1])[0],
            ],
            axis=1,
        )
    returned = shift_along(dhalo[:, :EDGE].astype(BF16), -1).astype(F32)
    tail = (dhalo[:, EDGE:] + returned).astype(BF16)
    dproj = lax.dynamic_update_slice(dproj, tail, (0, length - EDGE, 0))
    flat_grad = dproj.reshape(tokens, -1)
    if final:
        other_small = after(other_small, flat_grad)
        product = product_by_core(flat, flat_grad)
        dproj, product, pair = lax.optimization_barrier((dproj, product, pair))
        summed = over_cores(*product)
        cut = channels // 2 // LANES * LANES
        pair = scatter_over_chips(pair)
        first_parts = [
            halve_over_rows(summed[..., :cut], order[:1], order),
            halve_over_rows(summed[..., cut:], order[-1:], order),
        ]
    normed_grad = lax.dot_general(
        dproj, mix_weight, (((2,), (1,)), ((), ())), preferred_element_type=F32
    ) + lax.dot_general(dgates, gate_weight, (((2,), (1,)), ((), ())), preferred_element_type=F32)
    _, norm_pull = jax.vjp(rms_scale, hidden, gain)
    hidden_grad, norm_grad = norm_pull(normed_grad)
    small_terms = (norm_grad, dtaps, dgain, dheads)
    gradient = gradient + hidden_grad
    if not final:
        return gradient, small_terms, (flat, flat_gates, flat_grad) + output_terms
    chips = lax.axis_size("ctx") // 2
    core, chip = lax.axis_index("ctx") % 2, lax.axis_index("ctx") // 2
    devices = lax.axis_size("dp") * lax.axis_size("ctx")
    small = jnp.concatenate([by_device(devices, *small_terms), by_device(devices, *other_small)], axis=1)
    small = small.reshape(devices // 2, 2, -1)
    small = pick(small, core, 1) + swap_cores(pick(small, 1 - core, 1))
    first_parts, small = lax.optimization_barrier((first_parts, small))
    second_parts = [
        halve_over_rows(first_parts[0], order[1:], order[1:])[0],
        halve_over_rows(first_parts[1], order[:-1], order[:-1])[0],
    ]
    small = small.reshape(devices // 2 // chips, chips, -1)
    mine = lax.axis_index("dp")
    total = pick(small, mine)
    for distance in range(1, small.shape[0]):
        total = total + swap_rows(pick(small, mine ^ distance), distance)
    other_grads = scatter_packed(other_product, width // (inner // own), width)
    second_parts, total, other_grads = lax.optimization_barrier((second_parts, total, other_grads))
    last = scatter_over_chips(jnp.concatenate(second_parts, axis=-1))
    small = pick(total, chip)
    for distance in range(1, chips):
        small = small + swap_chips(pick(total, chip ^ distance), distance)
    small, pair, last = lax.optimization_barrier((small, pair, last))
    small = jnp.split(small, 2)
    output_grad = pair[:own]
    gates_grad = jnp.concatenate(jnp.split(pair[own:], inner // width, axis=0), axis=1)
    input_grad = jnp.concatenate([gates_grad, last], axis=1)
    return gradient, small, input_grad, output_grad, tuple(grad.astype(F32) for grad in other_grads)


def by_device(devices, norm_grad, dtaps, dgain, dheads):
    return jnp.concatenate(
        [
            norm_grad.reshape(devices, -1),
            dtaps[:5].reshape(5, devices, -1).swapaxes(0, 1).reshape(devices, -1),
            dgain[0].reshape(devices, -1),
            jnp.broadcast_to(dheads[:3].reshape(1, -1), (devices, 3 * dheads.shape[1])),
        ],
        axis=1,
    )


def unpack_small(total, shards, heads_n):
    norm, _, kernel, offset, gate, _ = shards
    sizes = (norm.size, kernel.size, offset.size, gate.size, heads_n, heads_n, heads_n)
    parts, start = [], 0
    for size in sizes:
        parts.append(total[start : start + size])
        start += size
    norm_grad, taps_grad, offset_grad, gain_grad, timestep, decay, skip = parts
    return norm_grad, taps_grad.reshape(kernel.shape), offset_grad, timestep, decay, skip, gain_grad


def gather_packed(shards):
    width = shards[0].shape[1]
    pieces = []
    for shard in shards:
        for start in range(0, shard.shape[1], width):
            piece = shard[:, start : start + width]
            pieces.append(jnp.pad(piece, ((0, 0), (0, width - piece.shape[1]))))
    packed = jnp.concatenate(pieces, axis=0)
    return lax.all_gather(packed, BOTH, axis=0, tiled=True).reshape((-1,) + packed.shape)


def unpack(packed, shapes):
    width = packed.shape[2]
    weights = []
    row = 0
    for rows, columns in shapes:
        parts = []
        for start in range(0, columns, width):
            part = packed[:, row : row + rows, : min(width, columns - start)]
            parts.append(part.reshape(-1, part.shape[2]))
            row += rows
        weights.append(parts[0] if len(parts) == 1 else jnp.concatenate(parts, axis=1))
    return weights


def small_rows(layers):
    rows = []
    for shards, _ in layers:
        norm, _, kernel, offset, gate, _ = shards
        rows += [norm, kernel.reshape(-1), offset, gate]
    return jnp.concatenate(rows)[None]


def small_weights(everyone, layers):
    parts, start = [], 0
    for shards, _ in layers:
        norm, _, kernel, offset, gate, _ = shards
        for row in (norm, kernel.reshape(-1), offset, gate):
            parts.append(everyone[:, start : start + row.shape[0]])
            start += row.shape[0]
    count = everyone.shape[0]
    result = []
    for layer in range(len(layers)):
        norm, kernel, offset, gate = parts[4 * layer : 4 * layer + 4]
        taps = layers[layer][0][2].shape[0]
        kernel = kernel.reshape(count, taps, -1).swapaxes(0, 1).reshape(taps, -1).astype(F32)
        offset = offset.reshape(1, -1).astype(F32)
        packed_taps = jnp.concatenate([kernel, offset, jnp.zeros((8 - taps - 1, kernel.shape[1]), F32)], axis=0)
        result.append((norm.reshape(-1), packed_taps, gate.reshape(-1)))
    return result


def segment_terms(segments):
    sequences, length = segments.shape
    ids = segments.astype(F32)
    before = shift_along(ids[:, length - EDGE :] + 1.0, 1) - 1.0
    joined = jnp.concatenate([before, ids], axis=1)
    after = jnp.concatenate([joined, jnp.full((sequences, EDGE), -2.0, F32)], axis=1)
    marks, backs = [], []
    for s in range(4):
        marks.append((joined[:, EDGE - s : EDGE - s + length] == ids).astype(F32))
        backs.append((after[:, s : s + length + EDGE] == joined).astype(F32))
    last = ids[:, -1:]
    prev = before[:, -1:]
    marks.append((ids == last).astype(F32))
    marks.append((ids == prev).astype(F32))
    marks += [jnp.zeros_like(ids)] * 2
    causal = jnp.tril(jnp.ones((length, length), jnp.bool_))
    allowed = causal[None] & (ids[:, :, None] == ids[:, None, :])
    allowed_t = causal.T[None] & (ids[:, :, None] == ids[:, None, :])
    return {
        "marks": jnp.stack(marks, axis=2),
        "backs": jnp.stack(backs + backs, axis=2),
        "bias": jnp.where(allowed, 0.0, FAR).astype(F32),
        "bias_t": jnp.where(allowed_t, 0.0, FAR).astype(F32),
        "carry": (last == prev).astype(F32)[:, 0],
    }


def on_device(
    tokens,
    segments,
    cotangent,
    first_norm,
    first_input,
    first_kernel,
    first_offset,
    first_timestep,
    first_decay,
    first_skip,
    first_gate,
    first_output,
    second_norm,
    second_input,
    second_kernel,
    second_offset,
    second_timestep,
    second_decay,
    second_skip,
    second_gate,
    second_output,
):
    layout = tokens.shape
    sequences = layout[0] * layout[1]
    hidden = tokens.astype(F32).reshape(sequences, layout[2], layout[3])
    ids = segment_terms(segments.reshape(sequences, layout[2]))
    layers = (
        (
            (first_norm, first_input, first_kernel, first_offset, first_gate, first_output),
            (first_timestep, first_decay, first_skip),
        ),
        (
            (second_norm, second_input, second_kernel, second_offset, second_gate, second_output),
            (second_timestep, second_decay, second_skip),
        ),
    )
    stored = []
    first, second = layers[0][0], layers[1][0]
    inner = first[4].shape[0] * lax.axis_size("dp") * lax.axis_size("ctx")
    mixer, everyone = gather_rows(first[1][:, inner:], small_rows(layers))
    smalls = small_weights(everyone, layers)
    shards = [first[5], first[1][:, :inner], second[1][:, inner:]]
    wave = (gather_packed(shards), [shard.shape for shard in shards])
    ids, mixer = lax.optimization_barrier((ids, mixer))
    later = [second[5], second[1][:, :inner]]
    for (_, head_params), small in zip(layers, smalls):
        heads = jnp.stack(list(head_params) + [jnp.zeros_like(head_params[0])] * 5)
        hidden, weights, following, wave, saved = layer_forward(hidden, ids, small, mixer, wave, later, heads)
        stored.append((weights, heads, saved))
        mixer, later = following[0] if following else None, []
    gradient = cotangent.astype(F32).reshape(hidden.shape)
    weights, heads, saved = stored[1]
    gradient, small, terms = layer_backward(gradient, ids, weights, heads, saved, False)
    weights, heads, saved = stored[0]
    gradient, smalls, input_grad, output_grad, other_grads = layer_backward(
        gradient, ids, weights, heads, saved, True, terms, small
    )
    results = []
    for total, (in_grad, out_grad) in (
        (smalls[0], (input_grad, output_grad)),
        (smalls[1], other_grads),
    ):
        parts = unpack_small(total, layers[0][0], heads.shape[1])
        results.append((parts[0], in_grad) + parts[1:] + (out_grad,))
    return (hidden.reshape(layout), gradient.reshape(layout)) + results[0] + results[1]


def solution(mesh):
    weight_specs = (P(BOTH), P(BOTH, None), P(None, BOTH), P(BOTH), P(), P(), P(), P(BOTH), P(BOTH, None))
    tokens_spec = P(None, "dp", "ctx", None)
    return jax.shard_map(
        on_device,
        mesh=mesh,
        in_specs=(tokens_spec, P(None, "dp", "ctx"), tokens_spec) + weight_specs + weight_specs,
        out_specs=(tokens_spec, tokens_spec) + weight_specs + weight_specs,
        check_vma=False,
    )
```

```python
import functools

import jax
import jax.numpy as jnp
from jax import lax
from jax.experimental import pallas as pl
from jax.experimental.pallas import tpu as pltpu
from jax.sharding import PartitionSpec as P

EPSILON = 1e-05
EXACT = lax.Precision.HIGHEST
BF16 = jnp.bfloat16
F32 = jnp.float32
BOTH = ("dp", "ctx")
FAR = -1e30
LANES = 128
EDGE = 8
VMEM_BYTES = 48 * 1024 * 1024
FREE = pl.CostEstimate(flops=0, bytes_accessed=0, transcendentals=0)


def shift_along(x, by):
    size = lax.axis_size("ctx")
    pairs = [(i, i + by) for i in range(size) if 0 <= i + by < size]
    return lax.ppermute(x, "ctx", pairs)


def swap_cores(x):
    return lax.ppermute(x, "ctx", [(i, i ^ 1) for i in range(lax.axis_size("ctx"))])


def swap_chips(x, distance):
    return lax.ppermute(
        x, "ctx", [(i, i ^ (2 * distance)) for i in range(lax.axis_size("ctx"))]
    )


def swap_rows(x, bit):
    return lax.ppermute(x, "dp", [(i, i ^ bit) for i in range(lax.axis_size("dp"))])


def pick(x, index, axis=0):
    return lax.dynamic_index_in_dim(x, index, axis=axis, keepdims=False)


def bits_of(count):
    return [1 << level for level in range((count - 1).bit_length())]


def in_order(mine, got, bit_is_set, axis):
    return jnp.concatenate(
        [jnp.where(bit_is_set, got, mine), jnp.where(bit_is_set, mine, got)], axis=axis
    )


def gather_over_chips(x):
    chips = lax.axis_size("ctx") // 2
    chip = lax.axis_index("ctx") // 2
    if chips <= 4:
        held = jnp.stack([x] + [swap_chips(x, distance) for distance in range(1, chips)])
        return jnp.stack([pick(held, chip ^ place) for place in range(chips)])
    x = x[None]
    for bit in bits_of(chips):
        x = in_order(x, swap_chips(x, bit), (chip // bit) % 2 == 1, 0)
    return x


def gather_rows(shard, aside):
    core = lax.axis_index("ctx") % 2
    order = bits_of(lax.axis_size("dp"))
    cut = shard.shape[1] // 2 // LANES * LANES
    x, aside = lax.optimization_barrier((gather_over_chips(shard), gather_over_chips(aside)))
    ways = [(x[..., :cut], order), (x[..., cut:], order[::-1]), (aside, order)]
    shapes = [part.shape for part, _ in ways]
    parts = [part.reshape((1,) * len(order) + part.shape) for part, _ in ways]
    for turn in range(len(order)):
        joined = []
        for part, (_, bits) in zip(parts, ways):
            bit = bits[turn]
            joined.append(
                in_order(
                    part,
                    swap_rows(part, bit),
                    (lax.axis_index("dp") // bit) % 2 == 1,
                    sorted(bits, reverse=True).index(bit),
                )
            )
        parts = lax.optimization_barrier(joined)
    left, right, aside = [part.reshape((-1,) + shape) for part, shape in zip(parts, shapes)]
    results = []
    for part in (jnp.concatenate([left, right], axis=-1), aside):
        whole = in_order(part[:, :, None], swap_cores(part)[:, :, None], core == 1, 2)
        results.append(whole.reshape((-1, part.shape[-1])))
    return results


def halve_over_rows(x, bits, left):
    me = lax.axis_index("dp")
    left = sorted(left, reverse=True)
    x = x.reshape((2,) * len(left) + x.shape[1:])
    for bit in bits:
        axis = left.index(bit)
        mine = (me // bit) % 2
        got = swap_rows(pick(x, 1 - mine, axis), bit)
        x = (pick(x, mine, axis).astype(F32) + got.astype(F32)).astype(BF16)
        left.remove(bit)
    return x.reshape((1 << len(left),) + x.shape[len(left) :])


def scatter_over_chips(x):
    chips = lax.axis_size("ctx") // 2
    chip = lax.axis_index("ctx") // 2
    if chips <= 4:
        total = pick(x, chip).astype(F32)
        for distance in range(1, chips):
            total = total + swap_chips(pick(x, chip ^ distance), distance).astype(F32)
        return total
    for bit in bits_of(chips)[::-1]:
        x = x.reshape((2, bit) + x.shape[1:])
        mine = (chip // bit) % 2
        got = swap_chips(pick(x, 1 - mine), bit)
        x = (pick(x, mine).astype(F32) + got.astype(F32)).astype(BF16)
    return x[0].astype(F32)


def split_cores(product, own):
    rows, columns = product.shape
    split = product.reshape(rows // own // 2, 2, own, columns)
    return split[:, 0], split[:, 1]


def store_by_core(core, product, own, rows, keep_out, give_out):
    first, second = split_cores(product, own)
    mine = core[0] == 0
    keep_out[:, rows : rows + own] = jnp.where(mine, first, second)
    give_out[:, rows : rows + own] = jnp.where(mine, second, first)


def product_halves(core, lhs, rhs, keep_out, give_out):
    product = dot(lhs[...], rhs[...], TN).astype(BF16)
    store_by_core(core, product, keep_out.shape[1], 0, keep_out, give_out)


def turns_of(groups):
    return 4 if groups % 4 == 0 else 1


def product_by_core(lhs, rhs, columns):
    dps = lax.axis_size("dp")
    chips = lax.axis_size("ctx") // 2
    core = lax.axis_index("ctx") % 2
    tokens, rows = lhs.shape
    groups = dps * chips
    own = rows // (groups * 2)
    shape = (dps, chips, own, columns)
    if own % 16:
        product = dot(lhs, rhs, TN).astype(BF16).reshape(dps, chips, 2, own, columns)
        return pick(product, core, 2), pick(product, 1 - core, 2)
    turns = turns_of(groups)
    out = jax.ShapeDtypeStruct((groups, own, columns), BF16)
    spec = pl.BlockSpec((groups // turns, own, columns), first_index_of_three)
    keep, give = pl.pallas_call(
        product_halves,
        grid=(turns,),
        in_specs=[
            pl.BlockSpec(memory_space=pltpu.SMEM),
            pl.BlockSpec((tokens, rows // turns), second_index_of_two),
            pl.BlockSpec((tokens, columns), no_index_of_two),
        ],
        out_specs=[spec, spec],
        out_shape=[out, out],
        compiler_params=pltpu.CompilerParams(vmem_limit_bytes=VMEM_BYTES),
        cost_estimate=FREE,
    )(core.reshape(1), lhs, rhs)
    return keep.reshape(shape), give.reshape(shape)


def packed_block(lhs, first, second, out_lhs, out_rhs, out):
    groups, height, columns = out.shape
    inner = first.shape[1]
    own = lhs.shape[1] // groups
    out[:, :own, :inner] = dot(lhs[...], first[...], TN).astype(BF16).reshape(groups, own, inner)
    out[:, :own, inner:] = dot(lhs[...], second[...], TN).astype(BF16).reshape(groups, own, columns - inner)
    product = dot(out_lhs[...], out_rhs[...], TN).astype(BF16)
    rest, width = height - own, product.shape[1]
    split = product.reshape(groups, -1, rest, width)
    for turn in range(split.shape[1]):
        out[:, own:, turn * width : (turn + 1) * width] = split[:, turn]
    out[:, own:, split.shape[1] * width :] = jnp.zeros((groups, rest, columns - split.shape[1] * width), BF16)


def packed_product(lhs, first, second, out_lhs, out_rhs):
    count = lax.axis_size("dp") * lax.axis_size("ctx")
    tokens, rows = lhs.shape
    inner, rest = first.shape[1], second.shape[1]
    columns = inner + rest
    own, out_own = rows // count, out_lhs.shape[1] // count
    width = out_rhs.shape[1]
    pieces = columns // width
    height = own + out_own // pieces
    turns = turns_of(count)
    if own % 16 or (out_own // pieces) % 16:
        product = jnp.concatenate([dot(lhs, first, TN), dot(lhs, second, TN)], axis=1).astype(BF16)
        other = dot(out_lhs, out_rhs, TN).astype(BF16).reshape(count, pieces, out_own // pieces, width)
        other = jnp.swapaxes(other, 1, 2).reshape(count, out_own // pieces, pieces * width)
        other = jnp.pad(other, ((0, 0), (0, 0), (0, columns - pieces * width)))
        return jnp.concatenate([product.reshape(count, own, columns), other], axis=1)
    return pl.pallas_call(
        packed_block,
        grid=(turns,),
        in_specs=[
            pl.BlockSpec((tokens, rows // turns), second_index_of_two),
            pl.BlockSpec((tokens, inner), no_index_of_two),
            pl.BlockSpec((tokens, rest), no_index_of_two),
            pl.BlockSpec((tokens, out_lhs.shape[1] // turns), second_index_of_two),
            pl.BlockSpec((tokens, width), no_index_of_two),
        ],
        out_specs=pl.BlockSpec((count // turns, height, columns), first_index_of_three),
        out_shape=jax.ShapeDtypeStruct((count, height, columns), BF16),
        compiler_params=pltpu.CompilerParams(vmem_limit_bytes=VMEM_BYTES),
        cost_estimate=FREE,
    )(lhs, first, second, out_lhs, out_rhs)


def scatter_packed(product, own, width):
    _, height, columns = product.shape
    total = lax.psum_scatter(product, BOTH, scatter_dimension=0, tiled=True).reshape(height, columns)
    pieces = columns // width
    return total[:own], jnp.concatenate([total[own:, i * width : (i + 1) * width] for i in range(pieces)], axis=0)


def first_index_of_three(i):
    return (i, 0, 0)


def second_index_of_two(i):
    return (0, i)


def no_index_of_two(i):
    return (0, 0)


def over_cores(keep, give):
    return (keep.astype(F32) + swap_cores(give).astype(F32)).astype(BF16)


def after(trees, ready):
    return lax.optimization_barrier((trees, ready))[0]


def exchange_chips(blocks):
    chips = blocks.shape[0]
    chip = lax.axis_index("ctx") // 2
    got = [pick(blocks, chip)]
    for distance in range(1, chips):
        got.append(swap_chips(pick(blocks, chip ^ distance), distance))
    return got


def by_sender(got):
    chip = lax.axis_index("ctx") // 2
    held = jnp.stack(got)
    return [pick(held, place ^ chip) for place in range(len(got))]


def carry_along(pair_t, pair_state, forward, work):
    count = lax.axis_size("ctx")
    chips = count // 2
    sequences, states, channels = pair_state.shape
    if chips > 4:

        def advance(_, carried):
            arrived = shift_along((carried * pair_t + pair_state).astype(BF16), 2 if forward else -2)
            return arrived.astype(F32)

        received = lax.fori_loop(0, chips - 1, advance, jnp.zeros_like(pair_state)).astype(BF16)
        done = []
        for items in work:
            for item in items:
                done.append(item(done, pair_state))
        return received, done
    share = channels // chips
    high = pair_t.astype(BF16)
    low = (pair_t - high.astype(F32)).astype(BF16)
    payload = jnp.concatenate(
        [pair_state.astype(BF16), high, low, jnp.zeros((sequences, 14, channels), BF16)], axis=1
    )
    blocks = jnp.moveaxis(payload.reshape(sequences, states + 16, chips, share), 2, 0)
    got = exchange_chips(blocks)
    done = []
    got, done = during(got, done, work[0], payload)
    carried = jnp.zeros((sequences, states, share), F32)
    entering = [None] * chips
    order = range(chips) if forward else range(chips - 1, -1, -1)
    held = by_sender(got)
    for place in order:
        entering[place] = carried.astype(BF16)
        decay = (held[place][:, states : states + 1].astype(F32) + held[place][:, states + 1 : states + 2].astype(F32))
        carried = carried * decay + held[place][:, :states].astype(F32)
    blocks = jnp.stack(entering)
    got = exchange_chips(blocks)
    got, done = during(got, done, work[1], blocks)
    return jnp.concatenate(by_sender(got), axis=-1), done


def during(got, done, items, ready):
    for item in items:
        made = item(done, ready)
        got, made = lax.optimization_barrier((got, made))
        done = done + [made]
    return got, done


def chain(through, mine, give, forward, work):
    core = lax.axis_index("ctx") % 2
    leading = core == (0 if forward else 1)
    other_t = swap_cores(through)
    sent = swap_cores(give).astype(F32)
    own_t, other_t = pick(through, core), pick(other_t, core)
    first_t = jnp.where(leading, own_t, other_t)
    second_t = jnp.where(leading, other_t, own_t)
    own = mine.astype(F32)
    first_state = jnp.where(leading, own, sent)
    pair_state = first_state * second_t + jnp.where(leading, sent, own)
    incoming, work = carry_along(first_t * second_t, pair_state, forward, work)
    second_in = (incoming.astype(F32) * first_t + first_state).astype(BF16)
    keep = jnp.where(leading, incoming, second_in)
    back = swap_cores(jnp.where(leading, second_in, incoming))
    return (keep, back), work


def silu_parts(v):
    gate = 0.5 + 0.5 * jnp.tanh(0.5 * v)
    return v * gate, gate


def pair_mask(rows):
    return lax.broadcasted_iota(jnp.int32, (rows, LANES), 1) < LANES // 2


def spread(per_head, k, mask):
    return jnp.where(mask, per_head[:, 2 * k : 2 * k + 1], per_head[:, 2 * k + 1 : 2 * k + 2])


def dot(a, b, contract, precision=None):
    return lax.dot_general(
        a, b, ((contract[0], contract[1]), ((), ())),
        preferred_element_type=F32, precision=precision,
    )


NN = ((1,), (0,))
NT = ((1,), (1,))
TN = ((0,), (0,))


def triangle(size, upper):
    row = lax.broadcasted_iota(jnp.int32, (size, size), 0)
    col = lax.broadcasted_iota(jnp.int32, (size, size), 1)
    keep = (col >= row) if upper else (col <= row)
    return jnp.where(keep, 1.0, 0.0).astype(F32)


def steps_of(raw, heads):
    shifted = raw + heads[0:1]
    step = jnp.maximum(shifted, 0.0) + jnp.log1p(jnp.exp(-jnp.abs(shifted)))
    rate = -step * jnp.exp(heads[1:2])
    return shifted, step, rate


def half_of(core, mine, other, part, lanes):
    return jnp.where(core[0] == part, mine[0, :, lanes], other[0, :, lanes])


def store_halves(core, values, mine_out, give_out):
    mine_out[0] = jnp.where(core[0] == 0, values[0], values[1])
    give_out[0] = jnp.where(core[0] == 0, values[1], values[0])


def add_up(out, rows, lanes, value):
    first = pl.program_id(0) == 0
    out[rows, lanes] = jnp.where(first, value, out[rows, lanes] + value)


def head_sums(values, selector):
    high = values.astype(BF16)
    low = (values - high.astype(F32)).astype(BF16)
    return dot(high, selector, NN) + dot(low, selector, NN)


def fwd_local(core, proj, halo, marks, bias, heads, taps, conv_out, ysum_out, read_out, cum_out, mine_out, give_out, ext, weighted):
    length = proj.shape[1]
    channels = halo.shape[2]
    states = read_out.shape[2]
    inner = channels - 2 * states
    head_rows = heads[...]
    raw = proj[0, :, channels:]
    _, step, rate = steps_of(raw, head_rows)
    cum = dot(triangle(length, False), rate, NN, EXACT)
    cum_t = dot(rate, triangle(length, False), ((0,), (1,)), EXACT)
    cum_out[0] = jnp.concatenate([cum, raw], axis=1)
    last = cum[length - 1 : length]
    end_weight = jnp.exp(last - cum) * marks[0, :, 4:5] * step
    ext[0:EDGE] = halo[0]
    ext[EDGE:] = proj[0, :, :channels]

    def activate(lo):
        lanes = slice(lo, lo + LANES)
        total = taps[4:5, lanes]
        for s in range(4):
            total = total + ext[EDGE - s : EDGE - s + length, lanes] * (
                taps[3 - s : 4 - s, lanes] * marks[0, :, s : s + 1]
            )
        conv_out[0, :, lanes] = total
        return silu_parts(total)[0]

    written = activate(inner).astype(BF16)
    readout = activate(inner + states).astype(BF16)
    read_out[0] = readout
    scores = dot(readout, written, NT)
    mask = pair_mask(length)
    blocked = bias[0]
    zero = jnp.zeros((length, LANES), BF16)
    for k in range(inner // LANES):
        lo = k * LANES
        x = activate(lo)
        scaled = (x * spread(step, k, mask)).astype(BF16)
        weighted[:, lo : lo + LANES] = (x * spread(end_weight, k, mask)).astype(BF16)
        mixing = []
        for h in (2 * k, 2 * k + 1):
            gap = cum[:, h : h + 1] - cum_t[h : h + 1, :]
            mixing.append((jnp.exp(gap + blocked) * scores).astype(BF16))
        values = jnp.concatenate(
            [jnp.where(mask, scaled, zero), jnp.where(mask, zero, scaled)], axis=0
        )
        result = dot(jnp.concatenate(mixing, axis=1), values, NN)
        ysum_out[0, :, lo : lo + LANES] = result + x * spread(head_rows[2:3], k, mask[0:1])
    half = inner // 2
    store_halves(
        core,
        [dot(written, weighted[:, part * half : (part + 1) * half], TN).astype(BF16) for part in range(2)],
        mine_out,
        give_out,
    )


def fwd_mix(core, ysum, read, cum, marks, in_mine, in_other, gates, gain, mixed_out, y_out, gated):
    length = ysum.shape[1]
    inner = ysum.shape[2]
    half = inner // 2
    entry = jnp.exp(cum[0][:, : cum.shape[2] // 2]) * marks[0, :, 5:6]
    mask = pair_mask(length)
    squares = jnp.zeros((length, LANES), F32)
    for k in range(inner // LANES):
        lo = k * LANES
        part, at = lo // half, lo % half
        carried = dot(read[0], half_of(core, in_mine, in_other, part, slice(at, at + LANES)), NN)
        y = ysum[0, :, lo : lo + LANES] + spread(entry, k, mask) * carried
        y_out[0, :, lo : lo + LANES] = y
        value = y * silu_parts(gates[0, :, lo : lo + LANES])[0]
        gated[:, lo : lo + LANES] = value
        squares = squares + value * value
    scale = lax.rsqrt(jnp.sum(squares, axis=1, keepdims=True) * (1.0 / inner) + EPSILON)
    for k in range(inner // LANES):
        lanes = slice(k * LANES, (k + 1) * LANES)
        mixed_out[0, :, lanes] = (gated[:, lanes] * scale * gain[:, lanes]).astype(BF16)


def bwd_gate(core, grad, y, gates, gain, cum, marks, read, dy_out, dgate_out, dgain_out, mine_out, give_out, weighted):
    length = y.shape[1]
    inner = y.shape[2]
    entry = jnp.exp(cum[0][:, : cum.shape[2] // 2]) * marks[0, :, 5:6]
    mask = pair_mask(length)
    squares = jnp.zeros((length, LANES), F32)
    cross = jnp.zeros((length, LANES), F32)
    for k in range(inner // LANES):
        lanes = slice(k * LANES, (k + 1) * LANES)
        value = y[0, :, lanes] * silu_parts(gates[0, :, lanes])[0]
        squares = squares + value * value
        cross = cross + value * grad[0, :, lanes] * gain[:, lanes]
    scale = lax.rsqrt(jnp.sum(squares, axis=1, keepdims=True) * (1.0 / inner) + EPSILON)
    inward = jnp.sum(cross, axis=1, keepdims=True) * (scale * scale * scale * (1.0 / inner))
    for k in range(inner // LANES):
        lanes = slice(k * LANES, (k + 1) * LANES)
        z = gates[0, :, lanes]
        active, sigmoid = silu_parts(z)
        yk = y[0, :, lanes]
        value = yk * active
        g = grad[0, :, lanes]
        add_up(dgain_out, slice(0, 1), lanes, jnp.sum(g * value * scale, axis=0, keepdims=True))
        dvalue = g * gain[:, lanes] * scale - value * inward
        dy = dvalue * active
        dy_out[0, :, lanes] = dy
        dgate_out[0, :, lanes] = (dvalue * yk * (sigmoid + active * (1.0 - sigmoid))).astype(BF16)
        weighted[:, lanes] = (dy * spread(entry, k, mask)).astype(BF16)
    half = inner // 2
    store_halves(
        core,
        [dot(read[0], weighted[:, part * half : (part + 1) * half], TN).astype(BF16) for part in range(2)],
        mine_out,
        give_out,
    )


def bwd_diag(core, conv, ysum, dy, read, cum, marks, bias_t, heads, selector, in_mine, in_other, dscaled_out, joint_out, terms, entered):
    length = ysum.shape[1]
    inner = ysum.shape[2]
    half = inner // 2
    states = read.shape[2]
    head_rows = heads[...]
    heads_n = heads.shape[1]
    _, step, rate = steps_of(cum[0][:, heads_n:], head_rows)
    cums = cum[0][:, :heads_n]
    cum_t = dot(rate, triangle(length, False), ((0,), (1,)), EXACT)
    entry = jnp.exp(cums) * marks[0, :, 5:6]
    written = silu_parts(conv[0, :, inner : inner + states])[0].astype(BF16)
    readout = read[0]
    scores_t = dot(written, readout, NT)
    mask = pair_mask(length)
    blocked = bias_t[0]
    zero = jnp.zeros((length, LANES), BF16)
    dscores_t = jnp.zeros((length, length), F32)
    for k in range(inner // LANES):
        lo = k * LANES
        lanes = slice(lo, lo + LANES)
        x = silu_parts(conv[0, :, lanes])[0]
        scaled = (x * spread(step, k, mask)).astype(BF16)
        grad = dy[0, :, lanes]
        low = grad.astype(BF16)
        decays, mixing = [], []
        for h in (2 * k, 2 * k + 1):
            gap = cum_t[h : h + 1, :] - cums[:, h : h + 1]
            decay = jnp.exp(gap + blocked)
            decays.append(decay)
            mixing.append((decay * scores_t).astype(BF16))
        grads = jnp.concatenate([jnp.where(mask, low, zero), jnp.where(mask, zero, low)], axis=0)
        dscaled = dot(jnp.concatenate(mixing, axis=1), grads, NN)
        dscaled_out[0, :, lanes] = dscaled
        values = jnp.concatenate(
            [jnp.where(mask, scaled, zero), jnp.where(mask, zero, scaled)], axis=0
        )
        dmixing = dot(values, low, NT)
        dscores_t = dscores_t + dmixing[:length] * decays[0] + dmixing[length:] * decays[1]
        entered_k = (grad * spread(entry, k, mask)).astype(BF16)
        entered[:, lanes] = entered_k
        part, at = lo // half, lo % half
        carried = dot(readout, half_of(core, in_mine, in_other, part, slice(at, at + LANES)), NN)
        diagonal = ysum[0, :, lanes] - x * spread(head_rows[2:3], k, mask[0:1])
        terms[:, lanes] = (
            low.astype(F32) * diagonal
            - scaled.astype(F32) * dscaled
            + entered_k.astype(F32) * carried
        )
    joint_out[0, :, 2 * states :] = head_sums(terms[...], selector[...])
    dlow = dscores_t.astype(BF16)
    joint_out[0, :, :states] = dot(dlow, readout, NN)
    dread = dot(dlow, written, TN)
    for part in range(2):
        dread = dread + dot(
            entered[:, part * half : (part + 1) * half],
            half_of(core, in_mine, in_other, part, slice(None)),
            NT,
        )
    joint_out[0, :, states : 2 * states] = dread


def bwd_local(core, proj, halo, conv, dy, dscaled, joint, cum, marks, backs, heads, taps, selector, in_mine, in_other, out_mine, out_other, through, dproj_out, dhalo_out, dtaps_out, dhead_out, ext, dconv, ending, terms):
    length = proj.shape[1]
    channels = halo.shape[2]
    states = (joint.shape[2] - LANES) // 2
    inner = channels - 2 * states
    half = inner // 2
    head_rows = heads[...]
    heads_n = heads.shape[1]
    shifted, step, rate = steps_of(cum[0][:, heads_n:], head_rows)
    cums = cum[0][:, :heads_n]
    last = cums[length - 1 : length]
    end_decay = jnp.exp(last - cums) * marks[0, :, 4:5]
    end_weight = end_decay * step
    mask = pair_mask(length)
    written_v, written_s = silu_parts(conv[0, :, inner : inner + states])
    written = written_v.astype(BF16)
    ext[0:EDGE] = halo[0]
    ext[EDGE:] = proj[0, :, :channels]
    dconv[0:EDGE] = jnp.zeros((EDGE, channels), F32)
    dconv[EDGE + length :] = jnp.zeros((EDGE, channels), F32)
    products, skips = [], []
    for k in range(inner // LANES):
        lo = k * LANES
        lanes = slice(lo, lo + LANES)
        part, at = lo // half, lo % half
        pre = conv[0, :, lanes]
        x, sigmoid = silu_parts(pre)
        grad = dy[0, :, lanes]
        back = half_of(core, out_mine, out_other, part, slice(at, at + LANES))
        entering = half_of(core, in_mine, in_other, part, slice(at, at + LANES))
        products.append(
            jnp.sum(back.astype(F32) * entering.astype(F32), axis=0, keepdims=True)
        )
        ends = dot(written, back, NN)
        inside = dscaled[0, :, lanes] + spread(end_decay, k, mask) * ends
        weighted = (x * spread(end_weight, k, mask)).astype(BF16)
        ending[:, lanes] = weighted
        terms[0:length, lanes] = x * inside
        terms[length : 2 * length, lanes] = weighted.astype(F32) * ends
        skips.append(jnp.sum(grad * x, axis=0, keepdims=True))
        dx = spread(step, k, mask) * inside + spread(head_rows[2:3], k, mask[0:1]) * grad
        dconv[EDGE : EDGE + length, lanes] = dx * (sigmoid + x * (1.0 - sigmoid))
    dw = joint[0, :, :states]
    for part in range(2):
        dw = dw + dot(
            ending[:, part * half : (part + 1) * half],
            half_of(core, out_mine, out_other, part, slice(None)),
            NT,
        )
    dconv[EDGE : EDGE + length, inner : inner + states] = dw * (
        written_s + written_v * (1.0 - written_s)
    )
    read_v, read_s = silu_parts(conv[0, :, inner + states :])
    dconv[EDGE : EDGE + length, inner + states :] = joint[0, :, states : 2 * states] * (read_s + read_v * (1.0 - read_s))
    sums = head_sums(terms[...], selector[...])
    dstep = sums[:length, :heads_n]
    ended = sums[length:, :heads_n]
    lane_sums = jnp.concatenate(
        [jnp.concatenate(products, axis=1), jnp.concatenate(skips, axis=1), jnp.zeros((6, inner), F32)], axis=0
    )
    by_head = head_sums(lane_sums, selector[...])[:, :heads_n]
    kept = by_head[0:1]
    at_last = jnp.sum(ended, axis=0, keepdims=True) + kept * through[0]
    row = lax.broadcasted_iota(jnp.int32, (length, heads_n), 0)
    dcums = joint[0, :, 2 * states : 2 * states + heads_n] - ended + jnp.where(row == length - 1, at_last, 0.0)
    drate = dot(triangle(length, True), dcums, NN, EXACT)
    dstep = dstep - drate * jnp.exp(head_rows[1:2])
    draw = dstep * (1.0 / (1.0 + jnp.exp(-shifted)))
    dproj_out[0, :, channels:] = draw.astype(BF16)
    add_up(
        dhead_out,
        slice(None),
        slice(None),
        jnp.concatenate(
            [
                jnp.sum(draw, axis=0, keepdims=True),
                jnp.sum(drate * rate, axis=0, keepdims=True),
                by_head[1:2],
                jnp.zeros((5, heads_n), F32),
            ],
            axis=0,
        ),
    )
    rows = length + EDGE
    for lo in range(0, channels, LANES):
        lanes = slice(lo, lo + LANES)
        total = jnp.zeros((rows, LANES), F32)
        own = dconv[EDGE : EDGE + length, lanes]
        sums = []
        for s in range(4):
            total = total + dconv[s : s + rows, lanes] * (taps[3 - s : 4 - s, lanes] * backs[0, :, s : s + 1])
            sums.append(
                jnp.sum(own * ext[EDGE - s : EDGE - s + length, lanes] * marks[0, :, s : s + 1], axis=0, keepdims=True)
            )
        dproj_out[0, :, lanes] = total[EDGE:].astype(BF16)
        dhalo_out[0, 0:EDGE, lanes] = total[:EDGE]
        dhalo_out[0, EDGE:, lanes] = total[length:]
        sums = sums[::-1] + [jnp.sum(own, axis=0, keepdims=True), jnp.zeros((3, LANES), F32)]
        add_up(dtaps_out, slice(None), lanes, jnp.concatenate(sums, axis=0))


def per_sequence(kernel, inputs, outputs, scratch):
    sequences = None
    in_specs = [pl.BlockSpec(memory_space=pltpu.SMEM)]
    arrays = [(lax.axis_index("ctx") % 2).reshape(1)]
    for array, axis in inputs:
        if axis is not None:
            sequences = array.shape[axis]
        in_specs.append(block_spec(array.shape, axis))
        arrays.append(array)
    out_specs = [block_spec(shape, axis) for shape, _, axis in outputs]
    out_shape = [jax.ShapeDtypeStruct(shape, dtype) for shape, dtype, _ in outputs]
    return pl.pallas_call(
        kernel,
        grid=(sequences,),
        in_specs=in_specs,
        out_specs=out_specs,
        out_shape=out_shape,
        scratch_shapes=scratch,
        compiler_params=pltpu.CompilerParams(vmem_limit_bytes=VMEM_BYTES),
        cost_estimate=FREE,
    )(*arrays)


def block_spec(shape, axis):
    block = tuple(1 if d == axis else size for d, size in enumerate(shape))
    rank = len(shape)
    return pl.BlockSpec(
        block, functools.partial(block_index, rank, axis)
    )


def block_index(rank, axis, i):
    return tuple(i if d == axis else 0 for d in range(rank))


def rms_scale(values, gain_vector):
    return (
        values
        * lax.rsqrt(jnp.mean(values * values, axis=-1, keepdims=True) + EPSILON)
        * gain_vector
    )


def lanes_of(per_head, size):
    sequences, heads = per_head.shape
    spread_out = jnp.repeat(per_head, size, axis=1).reshape(sequences, 2, 1, heads * size // 2)
    return jnp.moveaxis(spread_out, 1, 0)


def layer_forward(hidden, ids, small, mix_weight, wave, later, head_params):
    norm_gain, taps, gate_gain = small
    sequences, length, width = hidden.shape
    channels = taps.shape[1]
    inner = gate_gain.shape[0]
    states = (channels - inner) // 2
    heads_n = head_params.shape[1]
    size = inner // heads_n
    gain = norm_gain.astype(F32)
    normed = rms_scale(hidden, gain).astype(BF16)
    proj = jnp.dot(normed, mix_weight, preferred_element_type=F32)
    edge = shift_along(proj[:, length - EDGE :, :channels], 1)
    conv, ysum, read, cum, mine, give = per_sequence(
        fwd_local,
        [(proj, 0), (edge, 0), (ids["marks"], 0), (ids["bias"], 0), (head_params, None), (taps, None)],
        [
            ((sequences, length, channels), F32, 0),
            ((sequences, length, inner), F32, 0),
            ((sequences, length, states), BF16, 0),
            ((sequences, length, 2 * heads_n), F32, 0),
            ((sequences, states, inner // 2), BF16, 0),
            ((sequences, states, inner // 2), BF16, 0),
        ],
        [pltpu.VMEM((length + EDGE, channels), F32), pltpu.VMEM((length, inner), BF16)],
    )
    through = jnp.exp(cum[:, -1, :heads_n]) * ids["carry"][:, None]
    through_lanes = lanes_of(through, size)
    packed, shapes = wave
    following_wave = None
    if later:
        following_wave = (gather_packed(after(later, mine)), [shard.shape for shard in later])
    arrived = lambda done, ready: unpack(after(packed, ready), shapes)[:2]
    used = lambda done, ready: [jnp.dot(normed, done[0][1], preferred_element_type=F32)] + unpack(
        after(packed, ready), shapes
    )[2:]
    incoming, made = chain(
        through_lanes, mine, give, True, [[arrived], [used]] if later else [[], [arrived, used]]
    )
    (out_weight, gate_weight), (gates, *following) = made
    weights = (norm_gain, mix_weight, gate_weight, taps, gate_gain, out_weight)
    mixed, y = per_sequence(
        fwd_mix,
        [(ysum, 0), (read, 0), (cum, 0), (ids["marks"], 0), (incoming[0], 0), (incoming[1], 0), (gates, 0), (gate_gain.astype(F32)[None], None)],
        [((sequences, length, inner), BF16, 0), ((sequences, length, inner), F32, 0)],
        [pltpu.VMEM((length, inner), F32)],
    )
    update = jnp.dot(mixed, out_weight, preferred_element_type=F32)
    saved = (hidden, gain, normed, proj, edge, gates, conv, ysum, read, cum, through, through_lanes, incoming, mixed, y)
    return hidden + update, weights, following, following_wave, saved


def layer_backward(gradient, ids, weights, head_params, saved, final, other_terms=None, other_small=None):
    hidden, gain, normed, proj, edge, gates, conv, ysum, read, cum, through, through_lanes, incoming, mixed, y = saved
    _, mix_weight, gate_weight, taps, gate_gain, out_weight = weights
    sequences, length, width = hidden.shape
    tokens = sequences * length
    channels = taps.shape[1]
    inner = gate_gain.shape[0]
    states = (channels - inner) // 2
    heads_n = head_params.shape[1]
    size = inner // heads_n
    update_low = gradient.astype(BF16)
    mixed_grad = lax.dot_general(
        update_low, out_weight, (((2,), (1,)), ((), ())), preferred_element_type=F32
    )
    dy, dgates, dgain, mine, give = per_sequence(
        bwd_gate,
        [(mixed_grad, 0), (y, 0), (gates, 0), (gate_gain.astype(F32)[None], None), (cum, 0), (ids["marks"], 0), (read, 0)],
        [
            ((sequences, length, inner), F32, 0),
            ((sequences, length, inner), BF16, 0),
            ((8, inner), F32, None),
            ((sequences, states, inner // 2), BF16, 0),
            ((sequences, states, inner // 2), BF16, 0),
        ],
        [pltpu.VMEM((length, inner), BF16)],
    )
    head_of = jnp.arange(inner) // size
    selector = (head_of[:, None] == jnp.arange(LANES)[None]).astype(BF16)

    def diagonal(done, ready):
        return per_sequence(
            bwd_diag,
            [(conv, 0), (ysum, 0), (after(dy, ready), 0), (read, 0), (cum, 0), (ids["marks"], 0),
             (ids["bias_t"], 0), (head_params, None), (selector, None), (incoming[0], 0), (incoming[1], 0)],
            [
                ((sequences, length, inner), F32, 0),
                ((sequences, length, 2 * states + LANES), F32, 0),
            ],
            [pltpu.VMEM((length, inner), F32), pltpu.VMEM((length, inner), BF16)],
        )

    flat = normed.reshape(tokens, width)
    flat_gates = dgates.reshape(tokens, inner)
    output_terms = (mixed.reshape(tokens, inner), update_low.reshape(tokens, width))
    order = bits_of(lax.axis_size("dp"))
    if final:
        other_product = packed_product(*after(other_terms, mine))
        outgoing, made = chain(
            through_lanes,
            mine,
            give,
            False,
            [
                [
                    diagonal,
                    lambda done, ready: [
                        product_by_core(*after(output_terms, ready), width),
                        product_by_core(*after((flat, flat_gates), ready), inner),
                    ],
                ],
                [lambda done, ready: [over_cores(*product) for product in done[1]]],
            ],
        )
        (dscaled, joint), _, pair = made
        outgoing, pair = lax.optimization_barrier((outgoing, pair))
        own = inner // (2 * lax.axis_size("dp") * lax.axis_size("ctx") // 2)
        pair = [halve_over_rows(pair[0], order[:1], order), halve_over_rows(pair[1], order[-1:], order)]
    else:
        outgoing, made = chain(through_lanes, mine, give, False, [[diagonal], []])
        dscaled, joint = made[0]
    dproj, dhalo, dtaps, dheads = per_sequence(
        bwd_local,
        [(proj, 0), (edge, 0), (conv, 0), (dy, 0), (dscaled, 0), (joint, 0), (cum, 0),
         (ids["marks"], 0), (ids["backs"], 0), (head_params, None), (taps, None), (selector, None),
         (incoming[0], 0), (incoming[1], 0), (outgoing[0], 0), (outgoing[1], 0), (through[:, None], 0)],
        [
            ((sequences, length, channels + heads_n), BF16, 0),
            ((sequences, 2 * EDGE, channels), F32, 0),
            ((8, channels), F32, None),
            ((8, heads_n), F32, None),
        ],
        [
            pltpu.VMEM((length + EDGE, channels), F32),
            pltpu.VMEM((length + 2 * EDGE, channels), F32),
            pltpu.VMEM((length, inner), BF16),
            pltpu.VMEM((2 * length, inner), F32),
        ],
    )
    if final:
        dproj, dhalo, pair = lax.optimization_barrier((dproj, dhalo, pair))
        pair = [
            halve_over_rows(pair[0], order[1:], order[1:])[0],
            halve_over_rows(pair[1], order[:-1], order[:-1])[0],
        ]
        pair = jnp.concatenate([pair[0]] + jnp.split(pair[1], inner // width, axis=2), axis=1)
    returned = shift_along(dhalo[:, :EDGE].astype(BF16), -1).astype(F32)
    tail = (dhalo[:, EDGE:] + returned).astype(BF16)
    dproj = lax.dynamic_update_slice(dproj, tail, (0, length - EDGE, 0))
    flat_grad = dproj.reshape(tokens, -1)
    if final:
        other_small = after(other_small, flat_grad)
        product = product_by_core(flat, flat_grad, flat_grad.shape[1])
        dproj, product, pair = lax.optimization_barrier((dproj, product, pair))
        summed = over_cores(*product)
        cut = channels // 2 // LANES * LANES
        pair = scatter_over_chips(pair)
        first_parts = [
            halve_over_rows(summed[..., :cut], order[:1], order),
            halve_over_rows(summed[..., cut:], order[-1:], order),
        ]
    normed_grad = lax.dot_general(
        dproj, mix_weight, (((2,), (1,)), ((), ())), preferred_element_type=F32
    ) + lax.dot_general(dgates, gate_weight, (((2,), (1,)), ((), ())), preferred_element_type=F32)
    _, norm_pull = jax.vjp(rms_scale, hidden, gain)
    hidden_grad, norm_grad = norm_pull(normed_grad)
    small_terms = (norm_grad, dtaps, dgain, dheads)
    gradient = gradient + hidden_grad
    if not final:
        return gradient, small_terms, (flat, flat_gates, flat_grad) + output_terms
    chips = lax.axis_size("ctx") // 2
    core, chip = lax.axis_index("ctx") % 2, lax.axis_index("ctx") // 2
    devices = lax.axis_size("dp") * lax.axis_size("ctx")
    small = jnp.concatenate([by_device(devices, *small_terms), by_device(devices, *other_small)], axis=1)
    small = small.reshape(devices // 2, 2, -1)
    small = pick(small, core, 1) + swap_cores(pick(small, 1 - core, 1))
    first_parts, small = lax.optimization_barrier((first_parts, small))
    second_parts = [
        halve_over_rows(first_parts[0], order[1:], order[1:])[0],
        halve_over_rows(first_parts[1], order[:-1], order[:-1])[0],
    ]
    small = small.reshape(devices // 2 // chips, chips, -1)
    mine = lax.axis_index("dp")
    total = pick(small, mine)
    for distance in range(1, small.shape[0]):
        total = total + swap_rows(pick(small, mine ^ distance), distance)
    other_grads = scatter_packed(other_product, width // (inner // own), width)
    second_parts, total = lax.optimization_barrier((second_parts, total))
    last = scatter_over_chips(jnp.concatenate(second_parts, axis=-1))
    small = pick(total, chip)
    for distance in range(1, chips):
        small = small + swap_chips(pick(total, chip ^ distance), distance)
    small, pair, last, other_grads = lax.optimization_barrier((small, pair, last, other_grads))
    small = jnp.split(small, 2)
    output_grad = pair[:own]
    gates_grad = jnp.concatenate(jnp.split(pair[own:], inner // width, axis=0), axis=1)
    input_grad = jnp.concatenate([gates_grad, last], axis=1)
    return gradient, small, input_grad, output_grad, tuple(grad.astype(F32) for grad in other_grads)


def by_device(devices, norm_grad, dtaps, dgain, dheads):
    return jnp.concatenate(
        [
            norm_grad.reshape(devices, -1),
            dtaps[:5].reshape(5, devices, -1).swapaxes(0, 1).reshape(devices, -1),
            dgain[0].reshape(devices, -1),
            jnp.broadcast_to(dheads[:3].reshape(1, -1), (devices, 3 * dheads.shape[1])),
        ],
        axis=1,
    )


def unpack_small(total, shards, heads_n):
    norm, _, kernel, offset, gate, _ = shards
    sizes = (norm.size, kernel.size, offset.size, gate.size, heads_n, heads_n, heads_n)
    parts, start = [], 0
    for size in sizes:
        parts.append(total[start : start + size])
        start += size
    norm_grad, taps_grad, offset_grad, gain_grad, timestep, decay, skip = parts
    return norm_grad, taps_grad.reshape(kernel.shape), offset_grad, timestep, decay, skip, gain_grad


def gather_packed(shards):
    width = shards[0].shape[1]
    pieces = []
    for shard in shards:
        for start in range(0, shard.shape[1], width):
            piece = shard[:, start : start + width]
            pieces.append(jnp.pad(piece, ((0, 0), (0, width - piece.shape[1]))))
    packed = jnp.concatenate(pieces, axis=0)
    return lax.all_gather(packed, BOTH, axis=0, tiled=True).reshape((-1,) + packed.shape)


def unpack(packed, shapes):
    width = packed.shape[2]
    weights = []
    row = 0
    for rows, columns in shapes:
        parts = []
        for start in range(0, columns, width):
            part = packed[:, row : row + rows, : min(width, columns - start)]
            parts.append(part.reshape(-1, part.shape[2]))
            row += rows
        weights.append(parts[0] if len(parts) == 1 else jnp.concatenate(parts, axis=1))
    return weights


def small_rows(layers):
    rows = []
    for shards, _ in layers:
        norm, _, kernel, offset, gate, _ = shards
        rows += [norm, kernel.reshape(-1), offset, gate]
    return jnp.concatenate(rows)[None]


def small_weights(everyone, layers):
    parts, start = [], 0
    for shards, _ in layers:
        norm, _, kernel, offset, gate, _ = shards
        for row in (norm, kernel.reshape(-1), offset, gate):
            parts.append(everyone[:, start : start + row.shape[0]])
            start += row.shape[0]
    count = everyone.shape[0]
    result = []
    for layer in range(len(layers)):
        norm, kernel, offset, gate = parts[4 * layer : 4 * layer + 4]
        taps = layers[layer][0][2].shape[0]
        kernel = kernel.reshape(count, taps, -1).swapaxes(0, 1).reshape(taps, -1).astype(F32)
        offset = offset.reshape(1, -1).astype(F32)
        packed_taps = jnp.concatenate([kernel, offset, jnp.zeros((8 - taps - 1, kernel.shape[1]), F32)], axis=0)
        result.append((norm.reshape(-1), packed_taps, gate.reshape(-1)))
    return result


def segment_terms(segments):
    sequences, length = segments.shape
    ids = segments.astype(F32)
    before = shift_along(ids[:, length - EDGE :] + 1.0, 1) - 1.0
    joined = jnp.concatenate([before, ids], axis=1)
    after = jnp.concatenate([joined, jnp.full((sequences, EDGE), -2.0, F32)], axis=1)
    marks, backs = [], []
    for s in range(4):
        marks.append((joined[:, EDGE - s : EDGE - s + length] == ids).astype(F32))
        backs.append((after[:, s : s + length + EDGE] == joined).astype(F32))
    last = ids[:, -1:]
    prev = before[:, -1:]
    marks.append((ids == last).astype(F32))
    marks.append((ids == prev).astype(F32))
    marks += [jnp.zeros_like(ids)] * 2
    causal = jnp.tril(jnp.ones((length, length), jnp.bool_))
    allowed = causal[None] & (ids[:, :, None] == ids[:, None, :])
    allowed_t = causal.T[None] & (ids[:, :, None] == ids[:, None, :])
    return {
        "marks": jnp.stack(marks, axis=2),
        "backs": jnp.stack(backs + backs, axis=2),
        "bias": jnp.where(allowed, 0.0, FAR).astype(F32),
        "bias_t": jnp.where(allowed_t, 0.0, FAR).astype(F32),
        "carry": (last == prev).astype(F32)[:, 0],
    }


def on_device(
    tokens,
    segments,
    cotangent,
    first_norm,
    first_input,
    first_kernel,
    first_offset,
    first_timestep,
    first_decay,
    first_skip,
    first_gate,
    first_output,
    second_norm,
    second_input,
    second_kernel,
    second_offset,
    second_timestep,
    second_decay,
    second_skip,
    second_gate,
    second_output,
):
    layout = tokens.shape
    sequences = layout[0] * layout[1]
    hidden = tokens.astype(F32).reshape(sequences, layout[2], layout[3])
    ids = segment_terms(segments.reshape(sequences, layout[2]))
    layers = (
        (
            (first_norm, first_input, first_kernel, first_offset, first_gate, first_output),
            (first_timestep, first_decay, first_skip),
        ),
        (
            (second_norm, second_input, second_kernel, second_offset, second_gate, second_output),
            (second_timestep, second_decay, second_skip),
        ),
    )
    stored = []
    first, second = layers[0][0], layers[1][0]
    inner = first[4].shape[0] * lax.axis_size("dp") * lax.axis_size("ctx")
    mixer, everyone = gather_rows(first[1][:, inner:], small_rows(layers))
    smalls = small_weights(everyone, layers)
    shards = [first[5], first[1][:, :inner], second[1][:, inner:]]
    wave = (gather_packed(shards), [shard.shape for shard in shards])
    ids, mixer = lax.optimization_barrier((ids, mixer))
    later = [second[5], second[1][:, :inner]]
    for (_, head_params), small in zip(layers, smalls):
        heads = jnp.stack(list(head_params) + [jnp.zeros_like(head_params[0])] * 5)
        hidden, weights, following, wave, saved = layer_forward(hidden, ids, small, mixer, wave, later, heads)
        stored.append((weights, heads, saved))
        mixer, later = following[0] if following else None, []
    gradient = cotangent.astype(F32).reshape(hidden.shape)
    weights, heads, saved = stored[1]
    gradient, small, terms = layer_backward(gradient, ids, weights, heads, saved, False)
    weights, heads, saved = stored[0]
    gradient, smalls, input_grad, output_grad, other_grads = layer_backward(
        gradient, ids, weights, heads, saved, True, terms, small
    )
    results = []
    for total, (in_grad, out_grad) in (
        (smalls[0], (input_grad, output_grad)),
        (smalls[1], other_grads),
    ):
        parts = unpack_small(total, layers[0][0], heads.shape[1])
        results.append((parts[0], in_grad) + parts[1:] + (out_grad,))
    return (hidden.reshape(layout), gradient.reshape(layout)) + results[0] + results[1]


def solution(mesh):
    weight_specs = (P(BOTH), P(BOTH, None), P(None, BOTH), P(BOTH), P(), P(), P(), P(BOTH), P(BOTH, None))
    tokens_spec = P(None, "dp", "ctx", None)
    return jax.shard_map(
        on_device,
        mesh=mesh,
        in_specs=(tokens_spec, P(None, "dp", "ctx"), tokens_spec) + weight_specs + weight_specs,
        out_specs=(tokens_spec, tokens_spec) + weight_specs + weight_specs,
        check_vma=False,
    )
```

```python
import functools

import jax
import jax.numpy as jnp
from jax import lax
from jax.experimental import pallas as pl
from jax.experimental.pallas import tpu as pltpu
from jax.sharding import PartitionSpec as P

EPSILON = 1e-05
EXACT = lax.Precision.HIGHEST
BF16 = jnp.bfloat16
F32 = jnp.float32
BOTH = ("dp", "ctx")
FAR = -1e30
LANES = 128
EDGE = 8
VMEM_BYTES = 48 * 1024 * 1024
FREE = pl.CostEstimate(flops=0, bytes_accessed=0, transcendentals=0)


def shift_along(x, by):
    size = lax.axis_size("ctx")
    pairs = [(i, i + by) for i in range(size) if 0 <= i + by < size]
    return lax.ppermute(x, "ctx", pairs)


def swap_cores(x):
    return lax.ppermute(x, "ctx", [(i, i ^ 1) for i in range(lax.axis_size("ctx"))])


def swap_chips(x, distance):
    return lax.ppermute(
        x, "ctx", [(i, i ^ (2 * distance)) for i in range(lax.axis_size("ctx"))]
    )


def swap_rows(x, bit):
    return lax.ppermute(x, "dp", [(i, i ^ bit) for i in range(lax.axis_size("dp"))])


def pick(x, index, axis=0):
    return lax.dynamic_index_in_dim(x, index, axis=axis, keepdims=False)


def bits_of(count):
    return [1 << level for level in range((count - 1).bit_length())]


def in_order(mine, got, bit_is_set, axis):
    return jnp.concatenate(
        [jnp.where(bit_is_set, got, mine), jnp.where(bit_is_set, mine, got)], axis=axis
    )


def gather_over_chips(x):
    chips = lax.axis_size("ctx") // 2
    chip = lax.axis_index("ctx") // 2
    if chips <= 4:
        held = jnp.stack([x] + [swap_chips(x, distance) for distance in range(1, chips)])
        return jnp.stack([pick(held, chip ^ place) for place in range(chips)])
    x = x[None]
    for bit in bits_of(chips):
        x = in_order(x, swap_chips(x, bit), (chip // bit) % 2 == 1, 0)
    return x


def gather_rows(shard, aside):
    core = lax.axis_index("ctx") % 2
    order = bits_of(lax.axis_size("dp"))
    cut = shard.shape[1] // 2 // LANES * LANES
    x, aside = lax.optimization_barrier((gather_over_chips(shard), gather_over_chips(aside)))
    ways = [(x[..., :cut], order), (x[..., cut:], order[::-1]), (aside, order)]
    shapes = [part.shape for part, _ in ways]
    parts = [part.reshape((1,) * len(order) + part.shape) for part, _ in ways]
    for turn in range(len(order)):
        joined = []
        for part, (_, bits) in zip(parts, ways):
            bit = bits[turn]
            joined.append(
                in_order(
                    part,
                    swap_rows(part, bit),
                    (lax.axis_index("dp") // bit) % 2 == 1,
                    sorted(bits, reverse=True).index(bit),
                )
            )
        parts = lax.optimization_barrier(joined)
    left, right, aside = [part.reshape((-1,) + shape) for part, shape in zip(parts, shapes)]
    results = []
    for part in (jnp.concatenate([left, right], axis=-1), aside):
        whole = in_order(part[:, :, None], swap_cores(part)[:, :, None], core == 1, 2)
        results.append(whole.reshape((-1, part.shape[-1])))
    return results


def halve_over_rows(x, bits, left):
    me = lax.axis_index("dp")
    left = sorted(left, reverse=True)
    x = x.reshape((2,) * len(left) + x.shape[1:])
    for bit in bits:
        axis = left.index(bit)
        mine = (me // bit) % 2
        got = swap_rows(pick(x, 1 - mine, axis), bit)
        x = (pick(x, mine, axis).astype(F32) + got.astype(F32)).astype(BF16)
        left.remove(bit)
    return x.reshape((1 << len(left),) + x.shape[len(left) :])


def scatter_over_chips(x):
    chips = lax.axis_size("ctx") // 2
    chip = lax.axis_index("ctx") // 2
    if chips <= 4:
        total = pick(x, chip).astype(F32)
        for distance in range(1, chips):
            total = total + swap_chips(pick(x, chip ^ distance), distance).astype(F32)
        return total
    for bit in bits_of(chips)[::-1]:
        x = x.reshape((2, bit) + x.shape[1:])
        mine = (chip // bit) % 2
        got = swap_chips(pick(x, 1 - mine), bit)
        x = (pick(x, mine).astype(F32) + got.astype(F32)).astype(BF16)
    return x[0].astype(F32)


def split_cores(product, own):
    rows, columns = product.shape
    split = product.reshape(rows // own // 2, 2, own, columns)
    return split[:, 0], split[:, 1]


def store_by_core(core, product, own, rows, keep_out, give_out):
    first, second = split_cores(product, own)
    mine = core[0] == 0
    keep_out[:, rows : rows + own] = jnp.where(mine, first, second)
    give_out[:, rows : rows + own] = jnp.where(mine, second, first)


def product_halves(core, lhs, rhs, keep_out, give_out):
    product = dot(lhs[...], rhs[...], TN).astype(BF16)
    store_by_core(core, product, keep_out.shape[1], 0, keep_out, give_out)


def turns_of(groups):
    return 4 if groups % 4 == 0 else 1


def product_by_core(lhs, rhs, columns):
    dps = lax.axis_size("dp")
    chips = lax.axis_size("ctx") // 2
    core = lax.axis_index("ctx") % 2
    tokens, rows = lhs.shape
    groups = dps * chips
    own = rows // (groups * 2)
    shape = (dps, chips, own, columns)
    if own % 16:
        product = dot(lhs, rhs, TN).astype(BF16).reshape(dps, chips, 2, own, columns)
        return pick(product, core, 2), pick(product, 1 - core, 2)
    turns = turns_of(groups)
    out = jax.ShapeDtypeStruct((groups, own, columns), BF16)
    spec = pl.BlockSpec((groups // turns, own, columns), first_index_of_three)
    keep, give = pl.pallas_call(
        product_halves,
        grid=(turns,),
        in_specs=[
            pl.BlockSpec(memory_space=pltpu.SMEM),
            pl.BlockSpec((tokens, rows // turns), second_index_of_two),
            pl.BlockSpec((tokens, columns), no_index_of_two),
        ],
        out_specs=[spec, spec],
        out_shape=[out, out],
        compiler_params=pltpu.CompilerParams(vmem_limit_bytes=VMEM_BYTES),
        cost_estimate=FREE,
    )(core.reshape(1), lhs, rhs)
    return keep.reshape(shape), give.reshape(shape)


def packed_block(lhs, first, second, out_lhs, out_rhs, out):
    groups, height, columns = out.shape
    inner = first.shape[1]
    own = lhs.shape[1] // groups
    out[:, :own, :inner] = dot(lhs[...], first[...], TN).astype(BF16).reshape(groups, own, inner)
    out[:, :own, inner:] = dot(lhs[...], second[...], TN).astype(BF16).reshape(groups, own, columns - inner)
    product = dot(out_lhs[...], out_rhs[...], TN).astype(BF16)
    rest, width = height - own, product.shape[1]
    split = product.reshape(groups, -1, rest, width)
    for turn in range(split.shape[1]):
        out[:, own:, turn * width : (turn + 1) * width] = split[:, turn]
    out[:, own:, split.shape[1] * width :] = jnp.zeros((groups, rest, columns - split.shape[1] * width), BF16)


def packed_product(lhs, first, second, out_lhs, out_rhs):
    count = lax.axis_size("dp") * lax.axis_size("ctx")
    tokens, rows = lhs.shape
    inner, rest = first.shape[1], second.shape[1]
    columns = inner + rest
    own, out_own = rows // count, out_lhs.shape[1] // count
    width = out_rhs.shape[1]
    pieces = columns // width
    height = own + out_own // pieces
    turns = turns_of(count)
    if own % 16 or (out_own // pieces) % 16:
        product = jnp.concatenate([dot(lhs, first, TN), dot(lhs, second, TN)], axis=1).astype(BF16)
        other = dot(out_lhs, out_rhs, TN).astype(BF16).reshape(count, pieces, out_own // pieces, width)
        other = jnp.swapaxes(other, 1, 2).reshape(count, out_own // pieces, pieces * width)
        other = jnp.pad(other, ((0, 0), (0, 0), (0, columns - pieces * width)))
        return jnp.concatenate([product.reshape(count, own, columns), other], axis=1)
    return pl.pallas_call(
        packed_block,
        grid=(turns,),
        in_specs=[
            pl.BlockSpec((tokens, rows // turns), second_index_of_two),
            pl.BlockSpec((tokens, inner), no_index_of_two),
            pl.BlockSpec((tokens, rest), no_index_of_two),
            pl.BlockSpec((tokens, out_lhs.shape[1] // turns), second_index_of_two),
            pl.BlockSpec((tokens, width), no_index_of_two),
        ],
        out_specs=pl.BlockSpec((count // turns, height, columns), first_index_of_three),
        out_shape=jax.ShapeDtypeStruct((count, height, columns), BF16),
        compiler_params=pltpu.CompilerParams(vmem_limit_bytes=VMEM_BYTES),
        cost_estimate=FREE,
    )(lhs, first, second, out_lhs, out_rhs)


def scatter_packed(product, own, width):
    _, height, columns = product.shape
    total = lax.psum_scatter(product, BOTH, scatter_dimension=0, tiled=True).reshape(height, columns)
    pieces = columns // width
    return total[:own], jnp.concatenate([total[own:, i * width : (i + 1) * width] for i in range(pieces)], axis=0)


def first_index_of_three(i):
    return (i, 0, 0)


def second_index_of_two(i):
    return (0, i)


def no_index_of_two(i):
    return (0, 0)


def over_cores(keep, give):
    return (keep.astype(F32) + swap_cores(give).astype(F32)).astype(BF16)


def after(trees, ready):
    return lax.optimization_barrier((trees, ready))[0]


def exchange_chips(blocks):
    chips = blocks.shape[0]
    chip = lax.axis_index("ctx") // 2
    got = [pick(blocks, chip)]
    for distance in range(1, chips):
        got.append(swap_chips(pick(blocks, chip ^ distance), distance))
    return got


def by_sender(got):
    chip = lax.axis_index("ctx") // 2
    held = jnp.stack(got)
    return [pick(held, place ^ chip) for place in range(len(got))]


def carry_along(pair_t, pair_state, forward, work):
    count = lax.axis_size("ctx")
    chips = count // 2
    sequences, states, channels = pair_state.shape
    if chips > 4:

        def advance(_, carried):
            arrived = shift_along((carried * pair_t + pair_state).astype(BF16), 2 if forward else -2)
            return arrived.astype(F32)

        received = lax.fori_loop(0, chips - 1, advance, jnp.zeros_like(pair_state)).astype(BF16)
        done = []
        for items in work:
            for item in items:
                done.append(item(done, pair_state))
        return received, done
    share = channels // chips
    high = pair_t.astype(BF16)
    low = (pair_t - high.astype(F32)).astype(BF16)
    payload = jnp.concatenate(
        [pair_state.astype(BF16), high, low, jnp.zeros((sequences, 14, channels), BF16)], axis=1
    )
    blocks = jnp.moveaxis(payload.reshape(sequences, states + 16, chips, share), 2, 0)
    got = exchange_chips(blocks)
    done = []
    got, done = during(got, done, work[0], payload)
    carried = jnp.zeros((sequences, states, share), F32)
    entering = [None] * chips
    order = range(chips) if forward else range(chips - 1, -1, -1)
    held = by_sender(got)
    for place in order:
        entering[place] = carried.astype(BF16)
        decay = (held[place][:, states : states + 1].astype(F32) + held[place][:, states + 1 : states + 2].astype(F32))
        carried = carried * decay + held[place][:, :states].astype(F32)
    blocks = jnp.stack(entering)
    got = exchange_chips(blocks)
    got, done = during(got, done, work[1], blocks)
    return jnp.concatenate(by_sender(got), axis=-1), done


def during(got, done, items, ready):
    for item in items:
        made = item(done, ready)
        got, made = lax.optimization_barrier((got, made))
        done = done + [made]
    return got, done


def chain(through, mine, give, forward, work):
    core = lax.axis_index("ctx") % 2
    leading = core == (0 if forward else 1)
    other_t = swap_cores(through)
    sent = swap_cores(give).astype(F32)
    own_t, other_t = pick(through, core), pick(other_t, core)
    first_t = jnp.where(leading, own_t, other_t)
    second_t = jnp.where(leading, other_t, own_t)
    own = mine.astype(F32)
    first_state = jnp.where(leading, own, sent)
    pair_state = first_state * second_t + jnp.where(leading, sent, own)
    incoming, work = carry_along(first_t * second_t, pair_state, forward, work)
    second_in = (incoming.astype(F32) * first_t + first_state).astype(BF16)
    keep = jnp.where(leading, incoming, second_in)
    back = swap_cores(jnp.where(leading, second_in, incoming))
    return (keep, back), work


def silu_parts(v):
    gate = 0.5 + 0.5 * jnp.tanh(0.5 * v)
    return v * gate, gate


def pair_mask(rows):
    return lax.broadcasted_iota(jnp.int32, (rows, LANES), 1) < LANES // 2


def spread(per_head, k, mask):
    return jnp.where(mask, per_head[:, 2 * k : 2 * k + 1], per_head[:, 2 * k + 1 : 2 * k + 2])


def dot(a, b, contract, precision=None):
    return lax.dot_general(
        a, b, ((contract[0], contract[1]), ((), ())),
        preferred_element_type=F32, precision=precision,
    )


NN = ((1,), (0,))
NT = ((1,), (1,))
TN = ((0,), (0,))


def triangle(size, upper):
    row = lax.broadcasted_iota(jnp.int32, (size, size), 0)
    col = lax.broadcasted_iota(jnp.int32, (size, size), 1)
    keep = (col >= row) if upper else (col <= row)
    return jnp.where(keep, 1.0, 0.0).astype(F32)


def steps_of(raw, heads):
    shifted = raw + heads[0:1]
    step = jnp.maximum(shifted, 0.0) + jnp.log1p(jnp.exp(-jnp.abs(shifted)))
    rate = -step * jnp.exp(heads[1:2])
    return shifted, step, rate


def half_of(core, mine, other, part, lanes):
    return jnp.where(core[0] == part, mine[0, :, lanes], other[0, :, lanes])


def store_halves(core, values, mine_out, give_out):
    mine_out[0] = jnp.where(core[0] == 0, values[0], values[1])
    give_out[0] = jnp.where(core[0] == 0, values[1], values[0])


def add_up(out, rows, lanes, value):
    first = pl.program_id(0) == 0
    out[rows, lanes] = jnp.where(first, value, out[rows, lanes] + value)


def spread_masks(columns, wide):
    rows = wide.shape[1]
    for s in range(1, 4):
        wide[s - 1] = jnp.broadcast_to(columns[0, :, s : s + 1], (rows, LANES))


def head_sums(values, selector):
    high = values.astype(BF16)
    low = (values - high.astype(F32)).astype(BF16)
    return dot(high, selector, NN) + dot(low, selector, NN)


def fwd_local(core, proj, halo, marks, bias, heads, taps, conv_out, ysum_out, read_out, cum_out, mine_out, give_out, ext, weighted, wide):
    length = proj.shape[1]
    channels = halo.shape[2]
    states = read_out.shape[2]
    inner = channels - 2 * states
    head_rows = heads[...]
    raw = proj[0, :, channels:]
    _, step, rate = steps_of(raw, head_rows)
    cum = dot(triangle(length, False), rate, NN, EXACT)
    cum_t = dot(rate, triangle(length, False), ((0,), (1,)), EXACT)
    cum_out[0] = jnp.concatenate([cum, raw], axis=1)
    last = cum[length - 1 : length]
    end_weight = jnp.exp(last - cum) * marks[0, :, 4:5] * step
    ext[0:EDGE] = halo[0]
    ext[EDGE:] = proj[0, :, :channels]
    spread_masks(marks, wide)

    def activate(lo):
        lanes = slice(lo, lo + LANES)
        total = taps[4:5, lanes] + ext[EDGE:, lanes] * taps[3:4, lanes]
        for s in range(1, 4):
            total = total + ext[EDGE - s : EDGE - s + length, lanes] * (taps[3 - s : 4 - s, lanes] * wide[s - 1])
        conv_out[0, :, lanes] = total
        return silu_parts(total)[0]

    written = activate(inner).astype(BF16)
    readout = activate(inner + states).astype(BF16)
    read_out[0] = readout
    scores = dot(readout, written, NT)
    mask = pair_mask(length)
    blocked = bias[0]
    zero = jnp.zeros((length, LANES), BF16)
    for k in range(inner // LANES):
        lo = k * LANES
        x = activate(lo)
        scaled = (x * spread(step, k, mask)).astype(BF16)
        weighted[:, lo : lo + LANES] = (x * spread(end_weight, k, mask)).astype(BF16)
        mixing = []
        for h in (2 * k, 2 * k + 1):
            gap = cum[:, h : h + 1] - cum_t[h : h + 1, :]
            mixing.append((jnp.exp(gap + blocked) * scores).astype(BF16))
        values = jnp.concatenate(
            [jnp.where(mask, scaled, zero), jnp.where(mask, zero, scaled)], axis=0
        )
        result = dot(jnp.concatenate(mixing, axis=1), values, NN)
        ysum_out[0, :, lo : lo + LANES] = result + x * spread(head_rows[2:3], k, mask[0:1])
    half = inner // 2
    store_halves(
        core,
        [dot(written, weighted[:, part * half : (part + 1) * half], TN).astype(BF16) for part in range(2)],
        mine_out,
        give_out,
    )


def fwd_mix(core, ysum, read, cum, marks, in_mine, in_other, gates, gain, mixed_out, y_out, gated):
    length = ysum.shape[1]
    inner = ysum.shape[2]
    half = inner // 2
    entry = jnp.exp(cum[0][:, : cum.shape[2] // 2]) * marks[0, :, 5:6]
    mask = pair_mask(length)
    squares = jnp.zeros((length, LANES), F32)
    for k in range(inner // LANES):
        lo = k * LANES
        part, at = lo // half, lo % half
        carried = dot(read[0], half_of(core, in_mine, in_other, part, slice(at, at + LANES)), NN)
        y = ysum[0, :, lo : lo + LANES] + spread(entry, k, mask) * carried
        y_out[0, :, lo : lo + LANES] = y
        value = y * silu_parts(gates[0, :, lo : lo + LANES])[0]
        gated[:, lo : lo + LANES] = value
        squares = squares + value * value
    scale = lax.rsqrt(jnp.sum(squares, axis=1, keepdims=True) * (1.0 / inner) + EPSILON)
    for k in range(inner // LANES):
        lanes = slice(k * LANES, (k + 1) * LANES)
        mixed_out[0, :, lanes] = (gated[:, lanes] * scale * gain[:, lanes]).astype(BF16)


def bwd_gate(core, grad, y, gates, gain, cum, marks, read, dy_out, dgate_out, dgain_out, mine_out, give_out, weighted):
    length = y.shape[1]
    inner = y.shape[2]
    entry = jnp.exp(cum[0][:, : cum.shape[2] // 2]) * marks[0, :, 5:6]
    mask = pair_mask(length)
    squares = jnp.zeros((length, LANES), F32)
    cross = jnp.zeros((length, LANES), F32)
    for k in range(inner // LANES):
        lanes = slice(k * LANES, (k + 1) * LANES)
        value = y[0, :, lanes] * silu_parts(gates[0, :, lanes])[0]
        squares = squares + value * value
        cross = cross + value * grad[0, :, lanes] * gain[:, lanes]
    scale = lax.rsqrt(jnp.sum(squares, axis=1, keepdims=True) * (1.0 / inner) + EPSILON)
    inward = jnp.sum(cross, axis=1, keepdims=True) * (scale * scale * scale * (1.0 / inner))
    for k in range(inner // LANES):
        lanes = slice(k * LANES, (k + 1) * LANES)
        z = gates[0, :, lanes]
        active, sigmoid = silu_parts(z)
        yk = y[0, :, lanes]
        value = yk * active
        g = grad[0, :, lanes]
        add_up(dgain_out, slice(0, 1), lanes, jnp.sum(g * value * scale, axis=0, keepdims=True))
        dvalue = g * gain[:, lanes] * scale - value * inward
        dy = dvalue * active
        dy_out[0, :, lanes] = dy
        dgate_out[0, :, lanes] = (dvalue * yk * (sigmoid + active * (1.0 - sigmoid))).astype(BF16)
        weighted[:, lanes] = (dy * spread(entry, k, mask)).astype(BF16)
    half = inner // 2
    store_halves(
        core,
        [dot(read[0], weighted[:, part * half : (part + 1) * half], TN).astype(BF16) for part in range(2)],
        mine_out,
        give_out,
    )


def bwd_diag(core, conv, ysum, dy, read, cum, marks, bias_t, heads, selector, in_mine, in_other, dscaled_out, joint_out, terms, entered):
    length = ysum.shape[1]
    inner = ysum.shape[2]
    half = inner // 2
    states = read.shape[2]
    head_rows = heads[...]
    heads_n = heads.shape[1]
    _, step, rate = steps_of(cum[0][:, heads_n:], head_rows)
    cums = cum[0][:, :heads_n]
    cum_t = dot(rate, triangle(length, False), ((0,), (1,)), EXACT)
    entry = jnp.exp(cums) * marks[0, :, 5:6]
    written = silu_parts(conv[0, :, inner : inner + states])[0].astype(BF16)
    readout = read[0]
    scores_t = dot(written, readout, NT)
    mask = pair_mask(length)
    blocked = bias_t[0]
    zero = jnp.zeros((length, LANES), BF16)
    dscores_t = jnp.zeros((length, length), F32)
    for k in range(inner // LANES):
        lo = k * LANES
        lanes = slice(lo, lo + LANES)
        x = silu_parts(conv[0, :, lanes])[0]
        scaled = (x * spread(step, k, mask)).astype(BF16)
        grad = dy[0, :, lanes]
        low = grad.astype(BF16)
        decays, mixing = [], []
        for h in (2 * k, 2 * k + 1):
            gap = cum_t[h : h + 1, :] - cums[:, h : h + 1]
            decay = jnp.exp(gap + blocked)
            decays.append(decay)
            mixing.append((decay * scores_t).astype(BF16))
        grads = jnp.concatenate([jnp.where(mask, low, zero), jnp.where(mask, zero, low)], axis=0)
        dscaled = dot(jnp.concatenate(mixing, axis=1), grads, NN)
        dscaled_out[0, :, lanes] = dscaled
        values = jnp.concatenate(
            [jnp.where(mask, scaled, zero), jnp.where(mask, zero, scaled)], axis=0
        )
        dmixing = dot(values, low, NT)
        dscores_t = dscores_t + dmixing[:length] * decays[0] + dmixing[length:] * decays[1]
        entered_k = (grad * spread(entry, k, mask)).astype(BF16)
        entered[:, lanes] = entered_k
        part, at = lo // half, lo % half
        carried = dot(readout, half_of(core, in_mine, in_other, part, slice(at, at + LANES)), NN)
        diagonal = ysum[0, :, lanes] - x * spread(head_rows[2:3], k, mask[0:1])
        terms[:, lanes] = (
            low.astype(F32) * diagonal
            - scaled.astype(F32) * dscaled
            + entered_k.astype(F32) * carried
        )
    joint_out[0, :, 2 * states :] = head_sums(terms[...], selector[...])
    dlow = dscores_t.astype(BF16)
    joint_out[0, :, :states] = dot(dlow, readout, NN)
    dread = dot(dlow, written, TN)
    for part in range(2):
        dread = dread + dot(
            entered[:, part * half : (part + 1) * half],
            half_of(core, in_mine, in_other, part, slice(None)),
            NT,
        )
    joint_out[0, :, states : 2 * states] = dread


def bwd_local(core, proj, halo, conv, dy, dscaled, joint, cum, marks, backs, heads, taps, selector, in_mine, in_other, out_mine, out_other, through, dproj_out, dhalo_out, dtaps_out, dhead_out, ext, dconv, ending, terms, wide, wide_back):
    length = proj.shape[1]
    channels = halo.shape[2]
    states = (joint.shape[2] - LANES) // 2
    inner = channels - 2 * states
    half = inner // 2
    head_rows = heads[...]
    heads_n = heads.shape[1]
    shifted, step, rate = steps_of(cum[0][:, heads_n:], head_rows)
    cums = cum[0][:, :heads_n]
    last = cums[length - 1 : length]
    end_decay = jnp.exp(last - cums) * marks[0, :, 4:5]
    end_weight = end_decay * step
    mask = pair_mask(length)
    written_v, written_s = silu_parts(conv[0, :, inner : inner + states])
    written = written_v.astype(BF16)
    ext[0:EDGE] = halo[0]
    ext[EDGE:] = proj[0, :, :channels]
    dconv[0:EDGE] = jnp.zeros((EDGE, channels), F32)
    dconv[EDGE + length :] = jnp.zeros((EDGE, channels), F32)
    products, skips = [], []
    for k in range(inner // LANES):
        lo = k * LANES
        lanes = slice(lo, lo + LANES)
        part, at = lo // half, lo % half
        pre = conv[0, :, lanes]
        x, sigmoid = silu_parts(pre)
        grad = dy[0, :, lanes]
        back = half_of(core, out_mine, out_other, part, slice(at, at + LANES))
        entering = half_of(core, in_mine, in_other, part, slice(at, at + LANES))
        products.append(
            jnp.sum(back.astype(F32) * entering.astype(F32), axis=0, keepdims=True)
        )
        ends = dot(written, back, NN)
        inside = dscaled[0, :, lanes] + spread(end_decay, k, mask) * ends
        weighted = (x * spread(end_weight, k, mask)).astype(BF16)
        ending[:, lanes] = weighted
        terms[0:length, lanes] = x * inside
        terms[length : 2 * length, lanes] = weighted.astype(F32) * ends
        skips.append(jnp.sum(grad * x, axis=0, keepdims=True))
        dx = spread(step, k, mask) * inside + spread(head_rows[2:3], k, mask[0:1]) * grad
        dconv[EDGE : EDGE + length, lanes] = dx * (sigmoid + x * (1.0 - sigmoid))
    dw = joint[0, :, :states]
    for part in range(2):
        dw = dw + dot(
            ending[:, part * half : (part + 1) * half],
            half_of(core, out_mine, out_other, part, slice(None)),
            NT,
        )
    dconv[EDGE : EDGE + length, inner : inner + states] = dw * (
        written_s + written_v * (1.0 - written_s)
    )
    read_v, read_s = silu_parts(conv[0, :, inner + states :])
    dconv[EDGE : EDGE + length, inner + states :] = joint[0, :, states : 2 * states] * (read_s + read_v * (1.0 - read_s))
    sums = head_sums(terms[...], selector[...])
    dstep = sums[:length, :heads_n]
    ended = sums[length:, :heads_n]
    lane_sums = jnp.concatenate(
        [jnp.concatenate(products, axis=1), jnp.concatenate(skips, axis=1), jnp.zeros((6, inner), F32)], axis=0
    )
    by_head = head_sums(lane_sums, selector[...])[:, :heads_n]
    kept = by_head[0:1]
    at_last = jnp.sum(ended, axis=0, keepdims=True) + kept * through[0]
    row = lax.broadcasted_iota(jnp.int32, (length, heads_n), 0)
    dcums = joint[0, :, 2 * states : 2 * states + heads_n] - ended + jnp.where(row == length - 1, at_last, 0.0)
    drate = dot(triangle(length, True), dcums, NN, EXACT)
    dstep = dstep - drate * jnp.exp(head_rows[1:2])
    draw = dstep * (1.0 / (1.0 + jnp.exp(-shifted)))
    dproj_out[0, :, channels:] = draw.astype(BF16)
    add_up(
        dhead_out,
        slice(None),
        slice(None),
        jnp.concatenate(
            [
                jnp.sum(draw, axis=0, keepdims=True),
                jnp.sum(drate * rate, axis=0, keepdims=True),
                by_head[1:2],
                jnp.zeros((5, heads_n), F32),
            ],
            axis=0,
        ),
    )
    rows = length + EDGE
    spread_masks(marks, wide)
    spread_masks(backs, wide_back)
    for lo in range(0, channels, LANES):
        lanes = slice(lo, lo + LANES)
        own = dconv[EDGE : EDGE + length, lanes]
        total = dconv[0:rows, lanes] * taps[3:4, lanes]
        sums = [jnp.sum(own * ext[EDGE:, lanes], axis=0, keepdims=True)]
        for s in range(1, 4):
            total = total + dconv[s : s + rows, lanes] * (taps[3 - s : 4 - s, lanes] * wide_back[s - 1])
            sums.append(
                jnp.sum(own * ext[EDGE - s : EDGE - s + length, lanes] * wide[s - 1], axis=0, keepdims=True)
            )
        dproj_out[0, :, lanes] = total[EDGE:].astype(BF16)
        dhalo_out[0, 0:EDGE, lanes] = total[:EDGE]
        dhalo_out[0, EDGE:, lanes] = total[length:]
        sums = sums[::-1] + [jnp.sum(own, axis=0, keepdims=True), jnp.zeros((3, LANES), F32)]
        add_up(dtaps_out, slice(None), lanes, jnp.concatenate(sums, axis=0))


def per_sequence(kernel, inputs, outputs, scratch):
    sequences = None
    in_specs = [pl.BlockSpec(memory_space=pltpu.SMEM)]
    arrays = [(lax.axis_index("ctx") % 2).reshape(1)]
    for array, axis in inputs:
        if axis is not None:
            sequences = array.shape[axis]
        in_specs.append(block_spec(array.shape, axis))
        arrays.append(array)
    out_specs = [block_spec(shape, axis) for shape, _, axis in outputs]
    out_shape = [jax.ShapeDtypeStruct(shape, dtype) for shape, dtype, _ in outputs]
    return pl.pallas_call(
        kernel,
        grid=(sequences,),
        in_specs=in_specs,
        out_specs=out_specs,
        out_shape=out_shape,
        scratch_shapes=scratch,
        compiler_params=pltpu.CompilerParams(vmem_limit_bytes=VMEM_BYTES),
        cost_estimate=FREE,
    )(*arrays)


def block_spec(shape, axis):
    block = tuple(1 if d == axis else size for d, size in enumerate(shape))
    rank = len(shape)
    return pl.BlockSpec(
        block, functools.partial(block_index, rank, axis)
    )


def block_index(rank, axis, i):
    return tuple(i if d == axis else 0 for d in range(rank))


def rms_scale(values, gain_vector):
    return (
        values
        * lax.rsqrt(jnp.mean(values * values, axis=-1, keepdims=True) + EPSILON)
        * gain_vector
    )


def lanes_of(per_head, size):
    sequences, heads = per_head.shape
    spread_out = jnp.repeat(per_head, size, axis=1).reshape(sequences, 2, 1, heads * size // 2)
    return jnp.moveaxis(spread_out, 1, 0)


def layer_forward(hidden, ids, small, mix_weight, wave, later, head_params):
    norm_gain, taps, gate_gain = small
    sequences, length, width = hidden.shape
    channels = taps.shape[1]
    inner = gate_gain.shape[0]
    states = (channels - inner) // 2
    heads_n = head_params.shape[1]
    size = inner // heads_n
    gain = norm_gain.astype(F32)
    normed = rms_scale(hidden, gain).astype(BF16)
    proj = jnp.dot(normed, mix_weight, preferred_element_type=F32)
    edge = shift_along(proj[:, length - EDGE :, :channels], 1)
    conv, ysum, read, cum, mine, give = per_sequence(
        fwd_local,
        [(proj, 0), (edge, 0), (ids["marks"], 0), (ids["bias"], 0), (head_params, None), (taps, None)],
        [
            ((sequences, length, channels), F32, 0),
            ((sequences, length, inner), F32, 0),
            ((sequences, length, states), BF16, 0),
            ((sequences, length, 2 * heads_n), F32, 0),
            ((sequences, states, inner // 2), BF16, 0),
            ((sequences, states, inner // 2), BF16, 0),
        ],
        [
            pltpu.VMEM((length + EDGE, channels), F32),
            pltpu.VMEM((length, inner), BF16),
            pltpu.VMEM((3, length, LANES), F32),
        ],
    )
    through = jnp.exp(cum[:, -1, :heads_n]) * ids["carry"][:, None]
    through_lanes = lanes_of(through, size)
    packed, shapes = wave
    following_wave = None
    if later:
        following_wave = (gather_packed(after(later, mine)), [shard.shape for shard in later])
    arrived = lambda done, ready: unpack(after(packed, ready), shapes)[:2]
    used = lambda done, ready: [jnp.dot(normed, done[0][1], preferred_element_type=F32)] + unpack(
        after(packed, ready), shapes
    )[2:]
    incoming, made = chain(
        through_lanes, mine, give, True, [[arrived], [used]] if later else [[], [arrived, used]]
    )
    (out_weight, gate_weight), (gates, *following) = made
    weights = (norm_gain, mix_weight, gate_weight, taps, gate_gain, out_weight)
    mixed, y = per_sequence(
        fwd_mix,
        [(ysum, 0), (read, 0), (cum, 0), (ids["marks"], 0), (incoming[0], 0), (incoming[1], 0), (gates, 0), (gate_gain.astype(F32)[None], None)],
        [((sequences, length, inner), BF16, 0), ((sequences, length, inner), F32, 0)],
        [pltpu.VMEM((length, inner), F32)],
    )
    update = jnp.dot(mixed, out_weight, preferred_element_type=F32)
    saved = (hidden, gain, normed, proj, edge, gates, conv, ysum, read, cum, through, through_lanes, incoming, mixed, y)
    return hidden + update, weights, following, following_wave, saved


def layer_backward(gradient, ids, weights, head_params, saved, final, other_terms=None, other_small=None):
    hidden, gain, normed, proj, edge, gates, conv, ysum, read, cum, through, through_lanes, incoming, mixed, y = saved
    _, mix_weight, gate_weight, taps, gate_gain, out_weight = weights
    sequences, length, width = hidden.shape
    tokens = sequences * length
    channels = taps.shape[1]
    inner = gate_gain.shape[0]
    states = (channels - inner) // 2
    heads_n = head_params.shape[1]
    size = inner // heads_n
    update_low = gradient.astype(BF16)
    mixed_grad = lax.dot_general(
        update_low, out_weight, (((2,), (1,)), ((), ())), preferred_element_type=F32
    )
    dy, dgates, dgain, mine, give = per_sequence(
        bwd_gate,
        [(mixed_grad, 0), (y, 0), (gates, 0), (gate_gain.astype(F32)[None], None), (cum, 0), (ids["marks"], 0), (read, 0)],
        [
            ((sequences, length, inner), F32, 0),
            ((sequences, length, inner), BF16, 0),
            ((8, inner), F32, None),
            ((sequences, states, inner // 2), BF16, 0),
            ((sequences, states, inner // 2), BF16, 0),
        ],
        [pltpu.VMEM((length, inner), BF16)],
    )
    head_of = jnp.arange(inner) // size
    selector = (head_of[:, None] == jnp.arange(LANES)[None]).astype(BF16)

    def diagonal(done, ready):
        return per_sequence(
            bwd_diag,
            [(conv, 0), (ysum, 0), (after(dy, ready), 0), (read, 0), (cum, 0), (ids["marks"], 0),
             (ids["bias_t"], 0), (head_params, None), (selector, None), (incoming[0], 0), (incoming[1], 0)],
            [
                ((sequences, length, inner), F32, 0),
                ((sequences, length, 2 * states + LANES), F32, 0),
            ],
            [pltpu.VMEM((length, inner), F32), pltpu.VMEM((length, inner), BF16)],
        )

    flat = normed.reshape(tokens, width)
    flat_gates = dgates.reshape(tokens, inner)
    output_terms = (mixed.reshape(tokens, inner), update_low.reshape(tokens, width))
    order = bits_of(lax.axis_size("dp"))
    if final:
        other_product = packed_product(*after(other_terms, mine))
        outgoing, made = chain(
            through_lanes,
            mine,
            give,
            False,
            [
                [
                    diagonal,
                    lambda done, ready: [
                        product_by_core(*after(output_terms, ready), width),
                        product_by_core(*after((flat, flat_gates), ready), inner),
                    ],
                ],
                [lambda done, ready: [over_cores(*product) for product in done[1]]],
            ],
        )
        (dscaled, joint), _, pair = made
        outgoing, pair = lax.optimization_barrier((outgoing, pair))
        own = inner // (2 * lax.axis_size("dp") * lax.axis_size("ctx") // 2)
        pair = [halve_over_rows(pair[0], order[:1], order), halve_over_rows(pair[1], order[-1:], order)]
    else:
        outgoing, made = chain(through_lanes, mine, give, False, [[diagonal], []])
        dscaled, joint = made[0]
    dproj, dhalo, dtaps, dheads = per_sequence(
        bwd_local,
        [(proj, 0), (edge, 0), (conv, 0), (dy, 0), (dscaled, 0), (joint, 0), (cum, 0),
         (ids["marks"], 0), (ids["backs"], 0), (head_params, None), (taps, None), (selector, None),
         (incoming[0], 0), (incoming[1], 0), (outgoing[0], 0), (outgoing[1], 0), (through[:, None], 0)],
        [
            ((sequences, length, channels + heads_n), BF16, 0),
            ((sequences, 2 * EDGE, channels), F32, 0),
            ((8, channels), F32, None),
            ((8, heads_n), F32, None),
        ],
        [
            pltpu.VMEM((length + EDGE, channels), F32),
            pltpu.VMEM((length + 2 * EDGE, channels), F32),
            pltpu.VMEM((length, inner), BF16),
            pltpu.VMEM((2 * length, inner), F32),
            pltpu.VMEM((3, length, LANES), F32),
            pltpu.VMEM((3, length + EDGE, LANES), F32),
        ],
    )
    if final:
        dproj, dhalo, pair = lax.optimization_barrier((dproj, dhalo, pair))
        pair = [
            halve_over_rows(pair[0], order[1:], order[1:])[0],
            halve_over_rows(pair[1], order[:-1], order[:-1])[0],
        ]
        pair = jnp.concatenate([pair[0]] + jnp.split(pair[1], inner // width, axis=2), axis=1)
    returned = shift_along(dhalo[:, :EDGE].astype(BF16), -1).astype(F32)
    tail = (dhalo[:, EDGE:] + returned).astype(BF16)
    dproj = lax.dynamic_update_slice(dproj, tail, (0, length - EDGE, 0))
    flat_grad = dproj.reshape(tokens, -1)
    if final:
        other_small = after(other_small, flat_grad)
        product = product_by_core(flat, flat_grad, flat_grad.shape[1])
        dproj, product, pair = lax.optimization_barrier((dproj, product, pair))
        summed = over_cores(*product)
        cut = channels // 2 // LANES * LANES
        pair = scatter_over_chips(pair)
        first_parts = [
            halve_over_rows(summed[..., :cut], order[:1], order),
            halve_over_rows(summed[..., cut:], order[-1:], order),
        ]
    normed_grad = lax.dot_general(
        dproj, mix_weight, (((2,), (1,)), ((), ())), preferred_element_type=F32
    ) + lax.dot_general(dgates, gate_weight, (((2,), (1,)), ((), ())), preferred_element_type=F32)
    _, norm_pull = jax.vjp(rms_scale, hidden, gain)
    hidden_grad, norm_grad = norm_pull(normed_grad)
    small_terms = (norm_grad, dtaps, dgain, dheads)
    gradient = gradient + hidden_grad
    if not final:
        return gradient, small_terms, (flat, flat_gates, flat_grad) + output_terms
    chips = lax.axis_size("ctx") // 2
    core, chip = lax.axis_index("ctx") % 2, lax.axis_index("ctx") // 2
    devices = lax.axis_size("dp") * lax.axis_size("ctx")
    small = jnp.concatenate([by_device(devices, *small_terms), by_device(devices, *other_small)], axis=1)
    small = small.reshape(devices // 2, 2, -1)
    small = pick(small, core, 1) + swap_cores(pick(small, 1 - core, 1))
    first_parts, small = lax.optimization_barrier((first_parts, small))
    second_parts = [
        halve_over_rows(first_parts[0], order[1:], order[1:])[0],
        halve_over_rows(first_parts[1], order[:-1], order[:-1])[0],
    ]
    mine = lax.axis_index("dp")
    total = small
    for bit in order[::-1]:
        total = total.reshape((2, bit * chips) + total.shape[1:])
        half = (mine // bit) % 2
        total = pick(total, half) + swap_rows(pick(total, 1 - half), bit)
    other_grads = scatter_packed(other_product, width // (inner // own), width)
    second_parts, total = lax.optimization_barrier((second_parts, total))
    last = scatter_over_chips(jnp.concatenate(second_parts, axis=-1))
    total, other_grads = lax.optimization_barrier((total, other_grads))
    small = pick(total, chip)
    for distance in range(1, chips):
        small = small + swap_chips(pick(total, chip ^ distance), distance)
    small, pair = lax.optimization_barrier((small, pair))
    small = jnp.split(small, 2)
    output_grad = pair[:own]
    gates_grad = jnp.concatenate(jnp.split(pair[own:], inner // width, axis=0), axis=1)
    input_grad = jnp.concatenate([gates_grad, last], axis=1)
    return gradient, small, input_grad, output_grad, tuple(grad.astype(F32) for grad in other_grads)


def by_device(devices, norm_grad, dtaps, dgain, dheads):
    return jnp.concatenate(
        [
            norm_grad.reshape(devices, -1),
            dtaps[:5].reshape(5, devices, -1).swapaxes(0, 1).reshape(devices, -1),
            dgain[0].reshape(devices, -1),
            jnp.broadcast_to(dheads[:3].reshape(1, -1), (devices, 3 * dheads.shape[1])),
        ],
        axis=1,
    )


def unpack_small(total, shards, heads_n):
    norm, _, kernel, offset, gate, _ = shards
    sizes = (norm.size, kernel.size, offset.size, gate.size, heads_n, heads_n, heads_n)
    parts, start = [], 0
    for size in sizes:
        parts.append(total[start : start + size])
        start += size
    norm_grad, taps_grad, offset_grad, gain_grad, timestep, decay, skip = parts
    return norm_grad, taps_grad.reshape(kernel.shape), offset_grad, timestep, decay, skip, gain_grad


def gather_packed(shards):
    width = shards[0].shape[1]
    pieces = []
    for shard in shards:
        for start in range(0, shard.shape[1], width):
            piece = shard[:, start : start + width]
            pieces.append(jnp.pad(piece, ((0, 0), (0, width - piece.shape[1]))))
    packed = jnp.concatenate(pieces, axis=0)
    return lax.all_gather(packed, BOTH, axis=0, tiled=True).reshape((-1,) + packed.shape)


def unpack(packed, shapes):
    width = packed.shape[2]
    weights = []
    row = 0
    for rows, columns in shapes:
        parts = []
        for start in range(0, columns, width):
            part = packed[:, row : row + rows, : min(width, columns - start)]
            parts.append(part.reshape(-1, part.shape[2]))
            row += rows
        weights.append(parts[0] if len(parts) == 1 else jnp.concatenate(parts, axis=1))
    return weights


def small_rows(layers):
    rows = []
    for shards, _ in layers:
        norm, _, kernel, offset, gate, _ = shards
        rows += [norm, kernel.reshape(-1), offset, gate]
    return jnp.concatenate(rows)[None]


def small_weights(everyone, layers):
    parts, start = [], 0
    for shards, _ in layers:
        norm, _, kernel, offset, gate, _ = shards
        for row in (norm, kernel.reshape(-1), offset, gate):
            parts.append(everyone[:, start : start + row.shape[0]])
            start += row.shape[0]
    count = everyone.shape[0]
    result = []
    for layer in range(len(layers)):
        norm, kernel, offset, gate = parts[4 * layer : 4 * layer + 4]
        taps = layers[layer][0][2].shape[0]
        kernel = kernel.reshape(count, taps, -1).swapaxes(0, 1).reshape(taps, -1).astype(F32)
        offset = offset.reshape(1, -1).astype(F32)
        packed_taps = jnp.concatenate([kernel, offset, jnp.zeros((8 - taps - 1, kernel.shape[1]), F32)], axis=0)
        result.append((norm.reshape(-1), packed_taps, gate.reshape(-1)))
    return result


def segment_terms(segments):
    sequences, length = segments.shape
    ids = segments.astype(F32)
    before = shift_along(ids[:, length - EDGE :] + 1.0, 1) - 1.0
    joined = jnp.concatenate([before, ids], axis=1)
    after = jnp.concatenate([joined, jnp.full((sequences, EDGE), -2.0, F32)], axis=1)
    marks, backs = [], []
    for s in range(4):
        marks.append((joined[:, EDGE - s : EDGE - s + length] == ids).astype(F32))
        backs.append((after[:, s : s + length + EDGE] == joined).astype(F32))
    last = ids[:, -1:]
    prev = before[:, -1:]
    marks.append((ids == last).astype(F32))
    marks.append((ids == prev).astype(F32))
    marks += [jnp.zeros_like(ids)] * 2
    causal = jnp.tril(jnp.ones((length, length), jnp.bool_))
    allowed = causal[None] & (ids[:, :, None] == ids[:, None, :])
    allowed_t = causal.T[None] & (ids[:, :, None] == ids[:, None, :])
    return {
        "marks": jnp.stack(marks, axis=2),
        "backs": jnp.stack(backs + backs, axis=2),
        "bias": jnp.where(allowed, 0.0, FAR).astype(F32),
        "bias_t": jnp.where(allowed_t, 0.0, FAR).astype(F32),
        "carry": (last == prev).astype(F32)[:, 0],
    }


def on_device(
    tokens,
    segments,
    cotangent,
    first_norm,
    first_input,
    first_kernel,
    first_offset,
    first_timestep,
    first_decay,
    first_skip,
    first_gate,
    first_output,
    second_norm,
    second_input,
    second_kernel,
    second_offset,
    second_timestep,
    second_decay,
    second_skip,
    second_gate,
    second_output,
):
    layout = tokens.shape
    sequences = layout[0] * layout[1]
    hidden = tokens.astype(F32).reshape(sequences, layout[2], layout[3])
    ids = segment_terms(segments.reshape(sequences, layout[2]))
    layers = (
        (
            (first_norm, first_input, first_kernel, first_offset, first_gate, first_output),
            (first_timestep, first_decay, first_skip),
        ),
        (
            (second_norm, second_input, second_kernel, second_offset, second_gate, second_output),
            (second_timestep, second_decay, second_skip),
        ),
    )
    stored = []
    first, second = layers[0][0], layers[1][0]
    inner = first[4].shape[0] * lax.axis_size("dp") * lax.axis_size("ctx")
    mixer, everyone = gather_rows(first[1][:, inner:], small_rows(layers))
    smalls = small_weights(everyone, layers)
    shards = [first[5], first[1][:, :inner], second[1][:, inner:]]
    wave = (gather_packed(shards), [shard.shape for shard in shards])
    ids, mixer = lax.optimization_barrier((ids, mixer))
    later = [second[5], second[1][:, :inner]]
    for (_, head_params), small in zip(layers, smalls):
        heads = jnp.stack(list(head_params) + [jnp.zeros_like(head_params[0])] * 5)
        hidden, weights, following, wave, saved = layer_forward(hidden, ids, small, mixer, wave, later, heads)
        stored.append((weights, heads, saved))
        mixer, later = following[0] if following else None, []
    gradient = cotangent.astype(F32).reshape(hidden.shape)
    weights, heads, saved = stored[1]
    gradient, small, terms = layer_backward(gradient, ids, weights, heads, saved, False)
    weights, heads, saved = stored[0]
    gradient, smalls, input_grad, output_grad, other_grads = layer_backward(
        gradient, ids, weights, heads, saved, True, terms, small
    )
    results = []
    for total, (in_grad, out_grad) in (
        (smalls[0], (input_grad, output_grad)),
        (smalls[1], other_grads),
    ):
        parts = unpack_small(total, layers[0][0], heads.shape[1])
        results.append((parts[0], in_grad) + parts[1:] + (out_grad,))
    return (hidden.reshape(layout), gradient.reshape(layout)) + results[0] + results[1]


def solution(mesh):
    weight_specs = (P(BOTH), P(BOTH, None), P(None, BOTH), P(BOTH), P(), P(), P(), P(BOTH), P(BOTH, None))
    tokens_spec = P(None, "dp", "ctx", None)
    return jax.shard_map(
        on_device,
        mesh=mesh,
        in_specs=(tokens_spec, P(None, "dp", "ctx"), tokens_spec) + weight_specs + weight_specs,
        out_specs=(tokens_spec, tokens_spec) + weight_specs + weight_specs,
        check_vma=False,
    )
```

```python
import functools

import jax
import jax.numpy as jnp
from jax import lax
from jax.experimental import pallas as pl
from jax.experimental.pallas import tpu as pltpu
from jax.sharding import PartitionSpec as P

EPSILON = 1e-05
EXACT = lax.Precision.HIGHEST
BF16 = jnp.bfloat16
F32 = jnp.float32
BOTH = ("dp", "ctx")
FAR = -1e30
LANES = 128
EDGE = 8
VMEM_BYTES = 48 * 1024 * 1024
FREE = pl.CostEstimate(flops=0, bytes_accessed=0, transcendentals=0)


def shift_along(x, by):
    size = lax.axis_size("ctx")
    pairs = [(i, i + by) for i in range(size) if 0 <= i + by < size]
    return lax.ppermute(x, "ctx", pairs)


def swap_cores(x):
    return lax.ppermute(x, "ctx", [(i, i ^ 1) for i in range(lax.axis_size("ctx"))])


def swap_chips(x, distance):
    return lax.ppermute(
        x, "ctx", [(i, i ^ (2 * distance)) for i in range(lax.axis_size("ctx"))]
    )


def swap_rows(x, bit):
    return lax.ppermute(x, "dp", [(i, i ^ bit) for i in range(lax.axis_size("dp"))])


def pick(x, index, axis=0):
    return lax.dynamic_index_in_dim(x, index, axis=axis, keepdims=False)


def bits_of(count):
    return [1 << level for level in range((count - 1).bit_length())]


def in_order(mine, got, bit_is_set, axis):
    return jnp.concatenate(
        [jnp.where(bit_is_set, got, mine), jnp.where(bit_is_set, mine, got)], axis=axis
    )


def gather_over_chips(x):
    chips = lax.axis_size("ctx") // 2
    chip = lax.axis_index("ctx") // 2
    if chips <= 4:
        held = jnp.stack([x] + [swap_chips(x, distance) for distance in range(1, chips)])
        return jnp.stack([pick(held, chip ^ place) for place in range(chips)])
    x = x[None]
    for bit in bits_of(chips):
        x = in_order(x, swap_chips(x, bit), (chip // bit) % 2 == 1, 0)
    return x


def gather_rows(shard, aside):
    core = lax.axis_index("ctx") % 2
    order = bits_of(lax.axis_size("dp"))
    cut = shard.shape[1] // 2 // LANES * LANES
    x, aside = lax.optimization_barrier((gather_over_chips(shard), gather_over_chips(aside)))
    ways = [(x[..., :cut], order), (x[..., cut:], order[::-1]), (aside, order)]
    shapes = [part.shape for part, _ in ways]
    parts = [part.reshape((1,) * len(order) + part.shape) for part, _ in ways]
    for turn in range(len(order)):
        joined = []
        for part, (_, bits) in zip(parts, ways):
            bit = bits[turn]
            joined.append(
                in_order(
                    part,
                    swap_rows(part, bit),
                    (lax.axis_index("dp") // bit) % 2 == 1,
                    sorted(bits, reverse=True).index(bit),
                )
            )
        parts = lax.optimization_barrier(joined)
    left, right, aside = [part.reshape((-1,) + shape) for part, shape in zip(parts, shapes)]
    results = []
    for part in (jnp.concatenate([left, right], axis=-1), aside):
        whole = in_order(part[:, :, None], swap_cores(part)[:, :, None], core == 1, 2)
        results.append(whole.reshape((-1, part.shape[-1])))
    return results


def halve_over_rows(x, bits, left):
    me = lax.axis_index("dp")
    left = sorted(left, reverse=True)
    x = x.reshape((2,) * len(left) + x.shape[1:])
    for bit in bits:
        axis = left.index(bit)
        mine = (me // bit) % 2
        got = swap_rows(pick(x, 1 - mine, axis), bit)
        x = (pick(x, mine, axis).astype(F32) + got.astype(F32)).astype(BF16)
        left.remove(bit)
    return x.reshape((1 << len(left),) + x.shape[len(left) :])


def scatter_over_chips(x):
    chips = lax.axis_size("ctx") // 2
    chip = lax.axis_index("ctx") // 2
    if chips <= 4:
        total = pick(x, chip).astype(F32)
        for distance in range(1, chips):
            total = total + swap_chips(pick(x, chip ^ distance), distance).astype(F32)
        return total
    for bit in bits_of(chips)[::-1]:
        x = x.reshape((2, bit) + x.shape[1:])
        mine = (chip // bit) % 2
        got = swap_chips(pick(x, 1 - mine), bit)
        x = (pick(x, mine).astype(F32) + got.astype(F32)).astype(BF16)
    return x[0].astype(F32)


def split_cores(product, own):
    rows, columns = product.shape
    split = product.reshape(rows // own // 2, 2, own, columns)
    return split[:, 0], split[:, 1]


def store_by_core(core, product, own, rows, keep_out, give_out):
    first, second = split_cores(product, own)
    mine = core[0] == 0
    keep_out[:, rows : rows + own] = jnp.where(mine, first, second)
    give_out[:, rows : rows + own] = jnp.where(mine, second, first)


def product_halves(core, lhs, rhs, keep_out, give_out):
    product = dot(lhs[...], rhs[...], TN).astype(BF16)
    store_by_core(core, product, keep_out.shape[1], 0, keep_out, give_out)


def turns_of(groups):
    return 4 if groups % 4 == 0 else 1


def product_by_core(lhs, rhs, columns):
    dps = lax.axis_size("dp")
    chips = lax.axis_size("ctx") // 2
    core = lax.axis_index("ctx") % 2
    tokens, rows = lhs.shape
    groups = dps * chips
    own = rows // (groups * 2)
    shape = (dps, chips, own, columns)
    if own % 16:
        product = dot(lhs, rhs, TN).astype(BF16).reshape(dps, chips, 2, own, columns)
        return pick(product, core, 2), pick(product, 1 - core, 2)
    turns = turns_of(groups)
    out = jax.ShapeDtypeStruct((groups, own, columns), BF16)
    spec = pl.BlockSpec((groups // turns, own, columns), first_index_of_three)
    keep, give = pl.pallas_call(
        product_halves,
        grid=(turns,),
        in_specs=[
            pl.BlockSpec(memory_space=pltpu.SMEM),
            pl.BlockSpec((tokens, rows // turns), second_index_of_two),
            pl.BlockSpec((tokens, columns), no_index_of_two),
        ],
        out_specs=[spec, spec],
        out_shape=[out, out],
        compiler_params=pltpu.CompilerParams(vmem_limit_bytes=VMEM_BYTES),
        cost_estimate=FREE,
    )(core.reshape(1), lhs, rhs)
    return keep.reshape(shape), give.reshape(shape)


def packed_block(lhs, first, second, out_lhs, out_rhs, out):
    groups, height, columns = out.shape
    inner = first.shape[1]
    own = lhs.shape[1] // groups
    out[:, :own, :inner] = dot(lhs[...], first[...], TN).astype(BF16).reshape(groups, own, inner)
    out[:, :own, inner:] = dot(lhs[...], second[...], TN).astype(BF16).reshape(groups, own, columns - inner)
    product = dot(out_lhs[...], out_rhs[...], TN).astype(BF16)
    rest, width = height - own, product.shape[1]
    split = product.reshape(groups, -1, rest, width)
    for turn in range(split.shape[1]):
        out[:, own:, turn * width : (turn + 1) * width] = split[:, turn]
    out[:, own:, split.shape[1] * width :] = jnp.zeros((groups, rest, columns - split.shape[1] * width), BF16)


def packed_product(lhs, first, second, out_lhs, out_rhs):
    count = lax.axis_size("dp") * lax.axis_size("ctx")
    tokens, rows = lhs.shape
    inner, rest = first.shape[1], second.shape[1]
    columns = inner + rest
    own, out_own = rows // count, out_lhs.shape[1] // count
    width = out_rhs.shape[1]
    pieces = columns // width
    height = own + out_own // pieces
    turns = turns_of(count)
    if own % 16 or (out_own // pieces) % 16:
        product = jnp.concatenate([dot(lhs, first, TN), dot(lhs, second, TN)], axis=1).astype(BF16)
        other = dot(out_lhs, out_rhs, TN).astype(BF16).reshape(count, pieces, out_own // pieces, width)
        other = jnp.swapaxes(other, 1, 2).reshape(count, out_own // pieces, pieces * width)
        other = jnp.pad(other, ((0, 0), (0, 0), (0, columns - pieces * width)))
        return jnp.concatenate([product.reshape(count, own, columns), other], axis=1)
    return pl.pallas_call(
        packed_block,
        grid=(turns,),
        in_specs=[
            pl.BlockSpec((tokens, rows // turns), second_index_of_two),
            pl.BlockSpec((tokens, inner), no_index_of_two),
            pl.BlockSpec((tokens, rest), no_index_of_two),
            pl.BlockSpec((tokens, out_lhs.shape[1] // turns), second_index_of_two),
            pl.BlockSpec((tokens, width), no_index_of_two),
        ],
        out_specs=pl.BlockSpec((count // turns, height, columns), first_index_of_three),
        out_shape=jax.ShapeDtypeStruct((count, height, columns), BF16),
        compiler_params=pltpu.CompilerParams(vmem_limit_bytes=VMEM_BYTES),
        cost_estimate=FREE,
    )(lhs, first, second, out_lhs, out_rhs)


def scatter_packed(product, own, width):
    _, height, columns = product.shape
    total = lax.psum_scatter(product, BOTH, scatter_dimension=0, tiled=True).reshape(height, columns)
    pieces = columns // width
    return total[:own], jnp.concatenate([total[own:, i * width : (i + 1) * width] for i in range(pieces)], axis=0)


def first_index_of_three(i):
    return (i, 0, 0)


def second_index_of_two(i):
    return (0, i)


def no_index_of_two(i):
    return (0, 0)


def over_cores(keep, give):
    return (keep.astype(F32) + swap_cores(give).astype(F32)).astype(BF16)


def after(trees, ready):
    return lax.optimization_barrier((trees, ready))[0]


def exchange_chips(blocks):
    chips = blocks.shape[0]
    chip = lax.axis_index("ctx") // 2
    got = [pick(blocks, chip)]
    for distance in range(1, chips):
        got.append(swap_chips(pick(blocks, chip ^ distance), distance))
    return got


def by_sender(got):
    chip = lax.axis_index("ctx") // 2
    held = jnp.stack(got)
    return [pick(held, place ^ chip) for place in range(len(got))]


def carry_along(pair_t, pair_state, forward, work):
    count = lax.axis_size("ctx")
    chips = count // 2
    sequences, states, channels = pair_state.shape
    if chips > 4:

        def advance(_, carried):
            arrived = shift_along((carried * pair_t + pair_state).astype(BF16), 2 if forward else -2)
            return arrived.astype(F32)

        received = lax.fori_loop(0, chips - 1, advance, jnp.zeros_like(pair_state)).astype(BF16)
        done = []
        for items in work:
            for item in items:
                done.append(item(done, pair_state))
        return received, done
    share = channels // chips
    high = pair_t.astype(BF16)
    low = (pair_t - high.astype(F32)).astype(BF16)
    payload = jnp.concatenate(
        [pair_state.astype(BF16), high, low, jnp.zeros((sequences, 14, channels), BF16)], axis=1
    )
    blocks = jnp.moveaxis(payload.reshape(sequences, states + 16, chips, share), 2, 0)
    got = exchange_chips(blocks)
    done = []
    got, done = during(got, done, work[0], payload)
    carried = jnp.zeros((sequences, states, share), F32)
    entering = [None] * chips
    order = range(chips) if forward else range(chips - 1, -1, -1)
    held = by_sender(got)
    for place in order:
        entering[place] = carried.astype(BF16)
        decay = (held[place][:, states : states + 1].astype(F32) + held[place][:, states + 1 : states + 2].astype(F32))
        carried = carried * decay + held[place][:, :states].astype(F32)
    blocks = jnp.stack(entering)
    got = exchange_chips(blocks)
    got, done = during(got, done, work[1], blocks)
    return jnp.concatenate(by_sender(got), axis=-1), done


def during(got, done, items, ready):
    for item in items:
        made = item(done, ready)
        got, made = lax.optimization_barrier((got, made))
        done = done + [made]
    return got, done


def chain(through, mine, give, forward, work):
    core = lax.axis_index("ctx") % 2
    leading = core == (0 if forward else 1)
    other_t = swap_cores(through)
    sent = swap_cores(give).astype(F32)
    own_t, other_t = pick(through, core), pick(other_t, core)
    first_t = jnp.where(leading, own_t, other_t)
    second_t = jnp.where(leading, other_t, own_t)
    own = mine.astype(F32)
    first_state = jnp.where(leading, own, sent)
    pair_state = first_state * second_t + jnp.where(leading, sent, own)
    incoming, work = carry_along(first_t * second_t, pair_state, forward, work)
    second_in = (incoming.astype(F32) * first_t + first_state).astype(BF16)
    keep = jnp.where(leading, incoming, second_in)
    back = swap_cores(jnp.where(leading, second_in, incoming))
    return (keep, back), work


def silu_parts(v):
    gate = 0.5 + 0.5 * jnp.tanh(0.5 * v)
    return v * gate, gate


def pair_mask(rows):
    return lax.broadcasted_iota(jnp.int32, (rows, LANES), 1) < LANES // 2


def spread(per_head, k, mask):
    return jnp.where(mask, per_head[:, 2 * k : 2 * k + 1], per_head[:, 2 * k + 1 : 2 * k + 2])


def dot(a, b, contract, precision=None):
    return lax.dot_general(
        a, b, ((contract[0], contract[1]), ((), ())),
        preferred_element_type=F32, precision=precision,
    )


NN = ((1,), (0,))
NT = ((1,), (1,))
TN = ((0,), (0,))


def triangle(size, upper):
    row = lax.broadcasted_iota(jnp.int32, (size, size), 0)
    col = lax.broadcasted_iota(jnp.int32, (size, size), 1)
    keep = (col >= row) if upper else (col <= row)
    return jnp.where(keep, 1.0, 0.0).astype(F32)


def steps_of(raw, heads):
    shifted = raw + heads[0:1]
    step = jnp.maximum(shifted, 0.0) + jnp.log1p(jnp.exp(-jnp.abs(shifted)))
    rate = -step * jnp.exp(heads[1:2])
    return shifted, step, rate


def half_of(core, mine, other, part, lanes):
    return jnp.where(core[0] == part, mine[0, :, lanes], other[0, :, lanes])


def store_halves(core, values, mine_out, give_out):
    mine_out[0] = jnp.where(core[0] == 0, values[0], values[1])
    give_out[0] = jnp.where(core[0] == 0, values[1], values[0])


def add_up(out, rows, lanes, value):
    first = pl.program_id(0) == 0
    out[rows, lanes] = jnp.where(first, value, out[rows, lanes] + value)


def spread_masks(columns, wide):
    rows = wide.shape[1]
    for s in range(1, 4):
        wide[s - 1] = jnp.broadcast_to(columns[0, :, s : s + 1], (rows, LANES))


def head_sums(values, selector):
    high = values.astype(BF16)
    low = (values - high.astype(F32)).astype(BF16)
    return dot(high, selector, NN) + dot(low, selector, NN)


def fwd_local(core, proj, halo, marks, bias, heads, taps, conv_out, ysum_out, read_out, cum_out, mine_out, give_out, ext, weighted, wide):
    length = proj.shape[1]
    channels = halo.shape[2]
    states = read_out.shape[2]
    inner = channels - 2 * states
    head_rows = heads[...]
    raw = proj[0, :, channels:]
    _, step, rate = steps_of(raw, head_rows)
    cum = dot(triangle(length, False), rate, NN, EXACT)
    cum_t = dot(rate, triangle(length, False), ((0,), (1,)), EXACT)
    cum_out[0] = jnp.concatenate([cum, raw], axis=1)
    last = cum[length - 1 : length]
    end_weight = jnp.exp(last - cum) * marks[0, :, 4:5] * step
    ext[0:EDGE] = halo[0]
    ext[EDGE:] = proj[0, :, :channels]
    spread_masks(marks, wide)

    def activate(lo):
        lanes = slice(lo, lo + LANES)
        total = taps[4:5, lanes] + ext[EDGE:, lanes] * taps[3:4, lanes]
        for s in range(1, 4):
            total = total + ext[EDGE - s : EDGE - s + length, lanes] * (taps[3 - s : 4 - s, lanes] * wide[s - 1])
        conv_out[0, :, lanes] = total
        return silu_parts(total)[0]

    written = activate(inner).astype(BF16)
    readout = activate(inner + states).astype(BF16)
    read_out[0] = readout
    scores = dot(readout, written, NT)
    mask = pair_mask(length)
    blocked = bias[0]
    zero = jnp.zeros((length, LANES), BF16)
    for k in range(inner // LANES):
        lo = k * LANES
        x = activate(lo)
        scaled = (x * spread(step, k, mask)).astype(BF16)
        weighted[:, lo : lo + LANES] = (x * spread(end_weight, k, mask)).astype(BF16)
        mixing = []
        for h in (2 * k, 2 * k + 1):
            gap = cum[:, h : h + 1] - cum_t[h : h + 1, :]
            mixing.append((jnp.exp(gap + blocked) * scores).astype(BF16))
        values = jnp.concatenate(
            [jnp.where(mask, scaled, zero), jnp.where(mask, zero, scaled)], axis=0
        )
        result = dot(jnp.concatenate(mixing, axis=1), values, NN)
        ysum_out[0, :, lo : lo + LANES] = result + x * spread(head_rows[2:3], k, mask[0:1])
    half = inner // 2
    store_halves(
        core,
        [dot(written, weighted[:, part * half : (part + 1) * half], TN).astype(BF16) for part in range(2)],
        mine_out,
        give_out,
    )


def fwd_mix(core, ysum, read, cum, marks, in_mine, in_other, gates, gain, mixed_out, y_out, gated):
    length = ysum.shape[1]
    inner = ysum.shape[2]
    half = inner // 2
    entry = jnp.exp(cum[0][:, : cum.shape[2] // 2]) * marks[0, :, 5:6]
    mask = pair_mask(length)
    squares = jnp.zeros((length, LANES), F32)
    for k in range(inner // LANES):
        lo = k * LANES
        part, at = lo // half, lo % half
        carried = dot(read[0], half_of(core, in_mine, in_other, part, slice(at, at + LANES)), NN)
        y = ysum[0, :, lo : lo + LANES] + spread(entry, k, mask) * carried
        y_out[0, :, lo : lo + LANES] = y
        value = y * silu_parts(gates[0, :, lo : lo + LANES])[0]
        gated[:, lo : lo + LANES] = value
        squares = squares + value * value
    scale = lax.rsqrt(jnp.sum(squares, axis=1, keepdims=True) * (1.0 / inner) + EPSILON)
    for k in range(inner // LANES):
        lanes = slice(k * LANES, (k + 1) * LANES)
        mixed_out[0, :, lanes] = (gated[:, lanes] * scale * gain[:, lanes]).astype(BF16)


def bwd_gate(core, grad, y, gates, gain, cum, marks, read, dy_out, dgate_out, dgain_out, mine_out, give_out, weighted):
    length = y.shape[1]
    inner = y.shape[2]
    entry = jnp.exp(cum[0][:, : cum.shape[2] // 2]) * marks[0, :, 5:6]
    mask = pair_mask(length)
    squares = jnp.zeros((length, LANES), F32)
    cross = jnp.zeros((length, LANES), F32)
    for k in range(inner // LANES):
        lanes = slice(k * LANES, (k + 1) * LANES)
        value = y[0, :, lanes] * silu_parts(gates[0, :, lanes])[0]
        squares = squares + value * value
        cross = cross + value * grad[0, :, lanes] * gain[:, lanes]
    scale = lax.rsqrt(jnp.sum(squares, axis=1, keepdims=True) * (1.0 / inner) + EPSILON)
    inward = jnp.sum(cross, axis=1, keepdims=True) * (scale * scale * scale * (1.0 / inner))
    for k in range(inner // LANES):
        lanes = slice(k * LANES, (k + 1) * LANES)
        z = gates[0, :, lanes]
        active, sigmoid = silu_parts(z)
        yk = y[0, :, lanes]
        value = yk * active
        g = grad[0, :, lanes]
        add_up(dgain_out, slice(0, 1), lanes, jnp.sum(g * value * scale, axis=0, keepdims=True))
        dvalue = g * gain[:, lanes] * scale - value * inward
        dy = dvalue * active
        dy_out[0, :, lanes] = dy
        dgate_out[0, :, lanes] = (dvalue * yk * (sigmoid + active * (1.0 - sigmoid))).astype(BF16)
        weighted[:, lanes] = (dy * spread(entry, k, mask)).astype(BF16)
    half = inner // 2
    store_halves(
        core,
        [dot(read[0], weighted[:, part * half : (part + 1) * half], TN).astype(BF16) for part in range(2)],
        mine_out,
        give_out,
    )


def bwd_diag(core, conv, ysum, dy, read, cum, marks, bias_t, heads, selector, in_mine, in_other, dscaled_out, joint_out, terms, entered):
    length = ysum.shape[1]
    inner = ysum.shape[2]
    half = inner // 2
    states = read.shape[2]
    head_rows = heads[...]
    heads_n = heads.shape[1]
    _, step, rate = steps_of(cum[0][:, heads_n:], head_rows)
    cums = cum[0][:, :heads_n]
    cum_t = dot(rate, triangle(length, False), ((0,), (1,)), EXACT)
    entry = jnp.exp(cums) * marks[0, :, 5:6]
    written = silu_parts(conv[0, :, inner : inner + states])[0].astype(BF16)
    readout = read[0]
    scores_t = dot(written, readout, NT)
    mask = pair_mask(length)
    blocked = bias_t[0]
    zero = jnp.zeros((length, LANES), BF16)
    dscores_t = jnp.zeros((length, length), F32)
    for k in range(inner // LANES):
        lo = k * LANES
        lanes = slice(lo, lo + LANES)
        x = silu_parts(conv[0, :, lanes])[0]
        scaled = (x * spread(step, k, mask)).astype(BF16)
        grad = dy[0, :, lanes]
        low = grad.astype(BF16)
        decays, mixing = [], []
        for h in (2 * k, 2 * k + 1):
            gap = cum_t[h : h + 1, :] - cums[:, h : h + 1]
            decay = jnp.exp(gap + blocked)
            decays.append(decay)
            mixing.append((decay * scores_t).astype(BF16))
        grads = jnp.concatenate([jnp.where(mask, low, zero), jnp.where(mask, zero, low)], axis=0)
        dscaled = dot(jnp.concatenate(mixing, axis=1), grads, NN)
        dscaled_out[0, :, lanes] = dscaled
        values = jnp.concatenate(
            [jnp.where(mask, scaled, zero), jnp.where(mask, zero, scaled)], axis=0
        )
        dmixing = dot(values, low, NT)
        dscores_t = dscores_t + dmixing[:length] * decays[0] + dmixing[length:] * decays[1]
        entered_k = (grad * spread(entry, k, mask)).astype(BF16)
        entered[:, lanes] = entered_k
        part, at = lo // half, lo % half
        carried = dot(readout, half_of(core, in_mine, in_other, part, slice(at, at + LANES)), NN)
        diagonal = ysum[0, :, lanes] - x * spread(head_rows[2:3], k, mask[0:1])
        terms[:, lanes] = (
            low.astype(F32) * diagonal
            - scaled.astype(F32) * dscaled
            + entered_k.astype(F32) * carried
        )
    joint_out[0, :, 2 * states :] = head_sums(terms[...], selector[...])
    dlow = dscores_t.astype(BF16)
    joint_out[0, :, :states] = dot(dlow, readout, NN)
    dread = dot(dlow, written, TN)
    for part in range(2):
        dread = dread + dot(
            entered[:, part * half : (part + 1) * half],
            half_of(core, in_mine, in_other, part, slice(None)),
            NT,
        )
    joint_out[0, :, states : 2 * states] = dread


def bwd_local(core, proj, halo, conv, dy, dscaled, joint, cum, marks, backs, heads, taps, selector, in_mine, in_other, out_mine, out_other, through, dproj_out, dhalo_out, dtaps_out, dhead_out, ext, dconv, ending, terms, wide, wide_back):
    length = proj.shape[1]
    channels = halo.shape[2]
    states = (joint.shape[2] - LANES) // 2
    inner = channels - 2 * states
    half = inner // 2
    head_rows = heads[...]
    heads_n = heads.shape[1]
    shifted, step, rate = steps_of(cum[0][:, heads_n:], head_rows)
    cums = cum[0][:, :heads_n]
    last = cums[length - 1 : length]
    end_decay = jnp.exp(last - cums) * marks[0, :, 4:5]
    end_weight = end_decay * step
    mask = pair_mask(length)
    written_v, written_s = silu_parts(conv[0, :, inner : inner + states])
    written = written_v.astype(BF16)
    ext[0:EDGE] = halo[0]
    ext[EDGE:] = proj[0, :, :channels]
    dconv[0:EDGE] = jnp.zeros((EDGE, channels), F32)
    dconv[EDGE + length :] = jnp.zeros((EDGE, channels), F32)
    products, skips = [], []
    for k in range(inner // LANES):
        lo = k * LANES
        lanes = slice(lo, lo + LANES)
        part, at = lo // half, lo % half
        pre = conv[0, :, lanes]
        x, sigmoid = silu_parts(pre)
        grad = dy[0, :, lanes]
        back = half_of(core, out_mine, out_other, part, slice(at, at + LANES))
        entering = half_of(core, in_mine, in_other, part, slice(at, at + LANES))
        products.append(
            jnp.sum(back.astype(F32) * entering.astype(F32), axis=0, keepdims=True)
        )
        ends = dot(written, back, NN)
        inside = dscaled[0, :, lanes] + spread(end_decay, k, mask) * ends
        weighted = (x * spread(end_weight, k, mask)).astype(BF16)
        ending[:, lanes] = weighted
        terms[0:length, lanes] = x * inside
        terms[length : 2 * length, lanes] = weighted.astype(F32) * ends
        skips.append(jnp.sum(grad * x, axis=0, keepdims=True))
        dx = spread(step, k, mask) * inside + spread(head_rows[2:3], k, mask[0:1]) * grad
        dconv[EDGE : EDGE + length, lanes] = dx * (sigmoid + x * (1.0 - sigmoid))
    dw = joint[0, :, :states]
    for part in range(2):
        dw = dw + dot(
            ending[:, part * half : (part + 1) * half],
            half_of(core, out_mine, out_other, part, slice(None)),
            NT,
        )
    dconv[EDGE : EDGE + length, inner : inner + states] = dw * (
        written_s + written_v * (1.0 - written_s)
    )
    read_v, read_s = silu_parts(conv[0, :, inner + states :])
    dconv[EDGE : EDGE + length, inner + states :] = joint[0, :, states : 2 * states] * (read_s + read_v * (1.0 - read_s))
    sums = head_sums(terms[...], selector[...])
    dstep = sums[:length, :heads_n]
    ended = sums[length:, :heads_n]
    lane_sums = jnp.concatenate(
        [jnp.concatenate(products, axis=1), jnp.concatenate(skips, axis=1), jnp.zeros((6, inner), F32)], axis=0
    )
    by_head = head_sums(lane_sums, selector[...])[:, :heads_n]
    kept = by_head[0:1]
    at_last = jnp.sum(ended, axis=0, keepdims=True) + kept * through[0]
    row = lax.broadcasted_iota(jnp.int32, (length, heads_n), 0)
    dcums = joint[0, :, 2 * states : 2 * states + heads_n] - ended + jnp.where(row == length - 1, at_last, 0.0)
    drate = dot(triangle(length, True), dcums, NN, EXACT)
    dstep = dstep - drate * jnp.exp(head_rows[1:2])
    draw = dstep * (1.0 / (1.0 + jnp.exp(-shifted)))
    dproj_out[0, :, channels:] = draw.astype(BF16)
    add_up(
        dhead_out,
        slice(None),
        slice(None),
        jnp.concatenate(
            [
                jnp.sum(draw, axis=0, keepdims=True),
                jnp.sum(drate * rate, axis=0, keepdims=True),
                by_head[1:2],
                jnp.zeros((5, heads_n), F32),
            ],
            axis=0,
        ),
    )
    rows = length + EDGE
    spread_masks(marks, wide)
    spread_masks(backs, wide_back)
    for lo in range(0, channels, LANES):
        lanes = slice(lo, lo + LANES)
        own = dconv[EDGE : EDGE + length, lanes]
        total = dconv[0:rows, lanes] * taps[3:4, lanes]
        sums = [jnp.sum(own * ext[EDGE:, lanes], axis=0, keepdims=True)]
        for s in range(1, 4):
            total = total + dconv[s : s + rows, lanes] * (taps[3 - s : 4 - s, lanes] * wide_back[s - 1])
            sums.append(
                jnp.sum(own * ext[EDGE - s : EDGE - s + length, lanes] * wide[s - 1], axis=0, keepdims=True)
            )
        dproj_out[0, :, lanes] = total[EDGE:].astype(BF16)
        dhalo_out[0, 0:EDGE, lanes] = total[:EDGE]
        dhalo_out[0, EDGE:, lanes] = total[length:]
        sums = sums[::-1] + [jnp.sum(own, axis=0, keepdims=True), jnp.zeros((3, LANES), F32)]
        add_up(dtaps_out, slice(None), lanes, jnp.concatenate(sums, axis=0))


def per_sequence(kernel, inputs, outputs, scratch):
    sequences = None
    in_specs = [pl.BlockSpec(memory_space=pltpu.SMEM)]
    arrays = [(lax.axis_index("ctx") % 2).reshape(1)]
    for array, axis in inputs:
        if axis is not None:
            sequences = array.shape[axis]
        in_specs.append(block_spec(array.shape, axis))
        arrays.append(array)
    out_specs = [block_spec(shape, axis) for shape, _, axis in outputs]
    out_shape = [jax.ShapeDtypeStruct(shape, dtype) for shape, dtype, _ in outputs]
    return pl.pallas_call(
        kernel,
        grid=(sequences,),
        in_specs=in_specs,
        out_specs=out_specs,
        out_shape=out_shape,
        scratch_shapes=scratch,
        compiler_params=pltpu.CompilerParams(vmem_limit_bytes=VMEM_BYTES),
        cost_estimate=FREE,
    )(*arrays)


def block_spec(shape, axis):
    block = tuple(1 if d == axis else size for d, size in enumerate(shape))
    rank = len(shape)
    return pl.BlockSpec(
        block, functools.partial(block_index, rank, axis)
    )


def block_index(rank, axis, i):
    return tuple(i if d == axis else 0 for d in range(rank))


def rms_scale(values, gain_vector):
    return (
        values
        * lax.rsqrt(jnp.mean(values * values, axis=-1, keepdims=True) + EPSILON)
        * gain_vector
    )


def lanes_of(per_head, size):
    sequences, heads = per_head.shape
    spread_out = jnp.repeat(per_head, size, axis=1).reshape(sequences, 2, 1, heads * size // 2)
    return jnp.moveaxis(spread_out, 1, 0)


def layer_forward(hidden, ids, small, mix_weight, wave, later, head_params):
    norm_gain, taps, gate_gain = small
    sequences, length, width = hidden.shape
    channels = taps.shape[1]
    inner = gate_gain.shape[0]
    states = (channels - inner) // 2
    heads_n = head_params.shape[1]
    size = inner // heads_n
    gain = norm_gain.astype(F32)
    normed = rms_scale(hidden, gain).astype(BF16)
    proj = jnp.dot(normed, mix_weight, preferred_element_type=F32)
    edge = shift_along(proj[:, length - EDGE :, :channels], 1)
    conv, ysum, read, cum, mine, give = per_sequence(
        fwd_local,
        [(proj, 0), (edge, 0), (ids["marks"], 0), (ids["bias"], 0), (head_params, None), (taps, None)],
        [
            ((sequences, length, channels), F32, 0),
            ((sequences, length, inner), F32, 0),
            ((sequences, length, states), BF16, 0),
            ((sequences, length, 2 * heads_n), F32, 0),
            ((sequences, states, inner // 2), BF16, 0),
            ((sequences, states, inner // 2), BF16, 0),
        ],
        [
            pltpu.VMEM((length + EDGE, channels), F32),
            pltpu.VMEM((length, inner), BF16),
            pltpu.VMEM((3, length, LANES), F32),
        ],
    )
    through = jnp.exp(cum[:, -1, :heads_n]) * ids["carry"][:, None]
    through_lanes = lanes_of(through, size)
    packed, shapes = wave
    following_wave = None
    if later:
        following_wave = (gather_packed(after(later, mine)), [shard.shape for shard in later])
    arrived = lambda done, ready: unpack(after(packed, ready), shapes)[:2]
    used = lambda done, ready: [jnp.dot(normed, done[0][1], preferred_element_type=F32)] + unpack(
        after(packed, ready), shapes
    )[2:]
    incoming, made = chain(
        through_lanes, mine, give, True, [[arrived], [used]] if later else [[], [arrived, used]]
    )
    (out_weight, gate_weight), (gates, *following) = made
    weights = (norm_gain, mix_weight, gate_weight, taps, gate_gain, out_weight)
    mixed, y = per_sequence(
        fwd_mix,
        [(ysum, 0), (read, 0), (cum, 0), (ids["marks"], 0), (incoming[0], 0), (incoming[1], 0), (gates, 0), (gate_gain.astype(F32)[None], None)],
        [((sequences, length, inner), BF16, 0), ((sequences, length, inner), F32, 0)],
        [pltpu.VMEM((length, inner), F32)],
    )
    update = jnp.dot(mixed, out_weight, preferred_element_type=F32)
    saved = (hidden, gain, normed, proj, edge, gates, conv, ysum, read, cum, through, through_lanes, incoming, mixed, y)
    return hidden + update, weights, following, following_wave, saved


def layer_backward(gradient, ids, weights, head_params, saved, final, other_terms=None, other_small=None):
    hidden, gain, normed, proj, edge, gates, conv, ysum, read, cum, through, through_lanes, incoming, mixed, y = saved
    _, mix_weight, gate_weight, taps, gate_gain, out_weight = weights
    sequences, length, width = hidden.shape
    tokens = sequences * length
    channels = taps.shape[1]
    inner = gate_gain.shape[0]
    states = (channels - inner) // 2
    heads_n = head_params.shape[1]
    size = inner // heads_n
    if final:
        other_product = packed_product(*other_terms)
        gradient, other_product = lax.optimization_barrier((gradient, other_product))
    update_low = gradient.astype(BF16)
    mixed_grad = lax.dot_general(
        update_low, out_weight, (((2,), (1,)), ((), ())), preferred_element_type=F32
    )
    dy, dgates, dgain, mine, give = per_sequence(
        bwd_gate,
        [(mixed_grad, 0), (y, 0), (gates, 0), (gate_gain.astype(F32)[None], None), (cum, 0), (ids["marks"], 0), (read, 0)],
        [
            ((sequences, length, inner), F32, 0),
            ((sequences, length, inner), BF16, 0),
            ((8, inner), F32, None),
            ((sequences, states, inner // 2), BF16, 0),
            ((sequences, states, inner // 2), BF16, 0),
        ],
        [pltpu.VMEM((length, inner), BF16)],
    )
    head_of = jnp.arange(inner) // size
    selector = (head_of[:, None] == jnp.arange(LANES)[None]).astype(BF16)

    def diagonal(done, ready):
        return per_sequence(
            bwd_diag,
            [(conv, 0), (ysum, 0), (after(dy, ready), 0), (read, 0), (cum, 0), (ids["marks"], 0),
             (ids["bias_t"], 0), (head_params, None), (selector, None), (incoming[0], 0), (incoming[1], 0)],
            [
                ((sequences, length, inner), F32, 0),
                ((sequences, length, 2 * states + LANES), F32, 0),
            ],
            [pltpu.VMEM((length, inner), F32), pltpu.VMEM((length, inner), BF16)],
        )

    flat = normed.reshape(tokens, width)
    flat_gates = dgates.reshape(tokens, inner)
    output_terms = (mixed.reshape(tokens, inner), update_low.reshape(tokens, width))
    order = bits_of(lax.axis_size("dp"))
    if final:
        outgoing, made = chain(
            through_lanes,
            mine,
            give,
            False,
            [
                [
                    diagonal,
                    lambda done, ready: [
                        product_by_core(*after(output_terms, ready), width),
                        product_by_core(*after((flat, flat_gates), ready), inner),
                    ],
                ],
                [lambda done, ready: [over_cores(*product) for product in done[1]]],
            ],
        )
        (dscaled, joint), _, pair = made
        outgoing, pair = lax.optimization_barrier((outgoing, pair))
        own = inner // (2 * lax.axis_size("dp") * lax.axis_size("ctx") // 2)
        pair = [halve_over_rows(pair[0], order[:1], order), halve_over_rows(pair[1], order[-1:], order)]
    else:
        outgoing, made = chain(through_lanes, mine, give, False, [[diagonal], []])
        dscaled, joint = made[0]
    dproj, dhalo, dtaps, dheads = per_sequence(
        bwd_local,
        [(proj, 0), (edge, 0), (conv, 0), (dy, 0), (dscaled, 0), (joint, 0), (cum, 0),
         (ids["marks"], 0), (ids["backs"], 0), (head_params, None), (taps, None), (selector, None),
         (incoming[0], 0), (incoming[1], 0), (outgoing[0], 0), (outgoing[1], 0), (through[:, None], 0)],
        [
            ((sequences, length, channels + heads_n), BF16, 0),
            ((sequences, 2 * EDGE, channels), F32, 0),
            ((8, channels), F32, None),
            ((8, heads_n), F32, None),
        ],
        [
            pltpu.VMEM((length + EDGE, channels), F32),
            pltpu.VMEM((length + 2 * EDGE, channels), F32),
            pltpu.VMEM((length, inner), BF16),
            pltpu.VMEM((2 * length, inner), F32),
            pltpu.VMEM((3, length, LANES), F32),
            pltpu.VMEM((3, length + EDGE, LANES), F32),
        ],
    )
    if final:
        dproj, dhalo, pair = lax.optimization_barrier((dproj, dhalo, pair))
        pair = [
            halve_over_rows(pair[0], order[1:], order[1:])[0],
            halve_over_rows(pair[1], order[:-1], order[:-1])[0],
        ]
        pair = jnp.concatenate([pair[0]] + jnp.split(pair[1], inner // width, axis=2), axis=1)
    returned = shift_along(dhalo[:, :EDGE].astype(BF16), -1).astype(F32)
    tail = (dhalo[:, EDGE:] + returned).astype(BF16)
    dproj = lax.dynamic_update_slice(dproj, tail, (0, length - EDGE, 0))
    flat_grad = dproj.reshape(tokens, -1)
    if final:
        other_small = after(other_small, flat_grad)
        product = product_by_core(flat, flat_grad, flat_grad.shape[1])
        dproj, product, pair = lax.optimization_barrier((dproj, product, pair))
        summed = over_cores(*product)
        cut = channels // 2 // LANES * LANES
        pair = scatter_over_chips(pair)
        first_parts = [
            halve_over_rows(summed[..., :cut], order[:1], order),
            halve_over_rows(summed[..., cut:], order[-1:], order),
        ]
    normed_grad = lax.dot_general(
        dproj, mix_weight, (((2,), (1,)), ((), ())), preferred_element_type=F32
    ) + lax.dot_general(dgates, gate_weight, (((2,), (1,)), ((), ())), preferred_element_type=F32)
    _, norm_pull = jax.vjp(rms_scale, hidden, gain)
    hidden_grad, norm_grad = norm_pull(normed_grad)
    small_terms = (norm_grad, dtaps, dgain, dheads)
    gradient = gradient + hidden_grad
    if not final:
        return gradient, small_terms, (flat, flat_gates, flat_grad) + output_terms
    chips = lax.axis_size("ctx") // 2
    core, chip = lax.axis_index("ctx") % 2, lax.axis_index("ctx") // 2
    devices = lax.axis_size("dp") * lax.axis_size("ctx")
    small = jnp.concatenate([by_device(devices, *small_terms), by_device(devices, *other_small)], axis=1)
    small = small.reshape(devices // 2, 2, -1)
    small = pick(small, core, 1) + swap_cores(pick(small, 1 - core, 1))
    first_parts, small = lax.optimization_barrier((first_parts, small))
    second_parts = [
        halve_over_rows(first_parts[0], order[1:], order[1:])[0],
        halve_over_rows(first_parts[1], order[:-1], order[:-1])[0],
    ]
    mine = lax.axis_index("dp")
    total = small
    for bit in order[::-1]:
        total = total.reshape((2, bit * chips) + total.shape[1:])
        half = (mine // bit) % 2
        total = pick(total, half) + swap_rows(pick(total, 1 - half), bit)
        if bit == order[-1]:
            other_grads = scatter_packed(other_product, width // (inner // own), width)
            total, other_grads = lax.optimization_barrier((total, other_grads))
    second_parts, total = lax.optimization_barrier((second_parts, total))
    last = scatter_over_chips(jnp.concatenate(second_parts, axis=-1))
    small = pick(total, chip)
    for distance in range(1, chips):
        small = small + swap_chips(pick(total, chip ^ distance), distance)
    small, pair = lax.optimization_barrier((small, pair))
    small = jnp.split(small, 2)
    output_grad = pair[:own]
    gates_grad = jnp.concatenate(jnp.split(pair[own:], inner // width, axis=0), axis=1)
    input_grad = jnp.concatenate([gates_grad, last], axis=1)
    return gradient, small, input_grad, output_grad, tuple(grad.astype(F32) for grad in other_grads)


def by_device(devices, norm_grad, dtaps, dgain, dheads):
    return jnp.concatenate(
        [
            norm_grad.reshape(devices, -1),
            dtaps[:5].reshape(5, devices, -1).swapaxes(0, 1).reshape(devices, -1),
            dgain[0].reshape(devices, -1),
            jnp.broadcast_to(dheads[:3].reshape(1, -1), (devices, 3 * dheads.shape[1])),
        ],
        axis=1,
    )


def unpack_small(total, shards, heads_n):
    norm, _, kernel, offset, gate, _ = shards
    sizes = (norm.size, kernel.size, offset.size, gate.size, heads_n, heads_n, heads_n)
    parts, start = [], 0
    for size in sizes:
        parts.append(total[start : start + size])
        start += size
    norm_grad, taps_grad, offset_grad, gain_grad, timestep, decay, skip = parts
    return norm_grad, taps_grad.reshape(kernel.shape), offset_grad, timestep, decay, skip, gain_grad


def gather_packed(shards):
    width = shards[0].shape[1]
    pieces = []
    for shard in shards:
        for start in range(0, shard.shape[1], width):
            piece = shard[:, start : start + width]
            pieces.append(jnp.pad(piece, ((0, 0), (0, width - piece.shape[1]))))
    packed = jnp.concatenate(pieces, axis=0)
    return lax.all_gather(packed, BOTH, axis=0, tiled=True).reshape((-1,) + packed.shape)


def unpack(packed, shapes):
    width = packed.shape[2]
    weights = []
    row = 0
    for rows, columns in shapes:
        parts = []
        for start in range(0, columns, width):
            part = packed[:, row : row + rows, : min(width, columns - start)]
            parts.append(part.reshape(-1, part.shape[2]))
            row += rows
        weights.append(parts[0] if len(parts) == 1 else jnp.concatenate(parts, axis=1))
    return weights


def small_rows(layers):
    rows = []
    for shards, _ in layers:
        norm, _, kernel, offset, gate, _ = shards
        rows += [norm, kernel.reshape(-1), offset, gate]
    return jnp.concatenate(rows)[None]


def small_weights(everyone, layers):
    parts, start = [], 0
    for shards, _ in layers:
        norm, _, kernel, offset, gate, _ = shards
        for row in (norm, kernel.reshape(-1), offset, gate):
            parts.append(everyone[:, start : start + row.shape[0]])
            start += row.shape[0]
    count = everyone.shape[0]
    result = []
    for layer in range(len(layers)):
        norm, kernel, offset, gate = parts[4 * layer : 4 * layer + 4]
        taps = layers[layer][0][2].shape[0]
        kernel = kernel.reshape(count, taps, -1).swapaxes(0, 1).reshape(taps, -1).astype(F32)
        offset = offset.reshape(1, -1).astype(F32)
        packed_taps = jnp.concatenate([kernel, offset, jnp.zeros((8 - taps - 1, kernel.shape[1]), F32)], axis=0)
        result.append((norm.reshape(-1), packed_taps, gate.reshape(-1)))
    return result


def segment_terms(segments):
    sequences, length = segments.shape
    ids = segments.astype(F32)
    before = shift_along(ids[:, length - EDGE :] + 1.0, 1) - 1.0
    joined = jnp.concatenate([before, ids], axis=1)
    after = jnp.concatenate([joined, jnp.full((sequences, EDGE), -2.0, F32)], axis=1)
    marks, backs = [], []
    for s in range(4):
        marks.append((joined[:, EDGE - s : EDGE - s + length] == ids).astype(F32))
        backs.append((after[:, s : s + length + EDGE] == joined).astype(F32))
    last = ids[:, -1:]
    prev = before[:, -1:]
    marks.append((ids == last).astype(F32))
    marks.append((ids == prev).astype(F32))
    marks += [jnp.zeros_like(ids)] * 2
    causal = jnp.tril(jnp.ones((length, length), jnp.bool_))
    allowed = causal[None] & (ids[:, :, None] == ids[:, None, :])
    allowed_t = causal.T[None] & (ids[:, :, None] == ids[:, None, :])
    return {
        "marks": jnp.stack(marks, axis=2),
        "backs": jnp.stack(backs + backs, axis=2),
        "bias": jnp.where(allowed, 0.0, FAR).astype(F32),
        "bias_t": jnp.where(allowed_t, 0.0, FAR).astype(F32),
        "carry": (last == prev).astype(F32)[:, 0],
    }


def on_device(
    tokens,
    segments,
    cotangent,
    first_norm,
    first_input,
    first_kernel,
    first_offset,
    first_timestep,
    first_decay,
    first_skip,
    first_gate,
    first_output,
    second_norm,
    second_input,
    second_kernel,
    second_offset,
    second_timestep,
    second_decay,
    second_skip,
    second_gate,
    second_output,
):
    layout = tokens.shape
    sequences = layout[0] * layout[1]
    hidden = tokens.astype(F32).reshape(sequences, layout[2], layout[3])
    ids = segment_terms(segments.reshape(sequences, layout[2]))
    layers = (
        (
            (first_norm, first_input, first_kernel, first_offset, first_gate, first_output),
            (first_timestep, first_decay, first_skip),
        ),
        (
            (second_norm, second_input, second_kernel, second_offset, second_gate, second_output),
            (second_timestep, second_decay, second_skip),
        ),
    )
    stored = []
    first, second = layers[0][0], layers[1][0]
    inner = first[4].shape[0] * lax.axis_size("dp") * lax.axis_size("ctx")
    mixer, everyone = gather_rows(first[1][:, inner:], small_rows(layers))
    smalls = small_weights(everyone, layers)
    shards = [first[5], first[1][:, :inner], second[1][:, inner:]]
    wave = (gather_packed(shards), [shard.shape for shard in shards])
    ids, mixer = lax.optimization_barrier((ids, mixer))
    later = [second[5], second[1][:, :inner]]
    for (_, head_params), small in zip(layers, smalls):
        heads = jnp.stack(list(head_params) + [jnp.zeros_like(head_params[0])] * 5)
        hidden, weights, following, wave, saved = layer_forward(hidden, ids, small, mixer, wave, later, heads)
        stored.append((weights, heads, saved))
        mixer, later = following[0] if following else None, []
    gradient = cotangent.astype(F32).reshape(hidden.shape)
    weights, heads, saved = stored[1]
    gradient, small, terms = layer_backward(gradient, ids, weights, heads, saved, False)
    weights, heads, saved = stored[0]
    gradient, smalls, input_grad, output_grad, other_grads = layer_backward(
        gradient, ids, weights, heads, saved, True, terms, small
    )
    results = []
    for total, (in_grad, out_grad) in (
        (smalls[0], (input_grad, output_grad)),
        (smalls[1], other_grads),
    ):
        parts = unpack_small(total, layers[0][0], heads.shape[1])
        results.append((parts[0], in_grad) + parts[1:] + (out_grad,))
    return (hidden.reshape(layout), gradient.reshape(layout)) + results[0] + results[1]


def solution(mesh):
    weight_specs = (P(BOTH), P(BOTH, None), P(None, BOTH), P(BOTH), P(), P(), P(), P(BOTH), P(BOTH, None))
    tokens_spec = P(None, "dp", "ctx", None)
    return jax.shard_map(
        on_device,
        mesh=mesh,
        in_specs=(tokens_spec, P(None, "dp", "ctx"), tokens_spec) + weight_specs + weight_specs,
        out_specs=(tokens_spec, tokens_spec) + weight_specs + weight_specs,
        check_vma=False,
    )
```
